32 devices in a mesh: clique: 4 (over y, x), copy: 8 (over z, core).
Axes of the slice: x: 2, y: 2, z: 4, core: 2. Of those that a mesh axis runs over, the one named last changes fastest.
Arguments:
- out_grad: bfloat16 [65536, 512], P(('clique', 'copy')), may hold values from -6 to 6
- pre_act: bfloat16 [65536, 512], P(('clique', 'copy')), may hold values from -6 to 6
- batch_count: int32 [32], P(('clique', 'copy')), may hold values from 1024 to 2048, as said below
- layer_two: bfloat16 [512, 512], replicated, may hold values from -0.25 to 0.25
- hot_slots: int32 [65536, 10], P(('clique', 'copy')), may hold values from 0 to 2047
- cold_index: int32 [65536, 15], P(('clique', 'copy')), may hold values from 0 to 2047
- hot_feats: bfloat16 [2048, 768], P('clique'), may hold values from -6 to 6
- cold_feats: bfloat16 [65536, 768], P(('clique', 'copy')), may hold values from -6 to 6
Outputs:
- grad_one: float32 [768, 512], replicated
- grad_two: float32 [512, 512], replicated
The draws below stay inside these ranges and needn't reach their ends.
Inputs may be any that keep to these rules, and one draw needn't show every extreme that they name: `batch_count`: some device has all 2048 rows live in every draw.
All inputs are finite; a program needn't handle non-finite values.
Results may differ from the reference program's by a relative error of at most 0.015.
Values may be sent and summed in bfloat16 or wider, within the bound.
No kernel may reach another device: no remote copies, remote signals or barrier semaphores. Data moves between devices by JAX's collectives and lax.ppermute only.
A program may use at most 128 MiB of HBM per device.

```python
import math
import jax
import jax.numpy as jnp
import numpy as np
from jax import lax

D_IN = 768
D_H = 512
B_DEV = 2048
C_DEV = 2048
K_HOT = 10
K_COLD = 15
FANOUT = 25
HOT = 2048
DEVS = 32
TARGETS = 65536
COLD = 65536
N_CLIQUE = 4
N_COPY = 8


def draw_batch_count(key, part):
    counts = jax.random.randint(jax.random.fold_in(key, 11), (DEVS,), B_DEV // 2, B_DEV + 1)
    full_at = jax.random.randint(jax.random.fold_in(key, 12), (), 0, DEVS)
    return counts.at[full_at].set(B_DEV).astype(jnp.int32)


def touch_ends(array, stream_key, low, high):
    extent = array.shape
    place = [jax.random.randint(jax.random.fold_in(stream_key, axis), (), 0, extent[axis]) for axis in range(len(extent))]
    array = array.at[tuple(place)].set(low)
    longest = extent.index(max(extent))
    place[longest] = (place[longest] + 1) % extent[longest]
    return array.at[tuple(place)].set(high)


def block_scale(own_key, shape, cuts, smallest, largest):
    def one(axis_at, parts):
        steps = jax.random.uniform(jax.random.fold_in(jax.random.fold_in(own_key, 6), axis_at), (parts,), jnp.float32, smallest / len(cuts), largest / len(cuts))
        return jnp.repeat(jnp.exp(steps), shape[axis_at] // parts).reshape((-1,) + (1,) * (len(shape) - axis_at - 1))

    loudness = one(*cuts[0])
    for cut in cuts[1:]:
        loudness = loudness * one(*cut)
    return loudness


def rank_bounds(count, lean):
    loads = [(1 << 20) // math.isqrt(standing ** lean) + 1 for standing in range(1, count + 1)]
    spread = 1 + sum(loads) // (1 << 30)
    return np.cumsum(np.array([max(1, weight // spread) for weight in loads]))


def ranked_ids(rng, shape, number_of, skew):
    listing = rank_bounds(number_of, skew)
    ticket = jax.random.randint(jax.random.fold_in(rng, 1), shape, 0, int(listing[number_of - 1]))
    standing = jnp.searchsorted(jnp.asarray(listing, jnp.int32), ticket, side="right")
    return jax.random.permutation(jax.random.fold_in(rng, 2), number_of)[standing].astype(jnp.int32)


def bell_draw(key, shape, width, bound, split=(), held_as=jnp.bfloat16):
    array = width * jax.random.normal(key, shape, jnp.float32)
    if split:
        array = array * block_scale(key, shape, split, -0.22, 0.18)
    return jnp.clip(array, -bound, bound).astype(held_as)


def setup_inputs(seed: int = 0) -> dict:
    splits = jax.random.split(jax.random.key(seed), 9)
    out_grad = bell_draw(splits[0], (TARGETS, D_H), 1.0, 6.0, ((0, 32),))
    pre_act = bell_draw(splits[1], (TARGETS, D_H), 1.0, 6.0, ((0, 32),))
    batch_count = draw_batch_count(jax.random.fold_in(splits[8], 71), 0)
    layer_two = bell_draw(splits[3], (D_H, D_H), D_H ** -0.5, 0.25)
    hot_slots = touch_ends(ranked_ids(splits[4], (TARGETS, K_HOT), HOT, 2), jax.random.fold_in(splits[4], 3), 0, HOT - 1).astype(jnp.int32)
    cold_index = touch_ends(jax.random.randint(splits[5], (TARGETS, K_COLD), 0, C_DEV), jax.random.fold_in(splits[5], 1), 0, C_DEV - 1).astype(jnp.int32)
    hot_feats = bell_draw(splits[6], (HOT, D_IN), 1.0, 6.0, ((0, 4),))
    cold_feats = bell_draw(splits[7], (COLD, D_IN), 1.0, 6.0, ((0, 32),))
    return dict(out_grad=out_grad, pre_act=pre_act, batch_count=batch_count, layer_two=layer_two, hot_slots=hot_slots, cold_index=cold_index, hot_feats=hot_feats, cold_feats=cold_feats)


def device_terms(out_grad, pre_act, count, layer_two, hot_slots, cold_index, cold_feats):
    live = (jnp.arange(B_DEV, dtype=jnp.int32) < count)[:, None]
    masked = jnp.where(live, out_grad, jnp.zeros_like(out_grad))
    activ = jnp.maximum(pre_act, jnp.zeros_like(pre_act))
    grad_two = jnp.dot(activ.T, masked, preferred_element_type=jnp.float32)
    back = jnp.dot(masked, layer_two.T, preferred_element_type=jnp.float32)
    row_grad = jnp.where(pre_act > 0, back, jnp.zeros_like(back)).astype(jnp.bfloat16)
    rows_wide = row_grad.astype(jnp.float32)
    hot_part = jnp.zeros((HOT, D_H), jnp.float32)
    for column in range(K_HOT):
        hot_part = hot_part.at[hot_slots[:, column]].add(rows_wide)
    hot_part = (hot_part * (1.0 / FANOUT)).astype(jnp.bfloat16)
    cold_part = jnp.zeros((C_DEV, D_H), jnp.float32)
    for column in range(K_COLD):
        cold_part = cold_part.at[cold_index[:, column]].add(rows_wide)
    cold_part = (cold_part * (1.0 / FANOUT)).astype(jnp.bfloat16)
    grad_cold = jnp.dot(cold_feats.T, cold_part, preferred_element_type=jnp.float32)
    return hot_part, grad_cold, grad_two


def reference(out_grad, pre_act, batch_count, layer_two, hot_slots, cold_index, hot_feats, cold_feats):
    n_clq = N_CLIQUE
    n_cpy = N_COPY
    og = out_grad.reshape(n_clq, n_cpy, B_DEV, D_H)
    pa = pre_act.reshape(n_clq, n_cpy, B_DEV, D_H)
    bc = batch_count.reshape(n_clq, n_cpy)
    hs = hot_slots.reshape(n_clq, n_cpy, B_DEV, K_HOT)
    ci = cold_index.reshape(n_clq, n_cpy, B_DEV, K_COLD)
    cf = cold_feats.reshape(n_clq, n_cpy, C_DEV, D_IN)

    def per_copy(carry, j):
        grad_one, grad_two = carry

        def per_member(i, inner):
            hot_sum, g_one, g_two = inner
            hot_part, grad_cold, part_two = device_terms(og[i, j], pa[i, j], bc[i, j], layer_two, hs[i, j], ci[i, j], cf[i, j])
            return (hot_sum + hot_part.astype(jnp.float32), g_one + grad_cold, g_two + part_two)

        start = (jnp.zeros((HOT, D_H), jnp.float32), grad_one, grad_two)
        hot_sum, grad_one, grad_two = lax.fori_loop(0, n_clq, per_member, start)
        hot_b = hot_sum.astype(jnp.bfloat16)
        grad_one = grad_one + jnp.dot(hot_feats.T, hot_b, preferred_element_type=jnp.float32)
        return (grad_one, grad_two), None

    init = (jnp.zeros((D_IN, D_H), jnp.float32), jnp.zeros((D_H, D_H), jnp.float32))
    (grad_one, grad_two), _ = lax.scan(per_copy, init, jnp.arange(n_cpy, dtype=jnp.int32))
    return grad_one, grad_two
```

```python
import functools

import jax
import jax.numpy as jnp
from jax import lax
from jax.experimental import pallas as pl
from jax.experimental.pallas import tpu as pltpu
from jax.sharding import PartitionSpec as P

F32 = jnp.float32
BF16 = jnp.bfloat16
VMEM_LIMIT = 56 * 1024 * 1024
NIBBLES = 8


def whole():
    return pl.BlockSpec(memory_space=pltpu.VMEM)


def scalars():
    return pl.BlockSpec(memory_space=pltpu.SMEM)


def in_place():
    return pl.BlockSpec(memory_space=pl.ANY)


def params():
    return pltpu.CompilerParams(vmem_limit_bytes=VMEM_LIMIT)


def cost(flops, moved):
    return pl.CostEstimate(flops=int(flops), bytes_accessed=int(moved), transcendentals=0)


def transposed_dot(left, right):
    return lax.dot_general(left, right, (((0,), (0,)), ((), ())), preferred_element_type=F32)


def rows_kernel(count_ref, out_grad_ref, pre_act_ref, layer_two_ref, row_grad_ref, two_ref, sum_ref):
    step = pl.program_id(0)
    rows = out_grad_ref.shape[0]
    place = lax.broadcasted_iota(jnp.int32, out_grad_ref.shape, 0) + step * rows
    out_grad = out_grad_ref[...]
    masked = jnp.where(place < count_ref[0], out_grad, jnp.zeros_like(out_grad))
    pre_act = pre_act_ref[...]
    activ = jnp.maximum(pre_act, jnp.zeros_like(pre_act))
    part = transposed_dot(activ, masked)

    @pl.when(step == 0)
    def _():
        sum_ref[...] = part

    @pl.when(step > 0)
    def _():
        sum_ref[...] += part

    back = lax.dot_general(
        masked, layer_two_ref[...], (((1,), (1,)), ((), ())), preferred_element_type=F32
    )
    row_grad_ref[...] = jnp.where(pre_act > 0, back, jnp.zeros_like(back)).astype(BF16)

    @pl.when(step == pl.num_programs(0) - 1)
    def _():
        two_ref[...] = sum_ref[...].astype(BF16)


def row_gradients(batch_count, out_grad, pre_act, layer_two):
    rows, d_out = out_grad.shape
    d_h = pre_act.shape[1]
    block = min(256, rows)
    return pl.pallas_call(
        rows_kernel,
        grid=(rows // block,),
        in_specs=[
            scalars(),
            pl.BlockSpec((block, d_out), lambda i: (i, 0)),
            pl.BlockSpec((block, d_h), lambda i: (i, 0)),
            pl.BlockSpec((d_h, d_out), lambda i: (0, 0)),
        ],
        out_specs=[
            pl.BlockSpec((block, d_h), lambda i: (i, 0)),
            pl.BlockSpec((d_h, d_out), lambda i: (0, 0)),
        ],
        out_shape=[
            jax.ShapeDtypeStruct((rows, d_h), BF16),
            jax.ShapeDtypeStruct((d_h, d_out), BF16),
        ],
        scratch_shapes=[pltpu.VMEM((d_h, d_out), F32)],
        compiler_params=params(),
        cost_estimate=cost(4 * rows * d_h * d_out, 6 * rows * d_h),
        name="row_gradients",
    )(batch_count, out_grad, pre_act, layer_two)


def build_words(index_ref, word_ref, relabel):
    q_rows, rows = word_ref.shape
    terms = index_ref.shape[0]
    shift = q_rows.bit_length() - 1
    tall = min(128, q_rows)
    zero = jnp.zeros((tall, 128), jnp.int32)
    place = lax.broadcasted_iota(jnp.int32, (tall, 128), 0)

    @pl.loop(0, rows // 128)
    def _(tile):
        lanes = pl.ds(pl.multiple_of(tile * 128, 128), 128)
        index = relabel(index_ref[:, lanes])
        low = index & (q_rows - 1)
        unit = jnp.left_shift(jnp.ones_like(index), (index >> shift) * 4)
        for top in range(0, q_rows, tall):
            total = zero
            here = low - top
            for k in range(terms):
                total = total + jnp.where(place == here[k : k + 1, :], unit[k : k + 1, :], zero)
            word_ref[top : top + tall, lanes] = total


def counted_sum(word_ref, row_grad_ref, which, scale):
    counts = lax.shift_right_logical(word_ref[...], which * 4) & 15
    counts = counts.astype(F32).astype(BF16)
    return jnp.dot(counts, row_grad_ref[...], preferred_element_type=F32) * scale


def hot_kernel(
    scale, shard_bits, place_ref, index_ref, row_grad_ref, keep_ref, send_ref, word_ref
):
    q_rows = word_ref.shape[0]
    half_rows = keep_ref.shape[0]
    own_shard, own_core = place_ref[0], place_ref[1]
    part_bits = shard_bits - 1

    def relabel(index):
        row = index & ((1 << part_bits) - 1)
        half = ((index >> part_bits) & 1) ^ own_core
        shard = (index >> shard_bits) ^ own_shard
        return half * half_rows + (shard << part_bits) + row

    build_words(index_ref, word_ref, relabel)
    for out_ref, first in ((keep_ref, 0), (send_ref, NIBBLES // 2)):

        @pl.loop(0, NIBBLES // 2)
        def _(m, out_ref=out_ref, first=first):
            found = counted_sum(word_ref, row_grad_ref, m + first, scale)
            out_ref[pl.ds(pl.multiple_of(m * q_rows, q_rows), q_rows), :] = found.astype(BF16)


def hot_sums(place, index, row_grad, hot_total, shard_rows, fanout):
    terms, rows = index.shape
    d_h = row_grad.shape[1]
    q_rows = hot_total // NIBBLES
    half = jax.ShapeDtypeStruct((hot_total // 2, d_h), BF16)
    return pl.pallas_call(
        functools.partial(hot_kernel, 1.0 / fanout, shard_rows.bit_length() - 1),
        in_specs=[scalars(), whole(), whole()],
        out_specs=[whole(), whole()],
        out_shape=[half, half],
        scratch_shapes=[pltpu.VMEM((q_rows, rows), jnp.int32)],
        compiler_params=params(),
        cost_estimate=cost(2 * hot_total * rows * d_h, 4 * hot_total * d_h),
        name="hot_sums",
    )(place, index, row_grad)


def cold_kernel(
    scale, index_ref, row_grad_ref, feats_ref, grad_ref, word_ref, sums_ref, held_ref, sem
):
    fetch = pltpu.make_async_copy(feats_ref, held_ref, sem)
    fetch.start()
    q_rows = word_ref.shape[0]
    build_words(index_ref, word_ref, lambda index: index)

    @pl.loop(0, NIBBLES)
    def _(m):
        found = counted_sum(word_ref, row_grad_ref, m, scale)
        sums_ref[pl.ds(pl.multiple_of(m * q_rows, q_rows), q_rows), :] = found.astype(BF16)

    fetch.wait()
    d_in = held_ref.shape[1]
    for left in range(0, d_in, 256):
        grad_ref[left : left + 256, :] = transposed_dot(held_ref[:, left : left + 256], sums_ref[...])


def cold_grad(index, row_grad, feats, fanout):
    terms, rows = index.shape
    d_h = row_grad.shape[1]
    cold_rows, d_in = feats.shape
    q_rows = cold_rows // NIBBLES
    return pl.pallas_call(
        functools.partial(cold_kernel, 1.0 / fanout),
        in_specs=[whole(), whole(), in_place()],
        out_specs=whole(),
        out_shape=jax.ShapeDtypeStruct((d_in, d_h), F32),
        scratch_shapes=[
            pltpu.VMEM((q_rows, rows), jnp.int32),
            pltpu.VMEM((cold_rows, d_h), BF16),
            pltpu.VMEM((cold_rows, d_in), BF16),
            pltpu.SemaphoreType.DMA,
        ],
        compiler_params=params(),
        cost_estimate=cost(2 * cold_rows * d_h * (rows + d_in), 2 * cold_rows * (d_in + d_h)),
        name="cold_grad",
    )(index, row_grad, feats)


def join_kernel(parts, place_ref, cold_ref, keep_ref, other_ref, *rest):
    feats, (own_ref, send_ref, total_ref) = rest[:parts], rest[parts:]
    own_core = place_ref[1]
    depth = feats[0].shape[0]
    d_in, d_h = total_ref.shape
    total_ref[...] = cold_ref[...]
    for k in range(parts):
        rows = slice(k * depth, (k + 1) * depth)
        sums = (keep_ref[rows, :].astype(F32) + other_ref[rows, :].astype(F32)).astype(BF16)
        for left in range(0, d_in, 256):
            total_ref[left : left + 256, :] += transposed_dot(feats[k][:, left : left + 256], sums)
    wide = d_h // 2
    mine = pl.ds(pl.multiple_of(own_core * wide, wide), wide)
    twin = pl.ds(pl.multiple_of((1 - own_core) * wide, wide), wide)
    own_ref[...] = total_ref[:, mine].astype(BF16)
    send_ref[...] = total_ref[:, twin].astype(BF16)


def join(place, cold, keep, other, feats):
    d_in, d_h = cold.shape
    half = jax.ShapeDtypeStruct((d_in, d_h // 2), BF16)
    return pl.pallas_call(
        functools.partial(join_kernel, len(feats)),
        in_specs=[scalars()] + [whole()] * (3 + len(feats)),
        out_specs=[whole(), whole()],
        out_shape=[half, half],
        scratch_shapes=[pltpu.VMEM((d_in, d_h), F32)],
        compiler_params=params(),
        cost_estimate=cost(2 * keep.shape[0] * d_h * d_in, 4 * d_in * d_h),
        name="join",
    )(place, cold, keep, other, *feats)


def split_kernel(which, terms, pieces, place_ref, *rest):
    inputs, outputs = rest[:terms], rest[terms:]
    own = place_ref[which] if pieces > 1 else 0
    rows = outputs[0].shape[0]
    for k in range(pieces):
        at = pl.ds(pl.multiple_of((own ^ k) * rows, rows), rows)
        total = inputs[0][at, :].astype(F32)
        for other in inputs[1:]:
            total = total + other[at, :].astype(F32)
        outputs[k][...] = total.astype(BF16)


def add_and_split(place, which, arrays, pieces):
    rows, wide = arrays[0].shape
    piece = jax.ShapeDtypeStruct((rows // pieces, wide), BF16)
    return pl.pallas_call(
        functools.partial(split_kernel, which, len(arrays), pieces),
        in_specs=[scalars()] + [whole()] * len(arrays),
        out_specs=[whole()] * pieces,
        out_shape=[piece] * pieces,
        compiler_params=params(),
        cost_estimate=cost(len(arrays) * rows * wide, 2 * len(arrays) * rows * wide),
        name="add_and_split",
    )(place, *arrays)


def lay_kernel(which, by_column, place_ref, *rest):
    inputs, out_ref = rest[:-1], rest[-1]
    own = place_ref[which]
    rows, wide = inputs[0].shape
    for k, piece in enumerate(inputs):
        at = (own ^ k) * (wide if by_column else rows)
        value = piece[...].astype(out_ref.dtype)
        if by_column:
            out_ref[:, pl.ds(pl.multiple_of(at, wide), wide)] = value
        else:
            out_ref[pl.ds(pl.multiple_of(at, rows), rows), :] = value


def lay(place, which, arrays, by_column, dtype):
    rows, wide = arrays[0].shape
    pieces = len(arrays)
    shape = (rows, wide * pieces) if by_column else (rows * pieces, wide)
    return pl.pallas_call(
        functools.partial(lay_kernel, which, by_column),
        in_specs=[scalars()] + [whole()] * pieces,
        out_specs=whole(),
        out_shape=jax.ShapeDtypeStruct(shape, dtype),
        compiler_params=params(),
        cost_estimate=cost(0, 4 * pieces * rows * wide),
        name="lay",
    )(place, *arrays)


def exchange(array, axis, step):
    size = lax.axis_size(axis)
    return lax.ppermute(array, axis, [(source, source ^ step) for source in range(size)])


def on_device(
    out_grad, pre_act, batch_count, layer_two, hot_slots, cold_index, hot_feats, cold_feats
):
    n_clique = lax.axis_size("clique")
    n_copy = lax.axis_size("copy")
    n_deep = n_copy // 2
    shard_rows = hot_feats.shape[0]
    fanout = hot_slots.shape[1] + cold_index.shape[1]
    d_in = hot_feats.shape[1]
    copy_at = lax.axis_index("copy")
    place = jnp.stack([lax.axis_index("clique"), copy_at & 1, copy_at >> 1]).astype(jnp.int32)

    half_feats = lax.dynamic_slice_in_dim(
        hot_feats, (copy_at & 1) * (shard_rows // 2), shard_rows // 2, 0
    )
    feats = [half_feats] + [exchange(half_feats, "clique", k) for k in range(1, n_clique)]

    row_grad, two = row_gradients(batch_count, out_grad, pre_act, layer_two)
    grad_two = lax.psum(two, ("clique", "copy")).astype(F32)

    keep, send = hot_sums(
        place, hot_slots.T, row_grad, shard_rows * n_clique, shard_rows, fanout
    )
    other = exchange(send, "copy", 1)
    cold = cold_grad(cold_index.T, row_grad, cold_feats, fanout)
    own, twin = join(place, cold, keep, other, feats)
    fetched = exchange(twin, "copy", 1)
    if d_in % (16 * n_clique * n_deep) == 0:
        pieces = add_and_split(place, 0, [own, fetched], n_clique)
        got = [pieces[0]] + [exchange(pieces[k], "clique", k) for k in range(1, n_clique)]
        pieces = add_and_split(place, 2, got, n_deep)
        got = [pieces[0]] + [exchange(pieces[k], "copy", 2 * k) for k in range(1, n_deep)]
        (total,) = add_and_split(place, 2, got, 1)
        got = [total] + [exchange(total, "copy", 2 * k) for k in range(1, n_deep)]
        total = lay(place, 2, got, False, BF16)
        got = [total] + [exchange(total, "clique", k) for k in range(1, n_clique)]
        total = lay(place, 0, got, False, BF16)
    else:
        (total,) = add_and_split(place, 0, [own, fetched], 1)
        groups = [[j for j in range(n_copy) if j % 2 == core] for core in range(2)]
        total = lax.psum(total, "clique")
        total = lax.psum(total, "copy", axis_index_groups=groups)
    grad_one = lay(place, 1, [total, exchange(total, "copy", 1)], True, F32)
    return grad_one, grad_two


def solution(mesh):
    placed = (
        P(("clique", "copy"), None),
        P(("clique", "copy"), None),
        P(("clique", "copy")),
        P(),
        P(("clique", "copy"), None),
        P(("clique", "copy"), None),
        P("clique", None),
        P(("clique", "copy"), None),
    )
    return jax.shard_map(
        on_device, mesh=mesh, in_specs=placed, out_specs=(P(), P()), check_vma=False
    )
```

```python
import functools

import jax
import jax.numpy as jnp
from jax import lax
from jax.experimental import pallas as pl
from jax.experimental.pallas import tpu as pltpu
from jax.sharding import PartitionSpec as P

F32 = jnp.float32
BF16 = jnp.bfloat16
VMEM_LIMIT = 56 * 1024 * 1024
NIBBLES = 8


def whole():
    return pl.BlockSpec(memory_space=pltpu.VMEM)


def scalars():
    return pl.BlockSpec(memory_space=pltpu.SMEM)


def in_place():
    return pl.BlockSpec(memory_space=pl.ANY)


def params():
    return pltpu.CompilerParams(vmem_limit_bytes=VMEM_LIMIT)


def cost(flops, moved):
    return pl.CostEstimate(flops=int(flops), bytes_accessed=int(moved), transcendentals=0)


def transposed_dot(left, right):
    return lax.dot_general(left, right, (((0,), (0,)), ((), ())), preferred_element_type=F32)


def halves(total_ref, own_ref, send_ref, own_core):
    wide = own_ref.shape[1]
    mine = pl.ds(pl.multiple_of(own_core * wide, wide), wide)
    twin = pl.ds(pl.multiple_of((1 - own_core) * wide, wide), wide)
    own_ref[...] = total_ref[:, mine].astype(BF16)
    send_ref[...] = total_ref[:, twin].astype(BF16)


def rows_kernel(
    place_ref, count_ref, out_grad_ref, pre_act_ref, layer_two_ref,
    row_grad_ref, own_ref, send_ref, sum_ref,
):
    step = pl.program_id(0)
    rows = out_grad_ref.shape[0]
    place = lax.broadcasted_iota(jnp.int32, out_grad_ref.shape, 0) + step * rows
    out_grad = out_grad_ref[...]
    masked = jnp.where(place < count_ref[0], out_grad, jnp.zeros_like(out_grad))
    pre_act = pre_act_ref[...]
    activ = jnp.maximum(pre_act, jnp.zeros_like(pre_act))
    part = transposed_dot(activ, masked)

    @pl.when(step == 0)
    def _():
        sum_ref[...] = part

    @pl.when(step > 0)
    def _():
        sum_ref[...] += part

    back = lax.dot_general(
        masked, layer_two_ref[...], (((1,), (1,)), ((), ())), preferred_element_type=F32
    )
    row_grad_ref[...] = jnp.where(pre_act > 0, back, jnp.zeros_like(back)).astype(BF16)

    @pl.when(step == pl.num_programs(0) - 1)
    def _():
        halves(sum_ref, own_ref, send_ref, place_ref[1])


def row_gradients(place, batch_count, out_grad, pre_act, layer_two):
    rows, d_out = out_grad.shape
    d_h = pre_act.shape[1]
    block = min(512, rows)
    half = jax.ShapeDtypeStruct((d_h, d_out // 2), BF16)
    half_spec = pl.BlockSpec((d_h, d_out // 2), lambda i: (0, 0))
    return pl.pallas_call(
        rows_kernel,
        grid=(rows // block,),
        in_specs=[
            scalars(),
            scalars(),
            pl.BlockSpec((block, d_out), lambda i: (i, 0)),
            pl.BlockSpec((block, d_h), lambda i: (i, 0)),
            pl.BlockSpec((d_h, d_out), lambda i: (0, 0)),
        ],
        out_specs=[pl.BlockSpec((block, d_h), lambda i: (i, 0)), half_spec, half_spec],
        out_shape=[jax.ShapeDtypeStruct((rows, d_h), BF16), half, half],
        scratch_shapes=[pltpu.VMEM((d_h, d_out), F32)],
        compiler_params=params(),
        cost_estimate=cost(0, 0),
        name="row_gradients",
    )(place, batch_count, out_grad, pre_act, layer_two)


def build_words(index_ref, word_ref, relabel):
    q_rows, rows = word_ref.shape
    terms = index_ref.shape[0]
    shift = q_rows.bit_length() - 1
    tall = min(128, q_rows)
    zero = jnp.zeros((tall, 128), jnp.int32)
    place = lax.broadcasted_iota(jnp.int32, (tall, 128), 0)

    @pl.loop(0, rows // 128)
    def _(tile):
        lanes = pl.ds(pl.multiple_of(tile * 128, 128), 128)
        index = relabel(index_ref[:, lanes])
        low = index & (q_rows - 1)
        unit = jnp.left_shift(jnp.ones_like(index), (index >> shift) * 4)
        for top in range(0, q_rows, tall):
            total = zero
            here = low - top
            for k in range(terms):
                total = total + jnp.where(place == here[k : k + 1, :], unit[k : k + 1, :], zero)
            word_ref[top : top + tall, lanes] = total


def counts_of(word_ref, first, count_ref):
    q_rows = word_ref.shape[0]
    for k in range(2):
        counts = lax.shift_right_logical(word_ref[...], (first + k) * 4) & 15
        count_ref[k * q_rows : (k + 1) * q_rows, :] = counts.astype(F32).astype(BF16)


def all_sums(word_ref, row_grad_ref, counts, scale, out_refs):
    tall = counts[0].shape[0]
    counts_of(word_ref, 0, counts[0])
    turns = NIBBLES // 4
    per_ref = turns // len(out_refs)
    for place, out_ref in enumerate(out_refs):

        @pl.loop(0, per_ref)
        def _(turn, place=place, out_ref=out_ref):
            first = (turn + place * per_ref) * 4
            for k in range(2):
                ahead = jnp.minimum(first + 2 * k + 2, NIBBLES - 2)
                found = jnp.dot(counts[k][...], row_grad_ref[...], preferred_element_type=F32)
                counts_of(word_ref, ahead, counts[1 - k])
                at = pl.multiple_of((turn * 2 + k) * tall, tall)
                out_ref[pl.ds(at, tall), :] = (found * scale).astype(BF16)


def table_scratch(q_rows, rows):
    return [
        pltpu.VMEM((q_rows, rows), jnp.int32),
        pltpu.VMEM((2 * q_rows, rows), BF16),
        pltpu.VMEM((2 * q_rows, rows), BF16),
    ]


def hot_kernel(scale, shard_bits, place_ref, index_ref, row_grad_ref, *rest):
    send_ref, keep_ref, word_ref, *counts = rest[-5:]
    half_rows = keep_ref.shape[0]
    own_shard, own_core = place_ref[0], place_ref[1]
    part_bits = shard_bits - 1

    def relabel(index):
        row = index & ((1 << part_bits) - 1)
        half = ((index >> part_bits) & 1) ^ own_core ^ 1
        shard = (index >> shard_bits) ^ own_shard
        return half * half_rows + (shard << part_bits) + row

    build_words(index_ref, word_ref, relabel)
    all_sums(word_ref, row_grad_ref, counts, scale, [send_ref, keep_ref])


def hot_sums(place, index, row_grad, arrived, hot_total, shard_rows, fanout):
    terms, rows = index.shape
    d_h = row_grad.shape[1]
    q_rows = hot_total // NIBBLES
    half = jax.ShapeDtypeStruct((hot_total // 2, d_h), BF16)
    return pl.pallas_call(
        functools.partial(hot_kernel, 1.0 / fanout, shard_rows.bit_length() - 1),
        in_specs=[scalars(), whole(), whole()] + [in_place()] * len(arrived),
        out_specs=[whole(), whole()],
        out_shape=[half, half],
        scratch_shapes=table_scratch(q_rows, rows),
        compiler_params=params(),
        cost_estimate=cost(0, 0),
        name="hot_sums",
    )(place, index, row_grad, *arrived)


def cold_kernel(
    scale, index_ref, row_grad_ref, feats_ref, grad_ref, sums_ref, held_ref, sem, word_ref, *counts
):
    fetch = pltpu.make_async_copy(feats_ref, held_ref, sem)
    fetch.start()
    build_words(index_ref, word_ref, lambda index: index)
    all_sums(word_ref, row_grad_ref, counts, scale, [sums_ref])
    fetch.wait()
    d_in = held_ref.shape[1]
    for left in range(0, d_in, 256):
        grad_ref[left : left + 256, :] = transposed_dot(held_ref[:, left : left + 256], sums_ref[...])


def cold_grad(index, row_grad, feats, fanout):
    terms, rows = index.shape
    d_h = row_grad.shape[1]
    cold_rows, d_in = feats.shape
    q_rows = cold_rows // NIBBLES
    return pl.pallas_call(
        functools.partial(cold_kernel, 1.0 / fanout),
        in_specs=[whole(), whole(), in_place()],
        out_specs=whole(),
        out_shape=jax.ShapeDtypeStruct((d_in, d_h), F32),
        scratch_shapes=[
            pltpu.VMEM((cold_rows, d_h), BF16),
            pltpu.VMEM((cold_rows, d_in), BF16),
            pltpu.SemaphoreType.DMA,
        ]
        + table_scratch(q_rows, rows),
        compiler_params=params(),
        cost_estimate=cost(0, 0),
        name="cold_grad",
    )(index, row_grad, feats)


def join_kernel(parts, place_ref, cold_ref, keep_ref, other_ref, two_ref, fetched_ref, *rest):
    feats, (own_ref, send_ref, pair_ref, total_ref) = rest[:parts], rest[parts:]
    d_in = total_ref.shape[0]
    total_ref[...] = cold_ref[...]
    base = 0
    for part in feats:
        depth = part.shape[0]
        rows = slice(base, base + depth)
        sums = (keep_ref[rows, :].astype(F32) + other_ref[rows, :].astype(F32)).astype(BF16)
        for left in range(0, d_in, 256):
            total_ref[left : left + 256, :] += transposed_dot(part[:, left : left + 256], sums)
        base += depth
    halves(total_ref, own_ref, send_ref, place_ref[1])
    pair_ref[...] = (two_ref[...].astype(F32) + fetched_ref[...].astype(F32)).astype(BF16)


def join(place, cold, keep, other, two, fetched_two, feats):
    d_in, d_h = cold.shape
    half = jax.ShapeDtypeStruct((d_in, d_h // 2), BF16)
    return pl.pallas_call(
        functools.partial(join_kernel, len(feats)),
        in_specs=[scalars()] + [whole()] * (5 + len(feats)),
        out_specs=[whole()] * 3,
        out_shape=[half, half, jax.ShapeDtypeStruct(two.shape, BF16)],
        scratch_shapes=[pltpu.VMEM((d_in, d_h), F32)],
        compiler_params=params(),
        cost_estimate=cost(2 * keep.shape[0] * d_h * d_in, 4 * d_in * d_h),
        name="join",
    )(place, cold, keep, other, two, fetched_two, *feats)


def pair_kernel(members, one_ref, other_ref, two_ref, out_ref):
    rows_one, rows_two = one_ref.shape[0] // members, two_ref.shape[0] // members
    base = 0
    for member in range(members):
        here = slice(member * rows_one, (member + 1) * rows_one)
        total = one_ref[here, :].astype(F32) + other_ref[here, :].astype(F32)
        out_ref[base : base + rows_one, :] = total.astype(BF16)
        base += rows_one
        out_ref[base : base + rows_two, :] = two_ref[
            member * rows_two : (member + 1) * rows_two, :
        ]
        base += rows_two


def pair_sums(one, other, two, members):
    wide = one.shape[1]
    rows = one.shape[0] + two.shape[0]
    return pl.pallas_call(
        functools.partial(pair_kernel, members),
        in_specs=[whole()] * 3,
        out_specs=whole(),
        out_shape=jax.ShapeDtypeStruct((rows, wide), BF16),
        compiler_params=params(),
        cost_estimate=cost(0, 6 * rows * wide),
        name="pair_sums",
    )(one, other, two)


def share_kernel(members, copies, in_ref, out_ref):
    rows = in_ref.shape[0] // members
    total = in_ref[:rows, :].astype(F32)
    for k in range(1, members):
        total = total + in_ref[k * rows : (k + 1) * rows, :].astype(F32)
    total = total.astype(BF16)
    for k in range(copies):
        out_ref[k * rows : (k + 1) * rows, :] = total


def share_sum(array, members, copies):
    rows, wide = array.shape
    return pl.pallas_call(
        functools.partial(share_kernel, members, copies),
        in_specs=[whole()],
        out_specs=whole(),
        out_shape=jax.ShapeDtypeStruct((rows // members * copies, wide), BF16),
        compiler_params=params(),
        cost_estimate=cost(0, 4 * rows * wide),
        name="share_sum",
    )(array)


def lay_kernel(members, place_ref, own_ref, other_ref, *out_refs):
    own_core = place_ref[1]
    wide = own_ref.shape[1]
    for ref, core in ((own_ref, own_core), (other_ref, 1 - own_core)):
        lanes = pl.ds(pl.multiple_of(core * wide, wide), wide)
        base = 0
        for member in range(members):
            for out_ref in out_refs:
                rows = out_ref.shape[0] // members
                out_ref[member * rows : (member + 1) * rows, lanes] = ref[
                    base : base + rows, :
                ].astype(F32)
                base += rows


def lay(place, own, other, members, rows_of):
    wide = own.shape[1]
    return pl.pallas_call(
        functools.partial(lay_kernel, members),
        in_specs=[scalars(), whole(), whole()],
        out_specs=[whole()] * len(rows_of),
        out_shape=[jax.ShapeDtypeStruct((rows, 2 * wide), F32) for rows in rows_of],
        compiler_params=params(),
        cost_estimate=cost(0, 12 * own.shape[0] * wide),
        name="lay",
    )(place, own, other)


def exchange(array, axis, step):
    size = lax.axis_size(axis)
    return lax.ppermute(array, axis, [(source, source ^ step) for source in range(size)])


def gather_feats(own):
    members = lax.axis_size("clique")
    if members != 4:
        return [own] + [exchange(own, "clique", k) for k in range(1, members)]
    one, two = exchange(own, "clique", 1), exchange(own, "clique", 2)
    middle = own.shape[0] // 2
    top = exchange(two[:middle], "clique", 1)
    bottom = exchange(one[middle:], "clique", 2)
    return [own, one, two, top, bottom]


def swap(array, axis, groups=None):
    return lax.all_to_all(array, axis, 0, 0, axis_index_groups=groups, tiled=True)


def on_device(
    out_grad, pre_act, batch_count, layer_two, hot_slots, cold_index, hot_feats, cold_feats
):
    n_clique = lax.axis_size("clique")
    n_copy = lax.axis_size("copy")
    n_deep = n_copy // 2
    deep = [[j for j in range(n_copy) if j % 2 == core] for core in range(2)]
    shard_rows, d_in = hot_feats.shape
    d_h = pre_act.shape[1]
    fanout = hot_slots.shape[1] + cold_index.shape[1]
    copy_at = lax.axis_index("copy")
    place = jnp.stack([lax.axis_index("clique"), copy_at & 1]).astype(jnp.int32)

    half_feats = lax.dynamic_slice_in_dim(
        hot_feats, (copy_at & 1) * (shard_rows // 2), shard_rows // 2, 0
    )
    feats = gather_feats(half_feats)

    row_grad, own_two, twin_two = row_gradients(place, batch_count, out_grad, pre_act, layer_two)
    fetched_two = exchange(twin_two, "copy", 1)
    send, keep = hot_sums(
        place, hot_slots.T, row_grad, feats[1:3], shard_rows * n_clique, shard_rows, fanout
    )
    other = exchange(send, "copy", 1)
    cold = cold_grad(cold_index.T, row_grad, cold_feats, fanout)
    own_one, twin_one, two = join(place, cold, keep, other, own_two, fetched_two, feats)
    total = pair_sums(own_one, exchange(twin_one, "copy", 1), two, n_clique)
    if total.shape[0] % (16 * n_clique * n_deep) == 0:
        total = share_sum(swap(total, "clique"), n_clique, 1)
        total = share_sum(swap(total, "copy", deep), n_deep, n_deep)
        total = swap(total, "copy", deep)
        total = swap(jnp.tile(total, (n_clique, 1)), "clique")
    else:
        total = lax.psum(total, "clique")
        total = lax.psum(total, "copy", axis_index_groups=deep)
    grad_one, grad_two = lay(place, total, exchange(total, "copy", 1), n_clique, (d_in, d_h))
    return grad_one, grad_two


def solution(mesh):
    placed = (
        P(("clique", "copy"), None),
        P(("clique", "copy"), None),
        P(("clique", "copy")),
        P(),
        P(("clique", "copy"), None),
        P(("clique", "copy"), None),
        P("clique", None),
        P(("clique", "copy"), None),
    )
    return jax.shard_map(
        on_device, mesh=mesh, in_specs=placed, out_specs=(P(), P()), check_vma=False
    )
```

```python
import functools

import jax
import jax.numpy as jnp
from jax import lax
from jax.experimental import pallas as pl
from jax.experimental.pallas import tpu as pltpu
from jax.sharding import PartitionSpec as P

F32 = jnp.float32
BF16 = jnp.bfloat16
I16 = jnp.int16
FIELDS = 4
TILE = 16


def whole():
    return pl.BlockSpec(memory_space=pltpu.VMEM)


def scalars():
    return pl.BlockSpec(memory_space=pltpu.SMEM)


def in_place():
    return pl.BlockSpec(memory_space=pl.ANY)


def params(mebibytes):
    return pltpu.CompilerParams(vmem_limit_bytes=mebibytes << 20)


def cost(flops, moved):
    return pl.CostEstimate(flops=int(flops), bytes_accessed=int(moved), transcendentals=0)


def transposed_dot(left, right):
    return lax.dot_general(left, right, (((0,), (0,)), ((), ())), preferred_element_type=F32)


def halves(total_ref, own_ref, send_ref, own_core):
    wide = own_ref.shape[1]
    mine = pl.ds(pl.multiple_of(own_core * wide, wide), wide)
    twin = pl.ds(pl.multiple_of((1 - own_core) * wide, wide), wide)
    own_ref[...] = total_ref[:, mine].astype(BF16)
    send_ref[...] = total_ref[:, twin].astype(BF16)


def build_words(index, q_rows, store):
    terms = index.shape[0]
    shift = q_rows.bit_length() - 1
    low = index & (q_rows - 1)
    unit = jnp.left_shift(jnp.ones_like(index), (index >> shift) * 4)
    tall = min(256, q_rows) // TILE
    shape = (tall, TILE, 128)
    place = lax.broadcasted_iota(jnp.int32, shape, 0) * TILE + lax.broadcasted_iota(jnp.int32, shape, 1)
    place = place.astype(I16)

    def tile(row):
        return jnp.broadcast_to(row, (TILE, 128)).astype(I16)[None]

    lows = [tile(low[k : k + 1, :]) for k in range(terms)]
    units = [tile(unit[k : k + 1, :]) for k in range(terms)]
    zero = jnp.zeros(shape, I16)
    for top in range(0, q_rows // TILE, tall):
        total = zero
        for k in range(terms):
            total = total + jnp.where(place == lows[k] - I16(top * TILE), units[k], zero)
        store(top, tall, total)


def unpack(word_ref, field, count_ref):
    counts = (word_ref[...] >> (field * 4)) & 15
    count_ref[...] = counts.astype(BF16).reshape(count_ref.shape)


def rows_kernel(
    shard_bits, half_rows,
    place_ref, count_ref, out_grad_ref, pre_act_ref, layer_two_ref, index_ref,
    row_grad_ref, own_ref, send_ref, word_ref, sum_ref, masked_ref,
):
    step = pl.program_id(0)
    rows = out_grad_ref.shape[0]
    live = count_ref[0] - step * rows

    @pl.when(live >= rows)
    def _():
        masked_ref[...] = out_grad_ref[...]

    @pl.when(live < rows)
    def _():
        out_grad = out_grad_ref[...].astype(F32)
        place = lax.broadcasted_iota(jnp.int32, out_grad.shape, 0)
        masked_ref[...] = jnp.where(place < live, out_grad, jnp.zeros_like(out_grad)).astype(BF16)

    @pl.when(step == 0)
    def _():
        sum_ref[...] = jnp.zeros_like(sum_ref)

    own_shard, own_core = place_ref[0], place_ref[1]
    part_bits = shard_bits - 1
    for left in range(0, rows, 128):
        index = index_ref[:, left : left + 128]
        row = index & ((1 << part_bits) - 1)
        half = ((index >> part_bits) & 1) ^ own_core ^ 1
        index = half * half_rows + (((index >> shard_bits) ^ own_shard) << part_bits) + row

        def store(top, tall, words, left=left):
            word_ref[top : top + tall, :, left : left + 128] = words

        build_words(index, word_ref.shape[0] * TILE, store)

    pre_act = pre_act_ref[...]
    activ = jnp.maximum(pre_act, jnp.zeros_like(pre_act))
    sum_ref[...] += transposed_dot(activ, masked_ref[...])
    back = lax.dot_general(
        masked_ref[...], layer_two_ref[...], (((1,), (1,)), ((), ())), preferred_element_type=F32
    )
    row_grad_ref[...] = jnp.where(
        pre_act.astype(F32) > 0, back, jnp.zeros_like(back)
    ).astype(BF16)

    @pl.when(step == pl.num_programs(0) - 1)
    def _():
        halves(sum_ref, own_ref, send_ref, own_core)


def row_gradients(place, batch_count, out_grad, pre_act, layer_two, index, hot_total, shard_rows):
    rows, d_out = out_grad.shape
    d_h = pre_act.shape[1]
    block = min(512, rows)
    deep = hot_total // FIELDS // TILE
    half = jax.ShapeDtypeStruct((d_h, d_out // 2), BF16)
    half_spec = pl.BlockSpec((d_h, d_out // 2), lambda i: (0, 0))
    return pl.pallas_call(
        functools.partial(rows_kernel, shard_rows.bit_length() - 1, hot_total // 2),
        grid=(rows // block,),
        in_specs=[
            scalars(),
            scalars(),
            pl.BlockSpec((block, d_out), lambda i: (i, 0)),
            pl.BlockSpec((block, d_h), lambda i: (i, 0)),
            pl.BlockSpec((d_h, d_out), lambda i: (0, 0)),
            pl.BlockSpec((index.shape[0], block), lambda i: (0, i)),
        ],
        out_specs=[
            pl.BlockSpec((block, d_h), lambda i: (i, 0)),
            half_spec,
            half_spec,
            pl.BlockSpec((deep, TILE, block), lambda i: (0, 0, i)),
        ],
        out_shape=[
            jax.ShapeDtypeStruct((rows, d_h), BF16),
            half,
            half,
            jax.ShapeDtypeStruct((deep, TILE, rows), I16),
        ],
        scratch_shapes=[pltpu.VMEM((d_h, d_out), F32), pltpu.VMEM((block, d_out), BF16)],
        compiler_params=params(24),
        cost_estimate=cost(0, 0),
        name="row_gradients",
    )(place, batch_count, out_grad, pre_act, layer_two, index)


def hot_kernel(scale, arrived, word_ref, row_grad_ref, index_ref, *rest):
    send_ref, keep_ref, cold_word_ref, *counts = rest[arrived:]
    tall, rows = counts[0].shape
    tiles = rows // 128 // FIELDS
    unpack(word_ref, 0, counts[0])
    for field in range(FIELDS):
        found = jnp.dot(counts[field % 2][...], row_grad_ref[...], preferred_element_type=F32)
        if field + 1 < FIELDS:
            unpack(word_ref, field + 1, counts[(field + 1) % 2])
        for tile in range(field * tiles, (field + 1) * tiles):
            lanes = slice(tile * 128, (tile + 1) * 128)

            def store(top, deep, words, lanes=lanes):
                cold_word_ref[top : top + deep, :, lanes] = words

            build_words(index_ref[:, lanes], cold_word_ref.shape[0] * TILE, store)
        out_ref = (send_ref, keep_ref)[field // 2]
        out_ref[field % 2 * tall : (field % 2 + 1) * tall, :] = (found * scale).astype(BF16)


def hot_sums(words, row_grad, cold_index, arrived, cold_rows, fanout):
    rows, d_h = row_grad.shape
    q_rows = words.shape[0] * TILE
    half = jax.ShapeDtypeStruct((q_rows * FIELDS // 2, d_h), BF16)
    return pl.pallas_call(
        functools.partial(hot_kernel, 1.0 / fanout, len(arrived)),
        in_specs=[whole(), whole(), whole()] + [in_place()] * len(arrived),
        out_specs=[whole()] * 3,
        out_shape=[
            half,
            half,
            jax.ShapeDtypeStruct((cold_rows // FIELDS // TILE, TILE, rows), I16),
        ],
        scratch_shapes=[pltpu.VMEM((q_rows, rows), BF16)] * 2,
        compiler_params=params(40),
        cost_estimate=cost(0, 0),
        name="hot_sums",
    )(words, row_grad, cold_index, *arrived)


def cold_kernel(scale, word_ref, row_grad_ref, feats_ref, grad_ref, sums_ref, held_ref, sem, *counts):
    fetch = pltpu.make_async_copy(feats_ref, held_ref, sem)
    fetch.start()
    tall = counts[0].shape[0]

    def add_product(field):
        rows = slice(field * tall, (field + 1) * tall)
        part = transposed_dot(held_ref[rows, :], sums_ref[rows, :])
        grad_ref[...] = part if field == 0 else grad_ref[...] + part

    unpack(word_ref, 0, counts[0])
    for field in range(FIELDS):
        found = jnp.dot(counts[field % 2][...], row_grad_ref[...], preferred_element_type=F32)
        if field + 1 < FIELDS:
            unpack(word_ref, field + 1, counts[(field + 1) % 2])
        if field == 1:
            fetch.wait()
        if field > 0:
            add_product(field - 1)
        sums_ref[field * tall : (field + 1) * tall, :] = (found * scale).astype(BF16)
    add_product(FIELDS - 1)


def cold_grad(words, row_grad, feats, fanout):
    rows, d_h = row_grad.shape
    cold_rows, d_in = feats.shape
    q_rows = cold_rows // FIELDS
    return pl.pallas_call(
        functools.partial(cold_kernel, 1.0 / fanout),
        in_specs=[whole(), whole(), in_place()],
        out_specs=whole(),
        out_shape=jax.ShapeDtypeStruct((d_in, d_h), F32),
        scratch_shapes=[
            pltpu.VMEM((cold_rows, d_h), BF16),
            pltpu.VMEM((cold_rows, d_in), BF16),
            pltpu.SemaphoreType.DMA,
            pltpu.VMEM((q_rows, rows), BF16),
            pltpu.VMEM((q_rows, rows), BF16),
        ],
        compiler_params=params(40),
        cost_estimate=cost(0, 0),
        name="cold_grad",
    )(words, row_grad, feats)


def join_kernel(parts, place_ref, cold_ref, keep_ref, other_ref, two_ref, fetched_ref, *rest):
    feats, (own_ref, send_ref, pair_ref) = rest[:parts], rest[parts:]
    own_core = place_ref[1]
    d_in, d_h = cold_ref.shape
    wide = d_h // 2
    sums = (keep_ref[...].astype(F32) + other_ref[...].astype(F32)).astype(BF16)
    for left in range(0, d_in, 256):
        rows = slice(left, left + 256)
        part = jnp.concatenate([part[:, rows] for part in feats], axis=0)
        total = (cold_ref[rows, :] + transposed_dot(part, sums)).astype(BF16)
        first, second = total[:, :wide], total[:, wide:]

        @pl.when(own_core == 0)
        def _(rows=rows, first=first, second=second):
            own_ref[rows, :] = first
            send_ref[rows, :] = second

        @pl.when(own_core == 1)
        def _(rows=rows, first=first, second=second):
            own_ref[rows, :] = second
            send_ref[rows, :] = first

    pair_ref[...] = (two_ref[...].astype(F32) + fetched_ref[...].astype(F32)).astype(BF16)


def join(place, cold, keep, other, two, fetched_two, feats):
    d_in, d_h = cold.shape
    half = jax.ShapeDtypeStruct((d_in, d_h // 2), BF16)
    return pl.pallas_call(
        functools.partial(join_kernel, len(feats)),
        in_specs=[scalars()] + [whole()] * (5 + len(feats)),
        out_specs=[whole()] * 3,
        out_shape=[half, half, jax.ShapeDtypeStruct(two.shape, BF16)],
        compiler_params=params(32),
        cost_estimate=cost(2 * keep.shape[0] * d_h * d_in, 4 * d_in * d_h),
        name="join",
    )(place, cold, keep, other, two, fetched_two, *feats)


def share_rows(rows, members, place_ref, k, h):
    size = rows // (2 * members)
    share = (place_ref[0] ^ k) * 2 + (place_ref[2] ^ h)
    return pl.ds(pl.multiple_of(share * size, TILE), size)


def pair_kernel(members, place_ref, one_ref, other_ref, two_ref, *out_refs):
    for k, out_ref in enumerate(out_refs):
        base = 0
        for h in range(2):
            here = share_rows(one_ref.shape[0], members, place_ref, k, h)
            total = one_ref[here, :].astype(F32) + other_ref[here, :].astype(F32)
            out_ref[base : base + here.size, :] = total.astype(BF16)
            base += here.size
            here = share_rows(two_ref.shape[0], members, place_ref, k, h)
            out_ref[base : base + here.size, :] = two_ref[here, :]
            base += here.size


def pair_sums(place, one, other, two, members):
    wide = one.shape[1]
    rows = one.shape[0] + two.shape[0]
    share = jax.ShapeDtypeStruct((rows // members, wide), BF16)
    return pl.pallas_call(
        functools.partial(pair_kernel, members),
        in_specs=[scalars()] + [whole()] * 3,
        out_specs=[whole()] * members,
        out_shape=[share] * members,
        compiler_params=params(16),
        cost_estimate=cost(0, 6 * rows * wide),
        name="pair_sums",
    )(place, one, other, two)


def lay_kernel(members, place_ref, own_ref, other_ref, *out_refs):
    own_core = place_ref[1]
    wide = own_ref.shape[1]
    for ref, core in ((own_ref, own_core), (other_ref, 1 - own_core)):
        lanes = pl.ds(pl.multiple_of(core * wide, wide), wide)
        base = 0
        for k in range(members):
            for h in range(2):
                for out_ref in out_refs:
                    here = share_rows(out_ref.shape[0], members, place_ref, k, h)
                    out_ref[here, lanes] = ref[base : base + here.size, :].astype(F32)
                    base += here.size


def lay(place, own, other, members, rows_of):
    wide = own.shape[1]
    return pl.pallas_call(
        functools.partial(lay_kernel, members),
        in_specs=[scalars(), whole(), whole()],
        out_specs=[whole()] * len(rows_of),
        out_shape=[jax.ShapeDtypeStruct((rows, 2 * wide), F32) for rows in rows_of],
        compiler_params=params(16),
        cost_estimate=cost(0, 12 * own.shape[0] * wide),
        name="lay",
    )(place, own, other)


def exchange(array, axis, step):
    size = lax.axis_size(axis)
    return lax.ppermute(array, axis, [(source, source ^ step) for source in range(size)])


def added(*arrays):
    total = arrays[0].astype(F32)
    for array in arrays[1:]:
        total = total + array.astype(F32)
    return total.astype(BF16)


def sum_over_slice(shares):
    n_clique, n_copy = lax.axis_size("clique"), lax.axis_size("copy")
    got = [shares[0]] + [exchange(shares[k], "clique", k) for k in range(1, n_clique)]
    half = shares[0].shape[0] // 2
    z_steps = [2 << bit for bit in range((n_copy // 2).bit_length() - 1)]
    keep = added(*[array[:half] for array in got])
    send = added(*[array[half:] for array in got])
    keep = added(keep, exchange(send, "copy", z_steps[0]))
    for step in z_steps[1:]:
        keep = added(keep, exchange(keep, "copy", step))
    share = jnp.concatenate([keep, exchange(keep, "copy", z_steps[0])], axis=0)
    return jnp.concatenate(
        [share] + [exchange(share, "clique", k) for k in range(1, n_clique)], axis=0
    )


def gather_feats(own):
    members = lax.axis_size("clique")
    if members != 4:
        return [own] + [exchange(own, "clique", k) for k in range(1, members)]
    one, two = exchange(own, "clique", 1), exchange(own, "clique", 2)
    middle = own.shape[0] // 2
    top = exchange(two[:middle], "clique", 1)
    bottom = exchange(one[middle:], "clique", 2)
    return [own, one, two, top, bottom]


def on_device(
    out_grad, pre_act, batch_count, layer_two, hot_slots, cold_index, hot_feats, cold_feats
):
    n_clique = lax.axis_size("clique")
    shard_rows, d_in = hot_feats.shape
    d_h = pre_act.shape[1]
    cold_rows = cold_feats.shape[0]
    fanout = hot_slots.shape[1] + cold_index.shape[1]
    copy_at = lax.axis_index("copy")
    place = jnp.stack([lax.axis_index("clique"), copy_at & 1, (copy_at >> 1) & 1]).astype(jnp.int32)

    half_feats = lax.dynamic_slice_in_dim(
        hot_feats, (copy_at & 1) * (shard_rows // 2), shard_rows // 2, 0
    )
    feats = gather_feats(half_feats)

    row_grad, own_two, twin_two, words = row_gradients(
        place, batch_count, out_grad, pre_act, layer_two, hot_slots.T, shard_rows * n_clique, shard_rows
    )
    fetched_two = exchange(twin_two, "copy", 1)
    send, keep, words = hot_sums(words, row_grad, cold_index.T, feats[1:3], cold_rows, fanout)
    other = exchange(send, "copy", 1)
    cold = cold_grad(words, row_grad, cold_feats, fanout)
    own_one, twin_one, two = join(place, cold, keep, other, own_two, fetched_two, feats)
    shares = pair_sums(place, own_one, exchange(twin_one, "copy", 1), two, n_clique)
    total = sum_over_slice(shares)
    return tuple(lay(place, total, exchange(total, "copy", 1), n_clique, (d_in, d_h)))


def solution(mesh):
    placed = (
        P(("clique", "copy"), None),
        P(("clique", "copy"), None),
        P(("clique", "copy")),
        P(),
        P(("clique", "copy"), None),
        P(("clique", "copy"), None),
        P("clique", None),
        P(("clique", "copy"), None),
    )
    return jax.shard_map(
        on_device, mesh=mesh, in_specs=placed, out_specs=(P(), P()), check_vma=False
    )
```

```python
import functools

import jax
import jax.numpy as jnp
from jax import lax
from jax.experimental import pallas as pl
from jax.experimental.pallas import tpu as pltpu
from jax.sharding import PartitionSpec as P

F32 = jnp.float32
BF16 = jnp.bfloat16
I16 = jnp.int16
FIELDS = 4
TILE = 16


def whole():
    return pl.BlockSpec(memory_space=pltpu.VMEM)


def scalars():
    return pl.BlockSpec(memory_space=pltpu.SMEM)


def in_place():
    return pl.BlockSpec(memory_space=pl.ANY)


def params(mebibytes):
    return pltpu.CompilerParams(vmem_limit_bytes=mebibytes << 20)


def cost(flops, moved):
    return pl.CostEstimate(flops=int(flops), bytes_accessed=int(moved), transcendentals=0)


def transposed_dot(left, right):
    return lax.dot_general(left, right, (((0,), (0,)), ((), ())), preferred_element_type=F32)


def halves(total_ref, own_ref, send_ref, own_core):
    wide = own_ref.shape[1]
    mine = pl.ds(pl.multiple_of(own_core * wide, wide), wide)
    twin = pl.ds(pl.multiple_of((1 - own_core) * wide, wide), wide)
    own_ref[...] = total_ref[:, mine].astype(BF16)
    send_ref[...] = total_ref[:, twin].astype(BF16)


def build_words(index, q_rows, store):
    terms = index.shape[0]
    shift = q_rows.bit_length() - 1
    low = index & (q_rows - 1)
    one = jnp.left_shift(jnp.ones_like(index), (index >> shift) * 4)
    unit = one
    for other in range(1, terms):
        turned_low = jnp.concatenate([low[other:], low[:other]], axis=0)
        turned = jnp.concatenate([one[other:], one[:other]], axis=0)
        unit = unit + jnp.where(turned_low == low, turned, jnp.zeros_like(turned))
    tall = min(256, q_rows) // TILE
    shape = (tall, TILE, 128)
    place = lax.broadcasted_iota(jnp.int32, shape, 0) * TILE + lax.broadcasted_iota(jnp.int32, shape, 1)
    place = place.astype(I16)

    def tile(row):
        return jnp.broadcast_to(row, (TILE, 128)).astype(I16)[None]

    lows = [tile(low[k : k + 1, :]) for k in range(terms)]
    units = [tile(unit[k : k + 1, :]) for k in range(terms)]
    for top in range(0, q_rows // TILE, tall):
        word = jnp.zeros(shape, I16)
        for k in range(terms):
            word = jnp.where(place == lows[k] - I16(top * TILE), units[k], word)
        store(top, tall, word)


def unpack(word_ref, field, count_ref):
    counts = (word_ref[...] >> (field * 4)) & 15
    count_ref[...] = counts.astype(BF16).reshape(count_ref.shape)


def rows_kernel(
    shard_bits, half_rows, chunks,
    place_ref, count_ref, index_ref, out_grad_hbm, pre_act_hbm, layer_two_hbm,
    row_grad_ref, own_ref, send_ref, word_ref,
    out_grad_ref, pre_act_ref, layer_two_ref, sum_ref, sems,
):
    rows = out_grad_ref.shape[0] // chunks
    blocks = [slice(chunk * rows, (chunk + 1) * rows) for chunk in range(chunks)]
    fetch_layer = pltpu.make_async_copy(layer_two_hbm, layer_two_ref, sems.at[2 * chunks])
    fetches = []
    for chunk, block in enumerate(blocks):
        pair = []
        for at, (source, target) in enumerate(((out_grad_hbm, out_grad_ref), (pre_act_hbm, pre_act_ref))):
            fetch = pltpu.make_async_copy(
                source.at[block, :], target.at[block, :], sems.at[2 * chunk + at]
            )
            fetch.start()
            pair.append(fetch)
        fetches.append(pair)
        if chunk == 0:
            fetch_layer.start()

    own_shard, own_core = place_ref[0], place_ref[1]
    part_bits = shard_bits - 1

    def build(tile):
        lanes = slice(tile * 128, (tile + 1) * 128)
        index = index_ref[:, lanes]
        row = index & ((1 << part_bits) - 1)
        half = ((index >> part_bits) & 1) ^ own_core ^ 1
        index = half * half_rows + (((index >> shard_bits) ^ own_shard) << part_bits) + row

        def store(top, tall, words):
            word_ref[top : top + tall, :, lanes] = words

        build_words(index, word_ref.shape[0] * TILE, store)

    tiles = row_grad_ref.shape[0] // 128
    first = tiles // 4
    for tile in range(first):
        build(tile)
    ends = [first + (tiles - first) * chunk // chunks for chunk in range(chunks + 1)]
    for chunk, block in enumerate(blocks):
        for fetch in fetches[chunk]:
            fetch.wait()
        if chunk == 0:
            fetch_layer.wait()
        live = count_ref[0] - chunk * rows

        @pl.when(live < rows)
        def _(block=block, live=live):
            out_grad = out_grad_ref[block, :].astype(F32)
            place = lax.broadcasted_iota(jnp.int32, out_grad.shape, 0)
            masked = jnp.where(place < live, out_grad, jnp.zeros_like(out_grad))
            out_grad_ref[block, :] = masked.astype(BF16)

        masked = out_grad_ref[block, :]
        pre_act = pre_act_ref[block, :]
        back = lax.dot_general(
            masked, layer_two_ref[...], (((1,), (1,)), ((), ())), preferred_element_type=F32
        )
        activ = jnp.maximum(pre_act, jnp.zeros_like(pre_act))
        part = transposed_dot(activ, masked)
        sum_ref[...] = part if chunk == 0 else sum_ref[...] + part
        for tile in range(ends[chunk], ends[chunk + 1]):
            build(tile)
        row_grad_ref[block, :] = jnp.where(
            pre_act.astype(F32) > 0, back, jnp.zeros_like(back)
        ).astype(BF16)
    halves(sum_ref, own_ref, send_ref, own_core)


def row_gradients(place, batch_count, out_grad, pre_act, layer_two, index, hot_total, shard_rows):
    rows, d_out = out_grad.shape
    d_h = pre_act.shape[1]
    chunks = 4
    deep = hot_total // FIELDS // TILE
    half = jax.ShapeDtypeStruct((d_h, d_out // 2), BF16)
    return pl.pallas_call(
        functools.partial(rows_kernel, shard_rows.bit_length() - 1, hot_total // 2, chunks),
        in_specs=[scalars(), scalars(), whole()] + [pl.BlockSpec(memory_space=pltpu.HBM)] * 3,
        out_specs=[whole()] * 4,
        out_shape=[
            jax.ShapeDtypeStruct((rows, d_h), BF16),
            half,
            half,
            jax.ShapeDtypeStruct((deep, TILE, rows), I16),
        ],
        scratch_shapes=[
            pltpu.VMEM((rows, d_out), BF16),
            pltpu.VMEM((rows, d_h), BF16),
            pltpu.VMEM((d_h, d_out), BF16),
            pltpu.VMEM((d_h, d_out), F32),
            pltpu.SemaphoreType.DMA((2 * chunks + 1,)),
        ],
        compiler_params=params(48),
        cost_estimate=cost(0, 0),
        name="row_gradients",
    )(place, batch_count, index, out_grad, pre_act, layer_two)


def hot_kernel(scale, arrived, word_ref, row_grad_ref, index_ref, *rest):
    send_ref, keep_ref, cold_word_ref, *counts = rest[arrived:]
    tall, rows = counts[0].shape
    tiles = rows // 128 // FIELDS
    unpack(word_ref, 0, counts[0])
    for field in range(FIELDS):
        found = jnp.dot(counts[field % 2][...], row_grad_ref[...], preferred_element_type=F32)
        if field + 1 < FIELDS:
            unpack(word_ref, field + 1, counts[(field + 1) % 2])
        for tile in range(field * tiles, (field + 1) * tiles):
            lanes = slice(tile * 128, (tile + 1) * 128)

            def store(top, deep, words, lanes=lanes):
                cold_word_ref[top : top + deep, :, lanes] = words

            build_words(index_ref[:, lanes], cold_word_ref.shape[0] * TILE, store)
        out_ref = (send_ref, keep_ref)[field // 2]
        out_ref[field % 2 * tall : (field % 2 + 1) * tall, :] = (found * scale).astype(BF16)


def hot_sums(words, row_grad, cold_index, arrived, cold_rows, fanout):
    rows, d_h = row_grad.shape
    q_rows = words.shape[0] * TILE
    half = jax.ShapeDtypeStruct((q_rows * FIELDS // 2, d_h), BF16)
    return pl.pallas_call(
        functools.partial(hot_kernel, 1.0 / fanout, len(arrived)),
        in_specs=[whole(), whole(), whole()] + [in_place()] * len(arrived),
        out_specs=[whole()] * 3,
        out_shape=[
            half,
            half,
            jax.ShapeDtypeStruct((cold_rows // FIELDS // TILE, TILE, rows), I16),
        ],
        scratch_shapes=[pltpu.VMEM((q_rows, rows), BF16)] * 2,
        compiler_params=params(40),
        cost_estimate=cost(0, 0),
        name="hot_sums",
    )(words, row_grad, cold_index, *arrived)


def cold_kernel(scale, word_ref, row_grad_ref, feats_ref, grad_ref, sums_ref, held_ref, sem, *counts):
    fetch = pltpu.make_async_copy(feats_ref, held_ref, sem)
    fetch.start()
    tall = counts[0].shape[0]

    def add_product(field):
        rows = slice(field * tall, (field + 1) * tall)
        part = transposed_dot(held_ref[rows, :], sums_ref[rows, :])
        grad_ref[...] = part if field == 0 else grad_ref[...] + part

    unpack(word_ref, 0, counts[0])
    for field in range(FIELDS):
        found = jnp.dot(counts[field % 2][...], row_grad_ref[...], preferred_element_type=F32)
        if field + 1 < FIELDS:
            unpack(word_ref, field + 1, counts[(field + 1) % 2])
        if field == 1:
            fetch.wait()
        if field > 0:
            add_product(field - 1)
        sums_ref[field * tall : (field + 1) * tall, :] = (found * scale).astype(BF16)
    add_product(FIELDS - 1)


def cold_grad(words, row_grad, feats, fanout):
    rows, d_h = row_grad.shape
    cold_rows, d_in = feats.shape
    q_rows = cold_rows // FIELDS
    return pl.pallas_call(
        functools.partial(cold_kernel, 1.0 / fanout),
        in_specs=[whole(), whole(), in_place()],
        out_specs=whole(),
        out_shape=jax.ShapeDtypeStruct((d_in, d_h), F32),
        scratch_shapes=[
            pltpu.VMEM((cold_rows, d_h), BF16),
            pltpu.VMEM((cold_rows, d_in), BF16),
            pltpu.SemaphoreType.DMA,
            pltpu.VMEM((q_rows, rows), BF16),
            pltpu.VMEM((q_rows, rows), BF16),
        ],
        compiler_params=params(40),
        cost_estimate=cost(0, 0),
        name="cold_grad",
    )(words, row_grad, feats)


def join_kernel(parts, place_ref, cold_ref, keep_ref, other_ref, two_ref, fetched_ref, *rest):
    feats, (own_ref, send_ref, pair_ref) = rest[:parts], rest[parts:]
    own_core = place_ref[1]
    d_in, d_h = cold_ref.shape
    wide = d_h // 2
    sums = (keep_ref[...].astype(F32) + other_ref[...].astype(F32)).astype(BF16)
    for left in range(0, d_in, 256):
        rows = slice(left, left + 256)
        part = jnp.concatenate([part[:, rows] for part in feats], axis=0)
        total = (cold_ref[rows, :] + transposed_dot(part, sums)).astype(BF16)
        first, second = total[:, :wide], total[:, wide:]

        @pl.when(own_core == 0)
        def _(rows=rows, first=first, second=second):
            own_ref[rows, :] = first
            send_ref[rows, :] = second

        @pl.when(own_core == 1)
        def _(rows=rows, first=first, second=second):
            own_ref[rows, :] = second
            send_ref[rows, :] = first

    pair_ref[...] = (two_ref[...].astype(F32) + fetched_ref[...].astype(F32)).astype(BF16)


def join(place, cold, keep, other, two, fetched_two, feats):
    d_in, d_h = cold.shape
    half = jax.ShapeDtypeStruct((d_in, d_h // 2), BF16)
    return pl.pallas_call(
        functools.partial(join_kernel, len(feats)),
        in_specs=[scalars()] + [whole()] * (5 + len(feats)),
        out_specs=[whole()] * 3,
        out_shape=[half, half, jax.ShapeDtypeStruct(two.shape, BF16)],
        compiler_params=params(32),
        cost_estimate=cost(2 * keep.shape[0] * d_h * d_in, 4 * d_in * d_h),
        name="join",
    )(place, cold, keep, other, two, fetched_two, *feats)


def share_rows(rows, members, place_ref, k, h):
    size = rows // (2 * members)
    share = (place_ref[0] ^ k) * 2 + (place_ref[2] ^ h)
    return pl.ds(pl.multiple_of(share * size, TILE), size)


def pair_kernel(members, place_ref, one_ref, other_ref, two_ref, *out_refs):
    for at, out_ref in enumerate(out_refs):
        here = share_rows(one_ref.shape[0], members, place_ref, at // 2, at % 2)
        total = one_ref[here, :].astype(F32) + other_ref[here, :].astype(F32)
        out_ref[: here.size, :] = total.astype(BF16)
        base = here.size
        here = share_rows(two_ref.shape[0], members, place_ref, at // 2, at % 2)
        out_ref[base : base + here.size, :] = two_ref[here, :]


def pair_sums(place, one, other, two, members):
    wide = one.shape[1]
    rows = one.shape[0] + two.shape[0]
    share = jax.ShapeDtypeStruct((rows // (2 * members), wide), BF16)
    return pl.pallas_call(
        functools.partial(pair_kernel, members),
        in_specs=[scalars()] + [whole()] * 3,
        out_specs=[whole()] * (2 * members),
        out_shape=[share] * (2 * members),
        compiler_params=params(16),
        cost_estimate=cost(0, 6 * rows * wide),
        name="pair_sums",
    )(place, one, other, two)


def lay_kernel(members, parts, place_ref, *refs):
    owns, others, out_refs = refs[:parts], refs[parts : 2 * parts], refs[2 * parts :]
    own_core = place_ref[1]
    wide = owns[0].shape[1]
    each = 2 * members // parts
    for ref_list, core in ((owns, own_core), (others, 1 - own_core)):
        lanes = pl.ds(pl.multiple_of(core * wide, wide), wide)
        for part, ref in enumerate(ref_list):
            base = 0
            for at in range(part * each, (part + 1) * each):
                for out_ref in out_refs:
                    here = share_rows(out_ref.shape[0], members, place_ref, at // 2, at % 2)
                    out_ref[here, lanes] = ref[base : base + here.size, :].astype(F32)
                    base += here.size


def lay(place, owns, others, members, rows_of):
    wide = owns[0].shape[1]
    return pl.pallas_call(
        functools.partial(lay_kernel, members, len(owns)),
        in_specs=[scalars()] + [whole()] * (2 * len(owns)),
        out_specs=[whole()] * len(rows_of),
        out_shape=[jax.ShapeDtypeStruct((rows, 2 * wide), F32) for rows in rows_of],
        compiler_params=params(16),
        cost_estimate=cost(0, 12 * sum(rows_of) * wide),
        name="lay",
    )(place, *owns, *others)


def exchange(array, axis, step):
    size = lax.axis_size(axis)
    return lax.ppermute(array, axis, [(source, source ^ step) for source in range(size)])


def added(*arrays):
    total = arrays[0].astype(F32)
    for array in arrays[1:]:
        total = total + array.astype(F32)
    return total.astype(BF16)


def trade(arrays):
    n_clique, n_copy = lax.axis_size("clique"), lax.axis_size("copy")
    got = [arrays[0]]
    for at in range(1, 2 * n_clique):
        route = [
            (i * n_copy + j, (i ^ (at // 2)) * n_copy + (j ^ (2 * (at % 2))))
            for i in range(n_clique)
            for j in range(n_copy)
        ]
        got.append(lax.ppermute(arrays[at], ("clique", "copy"), route))
    return got


def sum_over_slice(shares):
    keep = added(*trade(shares))
    n_deep = lax.axis_size("copy") // 2
    for bit in range(1, n_deep.bit_length() - 1):
        keep = added(keep, exchange(keep, "copy", 2 << bit))
    return trade([keep] * len(shares))


def gather_feats(own):
    members = lax.axis_size("clique")
    if members != 4:
        return [own] + [exchange(own, "clique", k) for k in range(1, members)]
    one, two = exchange(own, "clique", 1), exchange(own, "clique", 2)
    middle = own.shape[0] // 2
    top = exchange(two[:middle], "clique", 1)
    bottom = exchange(one[middle:], "clique", 2)
    return [own, one, two, top, bottom]


def on_device(
    out_grad, pre_act, batch_count, layer_two, hot_slots, cold_index, hot_feats, cold_feats
):
    n_clique = lax.axis_size("clique")
    shard_rows, d_in = hot_feats.shape
    d_h = pre_act.shape[1]
    cold_rows = cold_feats.shape[0]
    fanout = hot_slots.shape[1] + cold_index.shape[1]
    copy_at = lax.axis_index("copy")
    place = jnp.stack([lax.axis_index("clique"), copy_at & 1, (copy_at >> 1) & 1]).astype(jnp.int32)

    half_feats = lax.dynamic_slice_in_dim(
        hot_feats, (copy_at & 1) * (shard_rows // 2), shard_rows // 2, 0
    )
    feats = gather_feats(half_feats)

    row_grad, own_two, twin_two, words = row_gradients(
        place, batch_count, out_grad, pre_act, layer_two, hot_slots.T, shard_rows * n_clique, shard_rows
    )
    fetched_two = exchange(twin_two, "copy", 1)
    send, keep, words = hot_sums(words, row_grad, cold_index.T, feats[1:3], cold_rows, fanout)
    other = exchange(send, "copy", 1)
    cold = cold_grad(words, row_grad, cold_feats, fanout)
    own_one, twin_one, two = join(place, cold, keep, other, own_two, fetched_two, feats)
    shares = pair_sums(place, own_one, exchange(twin_one, "copy", 1), two, n_clique)
    shares = sum_over_slice(shares)
    parts = [jnp.concatenate(shares[at : at + n_clique], axis=0) for at in (0, n_clique)]
    others = [exchange(part, "copy", 1) for part in parts]
    return tuple(lay(place, parts, others, n_clique, (d_in, d_h)))


def solution(mesh):
    placed = (
        P(("clique", "copy"), None),
        P(("clique", "copy"), None),
        P(("clique", "copy")),
        P(),
        P(("clique", "copy"), None),
        P(("clique", "copy"), None),
        P("clique", None),
        P(("clique", "copy"), None),
    )
    return jax.shard_map(
        on_device, mesh=mesh, in_specs=placed, out_specs=(P(), P()), check_vma=False
    )
```

```python
import functools

import jax
import jax.numpy as jnp
from jax import lax
from jax.experimental import pallas as pl
from jax.experimental.pallas import tpu as pltpu
from jax.sharding import PartitionSpec as P

F32 = jnp.float32
BF16 = jnp.bfloat16
I16 = jnp.int16
FIELDS = 4
TILE = 16


def whole():
    return pl.BlockSpec(memory_space=pltpu.VMEM)


def scalars():
    return pl.BlockSpec(memory_space=pltpu.SMEM)


def in_place():
    return pl.BlockSpec(memory_space=pl.ANY)


def params(mebibytes):
    return pltpu.CompilerParams(vmem_limit_bytes=mebibytes << 20)


def cost(flops, moved):
    return pl.CostEstimate(flops=int(flops), bytes_accessed=int(moved), transcendentals=0)


def transposed_dot(left, right):
    return lax.dot_general(left, right, (((0,), (0,)), ((), ())), preferred_element_type=F32)


def halves(total_ref, own_ref, send_ref, own_core):
    wide = own_ref.shape[1]
    mine = pl.ds(pl.multiple_of(own_core * wide, wide), wide)
    twin = pl.ds(pl.multiple_of((1 - own_core) * wide, wide), wide)
    own_ref[...] = total_ref[:, mine].astype(BF16)
    send_ref[...] = total_ref[:, twin].astype(BF16)


def build_words(index, q_rows, store):
    terms = index.shape[0]
    shift = q_rows.bit_length() - 1
    low = index & (q_rows - 1)
    one = jnp.left_shift(jnp.ones_like(index), (index >> shift) * 4)
    unit = one
    for other in range(1, terms):
        turned_low = jnp.concatenate([low[other:], low[:other]], axis=0)
        turned = jnp.concatenate([one[other:], one[:other]], axis=0)
        unit = unit + jnp.where(turned_low == low, turned, jnp.zeros_like(turned))
    tall = min(256, q_rows) // TILE
    shape = (tall, TILE, 128)
    place = lax.broadcasted_iota(jnp.int32, shape, 0) * TILE + lax.broadcasted_iota(jnp.int32, shape, 1)
    place = place.astype(I16)

    def tile(row):
        return jnp.broadcast_to(row, (TILE, 128)).astype(I16)[None]

    lows = [tile(low[k : k + 1, :]) for k in range(terms)]
    units = [tile(unit[k : k + 1, :]) for k in range(terms)]
    for top in range(0, q_rows // TILE, tall):
        word = jnp.zeros(shape, I16)
        for k in range(terms):
            word = jnp.where(place == lows[k] - I16(top * TILE), units[k], word)
        store(top, tall, word)


def unpack(word_ref, field, count_ref):
    if field < FIELDS - 1:
        counts = word_ref[...] & (15 << (4 * field))
    else:
        counts = (word_ref[...] >> (4 * field)) & 15
    count_ref[...] = counts.astype(BF16).reshape(count_ref.shape)


def unpacked_scale(field):
    return 16.0**field if field < FIELDS - 1 else 1.0


def rows_kernel(
    shard_bits, half_rows, chunks,
    place_ref, count_ref, index_ref, out_grad_hbm, pre_act_hbm, layer_two_hbm,
    row_grad_ref, own_ref, send_ref, word_ref,
    out_grad_ref, pre_act_ref, layer_two_ref, sum_ref, sems,
):
    rows = out_grad_ref.shape[0] // chunks
    blocks = [slice(chunk * rows, (chunk + 1) * rows) for chunk in range(chunks)]
    fetch_layer = pltpu.make_async_copy(layer_two_hbm, layer_two_ref, sems.at[2 * chunks])
    fetches = []
    for chunk, block in enumerate(blocks):
        pair = []
        for at, (source, target) in enumerate(((out_grad_hbm, out_grad_ref), (pre_act_hbm, pre_act_ref))):
            fetch = pltpu.make_async_copy(
                source.at[block, :], target.at[block, :], sems.at[2 * chunk + at]
            )
            fetch.start()
            pair.append(fetch)
        fetches.append(pair)
        if chunk == 0:
            fetch_layer.start()

    own_shard, own_core = place_ref[0], place_ref[1]
    part_bits = shard_bits - 1

    def build(tile):
        lanes = slice(tile * 128, (tile + 1) * 128)
        index = index_ref[:, lanes]
        row = index & ((1 << part_bits) - 1)
        half = ((index >> part_bits) & 1) ^ own_core ^ 1
        index = half * half_rows + (((index >> shard_bits) ^ own_shard) << part_bits) + row

        def store(top, tall, words):
            word_ref[top : top + tall, :, lanes] = words

        build_words(index, word_ref.shape[0] * TILE, store)

    tiles = row_grad_ref.shape[0] // 128
    first = tiles // 4
    for tile in range(first):
        build(tile)
    ends = [first + (tiles - first) * chunk // chunks for chunk in range(chunks + 1)]
    for chunk, block in enumerate(blocks):
        for fetch in fetches[chunk]:
            fetch.wait()
        if chunk == 0:
            fetch_layer.wait()
        live = count_ref[0] - chunk * rows

        @pl.when(live < rows)
        def _(block=block, live=live):
            out_grad = out_grad_ref[block, :].astype(F32)
            place = lax.broadcasted_iota(jnp.int32, out_grad.shape, 0)
            masked = jnp.where(place < live, out_grad, jnp.zeros_like(out_grad))
            out_grad_ref[block, :] = masked.astype(BF16)

        masked = out_grad_ref[block, :]
        pre_act = pre_act_ref[block, :]
        back = lax.dot_general(
            masked, layer_two_ref[...], (((1,), (1,)), ((), ())), preferred_element_type=F32
        )
        activ = jnp.maximum(pre_act, jnp.zeros_like(pre_act))
        part = transposed_dot(activ, masked)
        sum_ref[...] = part if chunk == 0 else sum_ref[...] + part
        for tile in range(ends[chunk], ends[chunk + 1]):
            build(tile)
        row_grad_ref[block, :] = jnp.where(
            pre_act.astype(F32) > 0, back, jnp.zeros_like(back)
        ).astype(BF16)
    halves(sum_ref, own_ref, send_ref, own_core)


def row_gradients(place, batch_count, out_grad, pre_act, layer_two, index, hot_total, shard_rows):
    rows, d_out = out_grad.shape
    d_h = pre_act.shape[1]
    chunks = 4
    deep = hot_total // FIELDS // TILE
    half = jax.ShapeDtypeStruct((d_h, d_out // 2), BF16)
    return pl.pallas_call(
        functools.partial(rows_kernel, shard_rows.bit_length() - 1, hot_total // 2, chunks),
        in_specs=[scalars(), scalars(), whole()] + [pl.BlockSpec(memory_space=pltpu.HBM)] * 3,
        out_specs=[whole()] * 4,
        out_shape=[
            jax.ShapeDtypeStruct((rows, d_h), BF16),
            half,
            half,
            jax.ShapeDtypeStruct((deep, TILE, rows), I16),
        ],
        scratch_shapes=[
            pltpu.VMEM((rows, d_out), BF16),
            pltpu.VMEM((rows, d_h), BF16),
            pltpu.VMEM((d_h, d_out), BF16),
            pltpu.VMEM((d_h, d_out), F32),
            pltpu.SemaphoreType.DMA((2 * chunks + 1,)),
        ],
        compiler_params=params(48),
        cost_estimate=cost(10**10, 10**8),
        name="row_gradients",
    )(place, batch_count, index, out_grad, pre_act, layer_two)


def hot_kernel(
    scale, word_ref, row_grad_ref, index_ref, send_ref, keep_ref, cold_word_ref, *counts
):
    tall, rows = counts[0].shape
    tiles = rows // 128 // FIELDS
    unpack(word_ref, 0, counts[0])
    for field in range(FIELDS):
        found = jnp.dot(counts[field % 2][...], row_grad_ref[...], preferred_element_type=F32)
        if field + 1 < FIELDS:
            unpack(word_ref, field + 1, counts[(field + 1) % 2])
        for tile in range(field * tiles, (field + 1) * tiles):
            lanes = slice(tile * 128, (tile + 1) * 128)

            def store(top, deep, words, lanes=lanes):
                cold_word_ref[top : top + deep, :, lanes] = words

            build_words(index_ref[:, lanes], cold_word_ref.shape[0] * TILE, store)
        out_ref = (send_ref, keep_ref)[field // 2]
        out_ref[field % 2 * tall : (field % 2 + 1) * tall, :] = (found * (scale / unpacked_scale(field))).astype(BF16)


def hot_sums(words, row_grad, cold_index, cold_rows, fanout):
    rows, d_h = row_grad.shape
    q_rows = words.shape[0] * TILE
    half = jax.ShapeDtypeStruct((q_rows * FIELDS // 2, d_h), BF16)
    return pl.pallas_call(
        functools.partial(hot_kernel, 1.0 / fanout),
        in_specs=[whole(), whole(), whole()],
        out_specs=[whole()] * 3,
        out_shape=[
            half,
            half,
            jax.ShapeDtypeStruct((cold_rows // FIELDS // TILE, TILE, rows), I16),
        ],
        scratch_shapes=[pltpu.VMEM((q_rows, rows), BF16)] * 2,
        compiler_params=params(40),
        cost_estimate=cost(10**10, 10**8),
        name="hot_sums",
    )(words, row_grad, cold_index)


def cold_kernel(scale, word_ref, row_grad_ref, feats_ref, grad_ref, sums_ref, held_ref, sem, *counts):
    fetch = pltpu.make_async_copy(feats_ref, held_ref, sem)
    fetch.start()
    tall = counts[0].shape[0]

    def add_product(field):
        rows = slice(field * tall, (field + 1) * tall)
        part = transposed_dot(held_ref[rows, :], sums_ref[rows, :])
        grad_ref[...] = part if field == 0 else grad_ref[...] + part

    unpack(word_ref, 0, counts[0])
    for field in range(FIELDS):
        found = jnp.dot(counts[field % 2][...], row_grad_ref[...], preferred_element_type=F32)
        if field + 1 < FIELDS:
            unpack(word_ref, field + 1, counts[(field + 1) % 2])
        if field == 1:
            fetch.wait()
        if field > 0:
            add_product(field - 1)
        sums_ref[field * tall : (field + 1) * tall, :] = (found * (scale / unpacked_scale(field))).astype(BF16)
    add_product(FIELDS - 1)


def cold_grad(words, row_grad, feats, fanout):
    rows, d_h = row_grad.shape
    cold_rows, d_in = feats.shape
    q_rows = cold_rows // FIELDS
    return pl.pallas_call(
        functools.partial(cold_kernel, 1.0 / fanout),
        in_specs=[whole(), whole(), in_place()],
        out_specs=whole(),
        out_shape=jax.ShapeDtypeStruct((d_in, d_h), F32),
        scratch_shapes=[
            pltpu.VMEM((cold_rows, d_h), BF16),
            pltpu.VMEM((cold_rows, d_in), BF16),
            pltpu.SemaphoreType.DMA,
            pltpu.VMEM((q_rows, rows), BF16),
            pltpu.VMEM((q_rows, rows), BF16),
        ],
        compiler_params=params(40),
        cost_estimate=cost(10**10, 10**8),
        name="cold_grad",
    )(words, row_grad, feats)


def join_kernel(parts, place_ref, cold_ref, keep_ref, other_ref, two_ref, fetched_ref, *rest):
    feats, (own_ref, send_ref, pair_ref) = rest[:parts], rest[parts:]
    own_core = place_ref[1]
    d_in, d_h = cold_ref.shape
    wide = d_h // 2
    sums = (keep_ref[...].astype(F32) + other_ref[...].astype(F32)).astype(BF16)
    for left in range(0, d_in, 256):
        rows = slice(left, left + 256)
        part = jnp.concatenate([part[:, rows] for part in feats], axis=0)
        total = (cold_ref[rows, :] + transposed_dot(part, sums)).astype(BF16)
        first, second = total[:, :wide], total[:, wide:]

        @pl.when(own_core == 0)
        def _(rows=rows, first=first, second=second):
            own_ref[rows, :] = first
            send_ref[rows, :] = second

        @pl.when(own_core == 1)
        def _(rows=rows, first=first, second=second):
            own_ref[rows, :] = second
            send_ref[rows, :] = first

    pair_ref[...] = (two_ref[...].astype(F32) + fetched_ref[...].astype(F32)).astype(BF16)


def join(place, cold, keep, other, two, fetched_two, feats):
    d_in, d_h = cold.shape
    half = jax.ShapeDtypeStruct((d_in, d_h // 2), BF16)
    return pl.pallas_call(
        functools.partial(join_kernel, len(feats)),
        in_specs=[scalars()] + [whole()] * (5 + len(feats)),
        out_specs=[whole()] * 3,
        out_shape=[half, half, jax.ShapeDtypeStruct(two.shape, BF16)],
        compiler_params=params(32),
        cost_estimate=cost(2 * keep.shape[0] * d_h * d_in, 4 * d_in * d_h),
        name="join",
    )(place, cold, keep, other, two, fetched_two, *feats)


def share_rows(rows, members, deep, place_ref, k, h):
    size = rows // (members * deep)
    share = (place_ref[0] ^ k) * deep + (place_ref[2] ^ h)
    return pl.ds(pl.multiple_of(share * size, TILE), size)


def pair_kernel(deep, place_ref, one_ref, other_ref, two_ref, *out_refs):
    members = len(out_refs)
    for k, out_ref in enumerate(out_refs):
        base = 0
        for h in range(deep):
            here = share_rows(one_ref.shape[0], members, deep, place_ref, k, h)
            total = one_ref[here, :].astype(F32) + other_ref[here, :].astype(F32)
            out_ref[base : base + here.size, :] = total.astype(BF16)
            base += here.size
            here = share_rows(two_ref.shape[0], members, deep, place_ref, k, h)
            out_ref[base : base + here.size, :] = two_ref[here, :]
            base += here.size


def pair_sums(place, one, other, two, members, deep):
    wide = one.shape[1]
    rows = one.shape[0] + two.shape[0]
    share = jax.ShapeDtypeStruct((rows // members, wide), BF16)
    return pl.pallas_call(
        functools.partial(pair_kernel, deep),
        in_specs=[scalars()] + [whole()] * 3,
        out_specs=[whole()] * members,
        out_shape=[share] * members,
        compiler_params=params(16),
        cost_estimate=cost(0, 6 * rows * wide),
        name="pair_sums",
    )(place, one, other, two)


def lay_kernel(members, deep, parts, place_ref, *refs):
    owns, others, out_refs = refs[:parts], refs[parts : 2 * parts], refs[2 * parts :]
    own_core = place_ref[1]
    wide = owns[0].shape[1]
    each = members // parts
    for ref_list, core in ((owns, own_core), (others, 1 - own_core)):
        lanes = pl.ds(pl.multiple_of(core * wide, wide), wide)
        for part, ref in enumerate(ref_list):
            base = 0
            for k in range(part * each, (part + 1) * each):
                for h in range(deep):
                    for out_ref in out_refs:
                        here = share_rows(out_ref.shape[0], members, deep, place_ref, k, h)
                        out_ref[here, lanes] = ref[base : base + here.size, :].astype(F32)
                        base += here.size


def lay(place, owns, others, members, deep, rows_of):
    wide = owns[0].shape[1]
    return pl.pallas_call(
        functools.partial(lay_kernel, members, deep, len(owns)),
        in_specs=[scalars()] + [whole()] * (2 * len(owns)),
        out_specs=[whole()] * len(rows_of),
        out_shape=[jax.ShapeDtypeStruct((rows, 2 * wide), F32) for rows in rows_of],
        compiler_params=params(16),
        cost_estimate=cost(0, 12 * sum(rows_of) * wide),
        name="lay",
    )(place, *owns, *others)


def exchange(array, axis, step):
    size = lax.axis_size(axis)
    return lax.ppermute(array, axis, [(source, source ^ step) for source in range(size)])


def added(*arrays):
    total = arrays[0].astype(F32)
    for array in arrays[1:]:
        total = total + array.astype(F32)
    return total.astype(BF16)


def trade(arrays, axis, step):
    return [arrays[0]] + [exchange(arrays[k], axis, k * step) for k in range(1, len(arrays))]


def sum_over_slice(shares, deep):
    got = trade(shares, "clique", 1)
    size = shares[0].shape[0] // deep
    cuts = [added(*[array[h * size : (h + 1) * size] for array in got]) for h in range(deep)]
    own = added(*trade(cuts, "copy", 2))
    step = 2 * deep
    while step < lax.axis_size("copy"):
        own = added(own, exchange(own, "copy", step))
        step *= 2
    share = jnp.concatenate(trade([own] * deep, "copy", 2), axis=0)
    return trade([share] * len(shares), "clique", 1)


def gather_feats(own):
    members = lax.axis_size("clique")
    if members != 4:
        return trade([own] * members, "clique", 1)
    one, two = exchange(own, "clique", 1), exchange(own, "clique", 2)
    middle = own.shape[0] // 2
    top = exchange(two[:middle], "clique", 1)
    bottom = exchange(one[middle:], "clique", 2)
    return [own, one, two, top, bottom]


def on_device(
    out_grad, pre_act, batch_count, layer_two, hot_slots, cold_index, hot_feats, cold_feats
):
    n_clique = lax.axis_size("clique")
    shard_rows, d_in = hot_feats.shape
    d_h = pre_act.shape[1]
    cold_rows = cold_feats.shape[0]
    fanout = hot_slots.shape[1] + cold_index.shape[1]
    copy_at = lax.axis_index("copy")
    deep = 4
    while deep > lax.axis_size("copy") // 2 or any(
        size % (TILE * n_clique * deep) for size in (d_in, d_h)
    ):
        deep //= 2
    place = jnp.stack([lax.axis_index("clique"), copy_at & 1, (copy_at >> 1) & (deep - 1)])
    place = place.astype(jnp.int32)

    half_feats = lax.dynamic_slice_in_dim(
        hot_feats, (copy_at & 1) * (shard_rows // 2), shard_rows // 2, 0
    )
    feats = gather_feats(half_feats)

    row_grad, own_two, twin_two, words = row_gradients(
        place, batch_count, out_grad, pre_act, layer_two, hot_slots.T, shard_rows * n_clique, shard_rows
    )
    fetched_two = exchange(twin_two, "copy", 1)
    send, keep, words = hot_sums(words, row_grad, cold_index.T, cold_rows, fanout)
    other = exchange(send, "copy", 1)
    cold = cold_grad(words, row_grad, cold_feats, fanout)
    own_one, twin_one, two = join(place, cold, keep, other, own_two, fetched_two, feats)
    shares = pair_sums(place, own_one, exchange(twin_one, "copy", 1), two, n_clique, deep)
    shares = sum_over_slice(shares, deep)
    middle = n_clique // 2
    parts = [jnp.concatenate(part, axis=0) for part in (shares[:middle], shares[middle:])]
    others = [exchange(part, "copy", 1) for part in parts]
    return tuple(lay(place, parts, others, n_clique, deep, (d_in, d_h)))


def solution(mesh):
    placed = (
        P(("clique", "copy"), None),
        P(("clique", "copy"), None),
        P(("clique", "copy")),
        P(),
        P(("clique", "copy"), None),
        P(("clique", "copy"), None),
        P("clique", None),
        P(("clique", "copy"), None),
    )
    return jax.shard_map(
        on_device, mesh=mesh, in_specs=placed, out_specs=(P(), P()), check_vma=False
    )
```

```python
import functools

import jax
import jax.numpy as jnp
from jax import lax
from jax.experimental import pallas as pl
from jax.experimental.pallas import tpu as pltpu
from jax.sharding import PartitionSpec as P

F32 = jnp.float32
BF16 = jnp.bfloat16
I16 = jnp.int16
FIELDS = 4
TILE = 16


def whole():
    return pl.BlockSpec(memory_space=pltpu.VMEM)


def scalars():
    return pl.BlockSpec(memory_space=pltpu.SMEM)


def in_place():
    return pl.BlockSpec(memory_space=pl.ANY)


def params(mebibytes):
    return pltpu.CompilerParams(vmem_limit_bytes=mebibytes << 20)


def cost(flops, moved):
    return pl.CostEstimate(flops=int(flops), bytes_accessed=int(moved), transcendentals=0)


def transposed_dot(left, right):
    return lax.dot_general(left, right, (((0,), (0,)), ((), ())), preferred_element_type=F32)


def halves(total_ref, own_ref, send_ref, own_core):
    wide = own_ref.shape[1]
    mine = pl.ds(pl.multiple_of(own_core * wide, wide), wide)
    twin = pl.ds(pl.multiple_of((1 - own_core) * wide, wide), wide)
    own_ref[...] = total_ref[:, mine].astype(BF16)
    send_ref[...] = total_ref[:, twin].astype(BF16)


def build_words(index, q_rows, store):
    terms = index.shape[0]
    shift = q_rows.bit_length() - 1
    low = index & (q_rows - 1)
    one = jnp.left_shift(jnp.ones_like(index), (index >> shift) * 4)
    unit = one
    for other in range(1, terms):
        turned_low = jnp.concatenate([low[other:], low[:other]], axis=0)
        turned = jnp.concatenate([one[other:], one[:other]], axis=0)
        unit = unit + jnp.where(turned_low == low, turned, jnp.zeros_like(turned))
    tall = min(256, q_rows) // TILE
    shape = (tall, TILE, 128)
    place = lax.broadcasted_iota(jnp.int32, shape, 0) * TILE + lax.broadcasted_iota(jnp.int32, shape, 1)
    place = place.astype(I16)

    def tile(row):
        return jnp.broadcast_to(row, (TILE, 128)).astype(I16)[None]

    lows = [tile(low[k : k + 1, :]) for k in range(terms)]
    units = [tile(unit[k : k + 1, :]) for k in range(terms)]
    for top in range(0, q_rows // TILE, tall):
        word = jnp.zeros(shape, I16)
        for k in range(terms):
            word = jnp.where(place == lows[k] - I16(top * TILE), units[k], word)
        store(top, tall, word)


def unpack(word_ref, field, first, count_ref):
    tall = count_ref.shape[0] // TILE
    words = word_ref[first // TILE : first // TILE + tall, :, :]
    counts = (words >> jnp.asarray(field * 4, I16)) & 15
    count_ref[...] = counts.astype(BF16).reshape(count_ref.shape)


def lane_tile(tile):
    return pl.ds(pl.multiple_of(tile * 128, 128), 128)


def rows_kernel(
    shard_bits, half_rows, chunks,
    place_ref, count_ref, index_ref, out_grad_hbm, pre_act_hbm, layer_two_hbm,
    row_grad_ref, own_ref, send_ref, word_ref,
    out_grad_ref, pre_act_ref, layer_two_ref, sum_ref, sems,
):
    rows = out_grad_ref.shape[0] // chunks
    fetch_layer = pltpu.make_async_copy(layer_two_hbm, layer_two_ref, sems.at[2 * chunks])
    fetch_layer.start()
    for chunk in range(chunks):
        block = pl.ds(chunk * rows, rows)
        for at, (source, target) in enumerate(((out_grad_hbm, out_grad_ref), (pre_act_hbm, pre_act_ref))):
            pltpu.make_async_copy(
                source.at[block, :], target.at[block, :], sems.at[2 * chunk + at]
            ).start()

    own_shard, own_core = place_ref[0], place_ref[1]
    part_bits = shard_bits - 1

    def build(tile):
        lanes = lane_tile(tile)
        index = index_ref[:, lanes]
        row = index & ((1 << part_bits) - 1)
        half = ((index >> part_bits) & 1) ^ own_core ^ 1
        index = half * half_rows + (((index >> shard_bits) ^ own_shard) << part_bits) + row

        def store(top, tall, words):
            word_ref[top : top + tall, :, lanes] = words

        build_words(index, word_ref.shape[0] * TILE, store)

    tiles = rows // 128
    fetch_layer.wait()
    sum_ref[...] = jnp.zeros_like(sum_ref)

    @pl.loop(0, chunks)
    def _(chunk):
        block = pl.ds(pl.multiple_of(chunk * rows, rows), rows)
        for at, (source, target) in enumerate(((out_grad_hbm, out_grad_ref), (pre_act_hbm, pre_act_ref))):
            pltpu.make_async_copy(
                source.at[block, :], target.at[block, :], sems.at[2 * chunk + at]
            ).wait()
        live = count_ref[0] - chunk * rows

        @pl.when(live < rows)
        def _():
            out_grad = out_grad_ref[block, :].astype(F32)
            place = lax.broadcasted_iota(jnp.int32, out_grad.shape, 0)
            masked = jnp.where(place < live, out_grad, jnp.zeros_like(out_grad))
            out_grad_ref[block, :] = masked.astype(BF16)

        masked = out_grad_ref[block, :]
        pre_act = pre_act_ref[block, :]
        back = lax.dot_general(
            masked, layer_two_ref[...], (((1,), (1,)), ((), ())), preferred_element_type=F32
        )
        activ = jnp.maximum(pre_act, jnp.zeros_like(pre_act))
        sum_ref[...] += transposed_dot(activ, masked)
        for tile in range(tiles):
            build(chunk * tiles + tile)
        row_grad_ref[block, :] = jnp.where(
            pre_act.astype(F32) > 0, back, jnp.zeros_like(back)
        ).astype(BF16)

    halves(sum_ref, own_ref, send_ref, own_core)


def row_gradients(place, batch_count, out_grad, pre_act, layer_two, index, hot_total, shard_rows):
    rows, d_out = out_grad.shape
    d_h = pre_act.shape[1]
    chunks = 4
    deep = hot_total // FIELDS // TILE
    half = jax.ShapeDtypeStruct((d_h, d_out // 2), BF16)
    return pl.pallas_call(
        functools.partial(rows_kernel, shard_rows.bit_length() - 1, hot_total // 2, chunks),
        in_specs=[scalars(), scalars(), whole()] + [pl.BlockSpec(memory_space=pltpu.HBM)] * 3,
        out_specs=[whole()] * 4,
        out_shape=[
            jax.ShapeDtypeStruct((rows, d_h), BF16),
            half,
            half,
            jax.ShapeDtypeStruct((deep, TILE, rows), I16),
        ],
        scratch_shapes=[
            pltpu.VMEM((rows, d_out), BF16),
            pltpu.VMEM((rows, d_h), BF16),
            pltpu.VMEM((d_h, d_out), BF16),
            pltpu.VMEM((d_h, d_out), F32),
            pltpu.SemaphoreType.DMA((2 * chunks + 1,)),
        ],
        compiler_params=params(48),
        cost_estimate=cost(10**10, 10**8),
        name="row_gradients",
    )(place, batch_count, index, out_grad, pre_act, layer_two)


def table_sums(word_ref, row_grad_ref, counts, scale, sums_ref, beside, after):
    tall = counts[0].shape[0]
    parts = word_ref.shape[0] * TILE // tall
    unpack(word_ref, 0, 0, counts[0])

    @pl.loop(0, FIELDS)
    def _(field):
        for part in range(parts):
            found = jnp.dot(counts[part % 2][...], row_grad_ref[...], preferred_element_type=F32)
            ahead = jnp.minimum(field + 1, FIELDS - 1) if part == parts - 1 else field
            unpack(word_ref, ahead, (part + 1) % parts * tall, counts[(part + 1) % 2])
            beside(field * parts + part, parts)
            rows = pl.ds(pl.multiple_of((field * parts + part) * tall, tall), tall)
            sums_ref[rows, :] = (found * scale).astype(BF16)
        after(field)


def hot_kernel(scale, word_ref, row_grad_ref, index_ref, sums_ref, cold_word_ref, *counts):
    rows = row_grad_ref.shape[0]

    def build(step, parts):
        tiles = rows // 128 // (FIELDS * parts)
        for tile in range(tiles):
            lanes = lane_tile(step * tiles + tile)

            def store(top, deep, words, lanes=lanes):
                cold_word_ref[top : top + deep, :, lanes] = words

            build_words(index_ref[:, lanes], cold_word_ref.shape[0] * TILE, store)

    table_sums(word_ref, row_grad_ref, counts, scale, sums_ref, build, lambda field: None)


def hot_sums(words, row_grad, cold_index, cold_rows, fanout):
    rows, d_h = row_grad.shape
    q_rows = words.shape[0] * TILE
    return pl.pallas_call(
        functools.partial(hot_kernel, 1.0 / fanout),
        in_specs=[whole(), whole(), whole()],
        out_specs=[whole()] * 2,
        out_shape=[
            jax.ShapeDtypeStruct((q_rows * FIELDS, d_h), BF16),
            jax.ShapeDtypeStruct((cold_rows // FIELDS // TILE, TILE, rows), I16),
        ],
        scratch_shapes=[pltpu.VMEM((min(256, q_rows), rows), BF16)] * 2,
        compiler_params=params(24),
        cost_estimate=cost(10**10, 10**8),
        name="hot_sums",
    )(words, row_grad, cold_index)


def cold_kernel(scale, word_ref, row_grad_ref, feats_ref, grad_ref, sums_ref, held_ref, sem, *counts):
    fetch = pltpu.make_async_copy(feats_ref, held_ref, sem)
    fetch.start()
    grad_ref[...] = jnp.zeros_like(grad_ref)
    tall = word_ref.shape[0] * TILE

    def add_product(field):
        @pl.when(field == 0)
        def _():
            pltpu.make_async_copy(feats_ref, held_ref, sem).wait()

        rows = pl.ds(pl.multiple_of(field * tall, tall), tall)
        grad_ref[...] += transposed_dot(held_ref[rows, :], sums_ref[rows, :])

    table_sums(
        word_ref, row_grad_ref, counts, scale, sums_ref, lambda step, parts: None, add_product
    )


def cold_grad(words, row_grad, feats, fanout):
    rows, d_h = row_grad.shape
    cold_rows, d_in = feats.shape
    q_rows = cold_rows // FIELDS
    return pl.pallas_call(
        functools.partial(cold_kernel, 1.0 / fanout),
        in_specs=[whole(), whole(), in_place()],
        out_specs=whole(),
        out_shape=jax.ShapeDtypeStruct((d_in, d_h), F32),
        scratch_shapes=[
            pltpu.VMEM((cold_rows, d_h), BF16),
            pltpu.VMEM((cold_rows, d_in), BF16),
            pltpu.SemaphoreType.DMA,
        ]
        + [pltpu.VMEM((min(256, q_rows), rows), BF16)] * 2,
        compiler_params=params(24),
        cost_estimate=cost(10**10, 10**8),
        name="cold_grad",
    )(words, row_grad, feats)


def join_kernel(parts, place_ref, cold_ref, keep_ref, other_ref, two_ref, fetched_ref, *rest):
    feats, (own_ref, send_ref, pair_ref, sums_ref) = rest[:parts], rest[parts:]
    own_core = place_ref[1]
    d_in, d_h = cold_ref.shape
    wide = d_h // 2
    sums = keep_ref[...].astype(F32) + other_ref[...].astype(F32)
    sums_ref[...] = sums.astype(BF16)

    @pl.loop(0, d_in // 256)
    def _(block):
        rows = pl.ds(pl.multiple_of(block * 256, 256), 256)
        part = jnp.concatenate([part[:, rows] for part in feats], axis=0)
        total = (cold_ref[rows, :] + transposed_dot(part, sums_ref[...])).astype(BF16)
        first, second = total[:, :wide], total[:, wide:]

        @pl.when(own_core == 0)
        def _():
            own_ref[rows, :] = first
            send_ref[rows, :] = second

        @pl.when(own_core == 1)
        def _():
            own_ref[rows, :] = second
            send_ref[rows, :] = first

    pair_ref[...] = (two_ref[...].astype(F32) + fetched_ref[...].astype(F32)).astype(BF16)


def join(place, cold, keep, other, two, fetched_two, feats):
    d_in, d_h = cold.shape
    half = jax.ShapeDtypeStruct((d_in, d_h // 2), BF16)
    return pl.pallas_call(
        functools.partial(join_kernel, len(feats)),
        in_specs=[scalars()] + [whole()] * (5 + len(feats)),
        out_specs=[whole()] * 3,
        out_shape=[half, half, jax.ShapeDtypeStruct(two.shape, BF16)],
        scratch_shapes=[pltpu.VMEM(keep.shape, BF16)],
        compiler_params=params(32),
        cost_estimate=cost(2 * keep.shape[0] * d_h * d_in, 4 * d_in * d_h),
        name="join",
    )(place, cold, keep, other, two, fetched_two, *feats)


def share_rows(rows, members, place_ref, k):
    size = rows // members
    return pl.ds(pl.multiple_of((place_ref[0] ^ k) * size, TILE), size)


def pair_kernel(place_ref, one_ref, other_ref, two_ref, *out_refs):
    members = len(out_refs)
    for k, out_ref in enumerate(out_refs):
        here = share_rows(one_ref.shape[0], members, place_ref, k)
        total = one_ref[here, :].astype(F32) + other_ref[here, :].astype(F32)
        out_ref[: here.size, :] = total.astype(BF16)
        base = here.size
        here = share_rows(two_ref.shape[0], members, place_ref, k)
        out_ref[base : base + here.size, :] = two_ref[here, :]


def pair_sums(place, one, other, two, members):
    wide = one.shape[1]
    rows = one.shape[0] + two.shape[0]
    share = jax.ShapeDtypeStruct((rows // members, wide), BF16)
    return pl.pallas_call(
        pair_kernel,
        in_specs=[scalars()] + [whole()] * 3,
        out_specs=[whole()] * members,
        out_shape=[share] * members,
        compiler_params=params(16),
        cost_estimate=cost(0, 6 * rows * wide),
        name="pair_sums",
    )(place, one, other, two)


def lay_kernel(members, parts, place_ref, *refs):
    owns, others, refs = refs[:parts], refs[parts : 2 * parts], refs[2 * parts :]
    outs, held, sems = refs[:2], refs[2:4], refs[4]
    own_core = place_ref[1]
    wide = owns[0].shape[1]
    each = members // parts
    copies = []
    for k in range(members):
        base = k % each * (owns[0].shape[0] // each)
        for at, (out_ref, held_ref) in enumerate(zip(outs, held)):
            here = share_rows(out_ref.shape[0], members, place_ref, k)
            for ref, core in ((owns[k // each], own_core), (others[k // each], 1 - own_core)):
                lanes = pl.ds(pl.multiple_of(core * wide, wide), wide)
                held_ref[here, lanes] = ref[base : base + here.size, :].astype(F32)
            copy = pltpu.make_async_copy(held_ref.at[here, :], out_ref.at[here, :], sems.at[2 * k + at])
            copy.start()
            copies.append(copy)
            base += here.size
    for copy in copies:
        copy.wait()


def lay(place, owns, others, members, rows_of):
    wide = owns[0].shape[1]
    shapes = [(rows, 2 * wide) for rows in rows_of]
    return pl.pallas_call(
        functools.partial(lay_kernel, members, len(owns)),
        in_specs=[scalars()] + [whole()] * (2 * len(owns)),
        out_specs=[in_place()] * len(rows_of),
        out_shape=[jax.ShapeDtypeStruct(shape, F32) for shape in shapes],
        scratch_shapes=[pltpu.VMEM(shape, F32) for shape in shapes]
        + [pltpu.SemaphoreType.DMA((2 * members,))],
        compiler_params=params(16),
        cost_estimate=cost(0, 12 * sum(rows_of) * wide),
        name="lay",
    )(place, *owns, *others)


def exchange(array, axis, step):
    size = lax.axis_size(axis)
    return lax.ppermute(array, axis, [(source, source ^ step) for source in range(size)])


def added(*arrays):
    total = arrays[0].astype(F32)
    for array in arrays[1:]:
        total = total + array.astype(F32)
    return total.astype(BF16)


def trade(arrays, axis, step):
    return [arrays[0]] + [exchange(arrays[k], axis, k * step) for k in range(1, len(arrays))]


def sum_over_slice(shares):
    own = added(*trade(shares, "clique", 1))
    n_copy = lax.axis_size("copy")
    steps = [2 << bit for bit in range((n_copy // 2).bit_length() - 1)]
    for near, far in zip(steps, reversed(steps)):
        route = [(j, j ^ (far if j & 1 else near)) for j in range(n_copy)]
        own = added(own, lax.ppermute(own, "copy", route))
    return trade([own] * len(shares), "clique", 1)


def gather_feats(own):
    members = lax.axis_size("clique")
    if members != 4:
        return trade([own] * members, "clique", 1)
    one, two = exchange(own, "clique", 1), exchange(own, "clique", 2)
    middle = own.shape[0] // 2
    top = exchange(two[:middle], "clique", 1)
    bottom = exchange(one[middle:], "clique", 2)
    return [own, one, two, top, bottom]


def on_device(
    out_grad, pre_act, batch_count, layer_two, hot_slots, cold_index, hot_feats, cold_feats
):
    n_clique = lax.axis_size("clique")
    shard_rows, d_in = hot_feats.shape
    d_h = pre_act.shape[1]
    cold_rows = cold_feats.shape[0]
    fanout = hot_slots.shape[1] + cold_index.shape[1]
    copy_at = lax.axis_index("copy")
    place = jnp.stack([lax.axis_index("clique"), copy_at & 1]).astype(jnp.int32)

    half_feats = lax.dynamic_slice_in_dim(
        hot_feats, (copy_at & 1) * (shard_rows // 2), shard_rows // 2, 0
    )
    feats = gather_feats(half_feats)

    row_grad, own_two, twin_two, words = row_gradients(
        place, batch_count, out_grad, pre_act, layer_two, hot_slots.T, shard_rows * n_clique, shard_rows
    )
    fetched_two = exchange(twin_two, "copy", 1)
    sums, words = hot_sums(words, row_grad, cold_index.T, cold_rows, fanout)
    middle = sums.shape[0] // 2
    other, keep = exchange(sums[:middle], "copy", 1), sums[middle:]
    cold = cold_grad(words, row_grad, cold_feats, fanout)
    own_one, twin_one, two = join(place, cold, keep, other, own_two, fetched_two, feats)
    shares = pair_sums(place, own_one, exchange(twin_one, "copy", 1), two, n_clique)
    shares = sum_over_slice(shares)
    middle = n_clique // 2
    parts = [jnp.concatenate(part, axis=0) for part in (shares[:middle], shares[middle:])]
    others = [exchange(part, "copy", 1) for part in parts]
    return tuple(lay(place, parts, others, n_clique, (d_in, d_h)))


def solution(mesh):
    placed = (
        P(("clique", "copy"), None),
        P(("clique", "copy"), None),
        P(("clique", "copy")),
        P(),
        P(("clique", "copy"), None),
        P(("clique", "copy"), None),
        P("clique", None),
        P(("clique", "copy"), None),
    )
    return jax.shard_map(
        on_device, mesh=mesh, in_specs=placed, out_specs=(P(), P()), check_vma=False
    )
```

```python
import functools

import jax
import jax.numpy as jnp
from jax import lax
from jax.experimental import pallas as pl
from jax.experimental.pallas import tpu as pltpu
from jax.sharding import PartitionSpec as P

F32 = jnp.float32
BF16 = jnp.bfloat16
I16 = jnp.int16
FIELDS = 4
TILE = 16


def whole():
    return pl.BlockSpec(memory_space=pltpu.VMEM)


def scalars():
    return pl.BlockSpec(memory_space=pltpu.SMEM)


def in_place():
    return pl.BlockSpec(memory_space=pl.ANY)


def params(mebibytes):
    return pltpu.CompilerParams(vmem_limit_bytes=mebibytes << 20)


def cost(flops, moved):
    return pl.CostEstimate(flops=int(flops), bytes_accessed=int(moved), transcendentals=0)


def transposed_dot(left, right):
    return lax.dot_general(left, right, (((0,), (0,)), ((), ())), preferred_element_type=F32)


def halves(total_ref, own_ref, send_ref, own_core):
    wide = own_ref.shape[1]
    mine = pl.ds(pl.multiple_of(own_core * wide, wide), wide)
    twin = pl.ds(pl.multiple_of((1 - own_core) * wide, wide), wide)
    own_ref[...] = total_ref[:, mine].astype(BF16)
    send_ref[...] = total_ref[:, twin].astype(BF16)


def build_words(index, q_rows, store):
    terms = index.shape[0]
    shift = q_rows.bit_length() - 1
    low = index & (q_rows - 1)
    one = jnp.left_shift(jnp.ones_like(index), (index >> shift) * 4)
    unit = one
    for other in range(1, terms):
        turned_low = jnp.concatenate([low[other:], low[:other]], axis=0)
        turned = jnp.concatenate([one[other:], one[:other]], axis=0)
        unit = unit + jnp.where(turned_low == low, turned, jnp.zeros_like(turned))
    tall = min(256, q_rows) // TILE
    shape = (tall, TILE, 128)
    place = lax.broadcasted_iota(jnp.int32, shape, 0) * TILE + lax.broadcasted_iota(jnp.int32, shape, 1)
    place = place.astype(I16)

    def tile(row):
        return jnp.broadcast_to(row, (TILE, 128)).astype(I16)[None]

    lows = [tile(low[k : k + 1, :]) for k in range(terms)]
    units = [tile(unit[k : k + 1, :]) for k in range(terms)]
    for top in range(0, q_rows // TILE, tall):
        word = jnp.zeros(shape, I16)
        for k in range(terms):
            word = jnp.where(place == lows[k] - I16(top * TILE), units[k], word)
        store(top, tall, word)


def unpack(word_ref, field, count_ref):
    if field < FIELDS - 1:
        counts = word_ref[...] & (15 << (4 * field))
    else:
        counts = (word_ref[...] >> (4 * field)) & 15
    count_ref[...] = counts.astype(BF16).reshape(count_ref.shape)


def unpacked_scale(field):
    return 16.0**field if field < FIELDS - 1 else 1.0


def rows_kernel(
    shard_bits, half_rows, chunks,
    place_ref, count_ref, index_ref, out_grad_hbm, pre_act_hbm, layer_two_hbm,
    row_grad_ref, own_ref, send_ref, word_ref,
    out_grad_ref, pre_act_ref, layer_two_ref, sum_ref, sems,
):
    rows = out_grad_ref.shape[0] // chunks
    blocks = [slice(chunk * rows, (chunk + 1) * rows) for chunk in range(chunks)]
    fetch_layer = pltpu.make_async_copy(layer_two_hbm, layer_two_ref, sems.at[2 * chunks])
    fetches = []
    for chunk, block in enumerate(blocks):
        pair = []
        for at, (source, target) in enumerate(((out_grad_hbm, out_grad_ref), (pre_act_hbm, pre_act_ref))):
            fetch = pltpu.make_async_copy(
                source.at[block, :], target.at[block, :], sems.at[2 * chunk + at]
            )
            fetch.start()
            pair.append(fetch)
        fetches.append(pair)
        if chunk == 0:
            fetch_layer.start()

    own_shard, own_core = place_ref[0], place_ref[1]
    part_bits = shard_bits - 1

    def build(tile):
        lanes = slice(tile * 128, (tile + 1) * 128)
        index = index_ref[:, lanes]
        row = index & ((1 << part_bits) - 1)
        half = ((index >> part_bits) & 1) ^ own_core ^ 1
        index = half * half_rows + (((index >> shard_bits) ^ own_shard) << part_bits) + row

        def store(top, tall, words):
            word_ref[top : top + tall, :, lanes] = words

        build_words(index, word_ref.shape[0] * TILE, store)

    tiles = row_grad_ref.shape[0] // 128
    first = tiles // 4
    for tile in range(first):
        build(tile)
    ends = [first + (tiles - first) * chunk // chunks for chunk in range(chunks + 1)]
    for chunk, block in enumerate(blocks):
        for fetch in fetches[chunk]:
            fetch.wait()
        if chunk == 0:
            fetch_layer.wait()
        live = count_ref[0] - chunk * rows

        @pl.when(live < rows)
        def _(block=block, live=live):
            out_grad = out_grad_ref[block, :].astype(F32)
            place = lax.broadcasted_iota(jnp.int32, out_grad.shape, 0)
            masked = jnp.where(place < live, out_grad, jnp.zeros_like(out_grad))
            out_grad_ref[block, :] = masked.astype(BF16)

        masked = out_grad_ref[block, :]
        pre_act = pre_act_ref[block, :]
        back = lax.dot_general(
            masked, layer_two_ref[...], (((1,), (1,)), ((), ())), preferred_element_type=F32
        )
        row_grad_ref[block, :] = jnp.where(
            pre_act.astype(F32) > 0, back, jnp.zeros_like(back)
        ).astype(BF16)
        activ = jnp.maximum(pre_act, jnp.zeros_like(pre_act))
        part = transposed_dot(activ, masked)
        sum_ref[...] = part if chunk == 0 else sum_ref[...] + part
        for tile in range(ends[chunk], ends[chunk + 1]):
            build(tile)
    halves(sum_ref, own_ref, send_ref, own_core)


def row_gradients(place, batch_count, out_grad, pre_act, layer_two, index, hot_total, shard_rows):
    rows, d_out = out_grad.shape
    d_h = pre_act.shape[1]
    chunks = 4
    deep = hot_total // FIELDS // TILE
    half = jax.ShapeDtypeStruct((d_h, d_out // 2), BF16)
    return pl.pallas_call(
        functools.partial(rows_kernel, shard_rows.bit_length() - 1, hot_total // 2, chunks),
        in_specs=[scalars(), scalars(), whole()] + [pl.BlockSpec(memory_space=pltpu.HBM)] * 3,
        out_specs=[whole()] * 4,
        out_shape=[
            jax.ShapeDtypeStruct((rows, d_h), BF16),
            half,
            half,
            jax.ShapeDtypeStruct((deep, TILE, rows), I16),
        ],
        scratch_shapes=[
            pltpu.VMEM((rows, d_out), BF16),
            pltpu.VMEM((rows, d_h), BF16),
            pltpu.VMEM((d_h, d_out), BF16),
            pltpu.VMEM((d_h, d_out), F32),
            pltpu.SemaphoreType.DMA((2 * chunks + 1,)),
        ],
        compiler_params=params(48),
        cost_estimate=cost(10**10, 10**8),
        name="row_gradients",
    )(place, batch_count, index, out_grad, pre_act, layer_two)


def hot_kernel(
    scale, word_ref, row_grad_ref, index_ref, send_ref, keep_ref, cold_word_ref, *counts
):
    tall, rows = counts[0].shape
    tiles = rows // 128 // FIELDS
    unpack(word_ref, 0, counts[0])
    for field in range(FIELDS):
        found = jnp.dot(counts[field % 2][...], row_grad_ref[...], preferred_element_type=F32)
        out_ref = (send_ref, keep_ref)[field // 2]
        out_ref[field % 2 * tall : (field % 2 + 1) * tall, :] = (
            found * (scale / unpacked_scale(field))
        ).astype(BF16)
        if field + 1 < FIELDS:
            unpack(word_ref, field + 1, counts[(field + 1) % 2])
        for tile in range(field * tiles, (field + 1) * tiles):
            lanes = slice(tile * 128, (tile + 1) * 128)

            def store(top, deep, words, lanes=lanes):
                cold_word_ref[top : top + deep, :, lanes] = words

            build_words(index_ref[:, lanes], cold_word_ref.shape[0] * TILE, store)


def hot_sums(words, row_grad, cold_index, cold_rows, fanout):
    rows, d_h = row_grad.shape
    q_rows = words.shape[0] * TILE
    half = jax.ShapeDtypeStruct((q_rows * FIELDS // 2, d_h), BF16)
    return pl.pallas_call(
        functools.partial(hot_kernel, 1.0 / fanout),
        in_specs=[whole(), whole(), whole()],
        out_specs=[whole()] * 3,
        out_shape=[
            half,
            half,
            jax.ShapeDtypeStruct((cold_rows // FIELDS // TILE, TILE, rows), I16),
        ],
        scratch_shapes=[pltpu.VMEM((q_rows, rows), BF16)] * 2,
        compiler_params=params(40),
        cost_estimate=cost(10**10, 10**8),
        name="hot_sums",
    )(words, row_grad, cold_index)


def cold_kernel(scale, word_ref, row_grad_ref, feats_ref, grad_ref, sums_ref, held_ref, sem, *counts):
    fetch = pltpu.make_async_copy(feats_ref, held_ref, sem)
    fetch.start()
    tall = counts[0].shape[0]

    def add_product(field):
        rows = slice(field * tall, (field + 1) * tall)
        part = transposed_dot(held_ref[rows, :], sums_ref[rows, :])
        grad_ref[...] = part if field == 0 else grad_ref[...] + part

    unpack(word_ref, 0, counts[0])
    for field in range(FIELDS):
        found = jnp.dot(counts[field % 2][...], row_grad_ref[...], preferred_element_type=F32)
        sums_ref[field * tall : (field + 1) * tall, :] = (
            found * (scale / unpacked_scale(field))
        ).astype(BF16)
        if field + 1 < FIELDS:
            unpack(word_ref, field + 1, counts[(field + 1) % 2])
        if field == 1:
            fetch.wait()
        if field > 0:
            add_product(field - 1)
    add_product(FIELDS - 1)


def cold_grad(words, row_grad, feats, fanout):
    rows, d_h = row_grad.shape
    cold_rows, d_in = feats.shape
    q_rows = cold_rows // FIELDS
    return pl.pallas_call(
        functools.partial(cold_kernel, 1.0 / fanout),
        in_specs=[whole(), whole(), in_place()],
        out_specs=whole(),
        out_shape=jax.ShapeDtypeStruct((d_in, d_h), F32),
        scratch_shapes=[
            pltpu.VMEM((cold_rows, d_h), BF16),
            pltpu.VMEM((cold_rows, d_in), BF16),
            pltpu.SemaphoreType.DMA,
            pltpu.VMEM((q_rows, rows), BF16),
            pltpu.VMEM((q_rows, rows), BF16),
        ],
        compiler_params=params(40),
        cost_estimate=cost(10**10, 10**8),
        name="cold_grad",
    )(words, row_grad, feats)


def join_kernel(parts, place_ref, cold_ref, keep_ref, other_ref, two_ref, fetched_ref, *rest):
    feats, (own_ref, send_ref, pair_ref) = rest[:parts], rest[parts:]
    own_core = place_ref[1]
    d_in, d_h = cold_ref.shape
    wide = d_h // 2
    sums = (keep_ref[...].astype(F32) + other_ref[...].astype(F32)).astype(BF16)
    for left in range(0, d_in, 256):
        rows = slice(left, left + 256)
        part = jnp.concatenate([part[:, rows] for part in feats], axis=0)
        total = (cold_ref[rows, :] + transposed_dot(part, sums)).astype(BF16)
        first, second = total[:, :wide], total[:, wide:]

        @pl.when(own_core == 0)
        def _(rows=rows, first=first, second=second):
            own_ref[rows, :] = first
            send_ref[rows, :] = second

        @pl.when(own_core == 1)
        def _(rows=rows, first=first, second=second):
            own_ref[rows, :] = second
            send_ref[rows, :] = first

    pair_ref[...] = (two_ref[...].astype(F32) + fetched_ref[...].astype(F32)).astype(BF16)


def join(place, cold, keep, other, two, fetched_two, feats):
    d_in, d_h = cold.shape
    half = jax.ShapeDtypeStruct((d_in, d_h // 2), BF16)
    return pl.pallas_call(
        functools.partial(join_kernel, len(feats)),
        in_specs=[scalars()] + [whole()] * (5 + len(feats)),
        out_specs=[whole()] * 3,
        out_shape=[half, half, jax.ShapeDtypeStruct(two.shape, BF16)],
        compiler_params=params(32),
        cost_estimate=cost(2 * keep.shape[0] * d_h * d_in, 4 * d_in * d_h),
        name="join",
    )(place, cold, keep, other, two, fetched_two, *feats)


def share_rows(rows, members, place_ref, core, turn):
    size = rows // members
    partner = turn
    if members == 4 and turn == 1:
        partner = 3
    elif members == 4 and turn > 1:
        partner = jnp.where(core == 0, turn - 1, 4 - turn)
    return pl.ds(pl.multiple_of((place_ref[0] ^ partner) * size, TILE), size)


def pair_kernel(place_ref, one_ref, other_ref, two_ref, *out_refs):
    members = len(out_refs)
    for k, out_ref in enumerate(out_refs):
        here = share_rows(one_ref.shape[0], members, place_ref, place_ref[1], k)
        total = one_ref[here, :].astype(F32) + other_ref[here, :].astype(F32)
        out_ref[: here.size, :] = total.astype(BF16)
        base = here.size
        here = share_rows(two_ref.shape[0], members, place_ref, place_ref[1], k)
        out_ref[base : base + here.size, :] = two_ref[here, :]


def pair_sums(place, one, other, two, members):
    wide = one.shape[1]
    rows = one.shape[0] + two.shape[0]
    share = jax.ShapeDtypeStruct((rows // members, wide), BF16)
    return pl.pallas_call(
        pair_kernel,
        in_specs=[scalars()] + [whole()] * 3,
        out_specs=[whole()] * members,
        out_shape=[share] * members,
        compiler_params=params(16),
        cost_estimate=cost(0, 6 * rows * wide),
        name="pair_sums",
    )(place, one, other, two)


def laid_turns(members):
    return [0, members - 1, *range(1, members - 1)]


def lay_kernel(members, parts, twin, place_ref, *refs):
    halves_in, refs = refs[:parts], refs[parts:]
    refs = refs[2:] if twin else refs
    outs, held, sems = refs[:2], refs[2:4], refs[4]
    core = 1 - place_ref[1] if twin else place_ref[1]
    wide = halves_in[0].shape[1]
    lanes = pl.ds(pl.multiple_of(core * wide, wide), wide)
    each = members // parts
    copies = []
    for k, turn in enumerate(laid_turns(members)):
        base = k % each * (halves_in[0].shape[0] // each)
        for at, (out_ref, held_ref) in enumerate(zip(outs, held)):
            here = share_rows(out_ref.shape[0], members, place_ref, core, turn)
            held_ref[here, :] = halves_in[k // each][base : base + here.size, :].astype(F32)
            copy = pltpu.make_async_copy(
                held_ref.at[here, :], out_ref.at[here, lanes], sems.at[2 * k + at]
            )
            copy.start()
            copies.append(copy)
            base += here.size
    for copy in copies:
        copy.wait()


def lay(place, parts, members, rows_of, before=()):
    wide = parts[0].shape[1]
    count = 1 + len(parts)
    return pl.pallas_call(
        functools.partial(lay_kernel, members, len(parts), bool(before)),
        in_specs=[scalars()] + [whole()] * len(parts) + [in_place()] * len(before),
        out_specs=[in_place()] * len(rows_of),
        out_shape=[jax.ShapeDtypeStruct((rows, 2 * wide), F32) for rows in rows_of],
        input_output_aliases={count + at: at for at in range(len(before))},
        scratch_shapes=[pltpu.VMEM((rows, wide), F32) for rows in rows_of]
        + [pltpu.SemaphoreType.DMA((2 * members,))],
        compiler_params=params(16),
        cost_estimate=cost(10**10, 10**8),
        name="lay",
    )(place, *parts, *before)


def exchange(array, axis, step):
    size = lax.axis_size(axis)
    return lax.ppermute(array, axis, [(source, source ^ step) for source in range(size)])


def added(*arrays):
    total = arrays[0].astype(F32)
    for array in arrays[1:]:
        total = total + array.astype(F32)
    return total.astype(BF16)


def route_of(n_clique, n_copy, turn):
    moves = [(0, 0), (3, 3), (1, 2), (2, 1)][turn] if n_clique == 4 else (turn, turn)
    return [
        (i * n_copy + j, (i ^ moves[j & 1]) * n_copy + j)
        for i in range(n_clique)
        for j in range(n_copy)
    ]


def trade(arrays):
    n_clique, n_copy = lax.axis_size("clique"), lax.axis_size("copy")
    return [arrays[0]] + [
        lax.ppermute(arrays[turn], ("clique", "copy"), route_of(n_clique, n_copy, turn))
        for turn in range(1, n_clique)
    ]


def sum_over_slice(shares):
    own = added(*trade(shares))
    n_copy = lax.axis_size("copy")
    steps = [2 << bit for bit in range((n_copy // 2).bit_length() - 1)]
    for near, far in zip(steps, reversed(steps)):
        route = [(j, j ^ (far if j & 1 else near)) for j in range(n_copy)]
        own = added(own, lax.ppermute(own, "copy", route))
    return trade([own] * len(shares))


def gather_feats(own):
    members = lax.axis_size("clique")
    if members != 4:
        return [own] + [exchange(own, "clique", k) for k in range(1, members)]
    one, two = exchange(own, "clique", 1), exchange(own, "clique", 2)
    middle = own.shape[0] // 2
    top = exchange(two[:middle], "clique", 1)
    bottom = exchange(one[middle:], "clique", 2)
    return [own, one, two, top, bottom]


def on_device(
    out_grad, pre_act, batch_count, layer_two, hot_slots, cold_index, hot_feats, cold_feats
):
    n_clique = lax.axis_size("clique")
    shard_rows, d_in = hot_feats.shape
    d_h = pre_act.shape[1]
    cold_rows = cold_feats.shape[0]
    fanout = hot_slots.shape[1] + cold_index.shape[1]
    copy_at = lax.axis_index("copy")
    place = jnp.stack([lax.axis_index("clique"), copy_at & 1]).astype(jnp.int32)

    half_feats = lax.dynamic_slice_in_dim(
        hot_feats, (copy_at & 1) * (shard_rows // 2), shard_rows // 2, 0
    )
    feats = gather_feats(half_feats)

    row_grad, own_two, twin_two, words = row_gradients(
        place, batch_count, out_grad, pre_act, layer_two, hot_slots.T, shard_rows * n_clique, shard_rows
    )
    fetched_two = exchange(twin_two, "copy", 1)
    send, keep, words = hot_sums(words, row_grad, cold_index.T, cold_rows, fanout)
    other = exchange(send, "copy", 1)
    cold = cold_grad(words, row_grad, cold_feats, fanout)
    own_one, twin_one, two = join(place, cold, keep, other, own_two, fetched_two, feats)
    shares = pair_sums(place, own_one, exchange(twin_one, "copy", 1), two, n_clique)
    shares = sum_over_slice(shares)
    middle = n_clique // 2
    shares = [shares[turn] for turn in laid_turns(n_clique)]
    parts = [jnp.concatenate(part, axis=0) for part in (shares[:middle], shares[middle:])]
    others = [exchange(part, "copy", 1) for part in parts]
    rows_of = (d_in, d_h)
    own = lay(place, parts, n_clique, rows_of)
    return tuple(lay(place, others, n_clique, rows_of, own))


def solution(mesh):
    placed = (
        P(("clique", "copy"), None),
        P(("clique", "copy"), None),
        P(("clique", "copy")),
        P(),
        P(("clique", "copy"), None),
        P(("clique", "copy"), None),
        P("clique", None),
        P(("clique", "copy"), None),
    )
    return jax.shard_map(
        on_device, mesh=mesh, in_specs=placed, out_specs=(P(), P()), check_vma=False
    )
```

```python
import functools

import jax
import jax.numpy as jnp
from jax import lax
from jax.experimental import pallas as pl
from jax.experimental.pallas import tpu as pltpu
from jax.sharding import PartitionSpec as P

F32 = jnp.float32
BF16 = jnp.bfloat16
I16 = jnp.int16
FIELDS = 4
TILE = 16
START_MIB = 60
ROWS_MIB = 50


def whole():
    return pl.BlockSpec(memory_space=pltpu.VMEM)


def scalars():
    return pl.BlockSpec(memory_space=pltpu.SMEM)


def in_place():
    return pl.BlockSpec(memory_space=pl.ANY)


def params(mebibytes):
    return pltpu.CompilerParams(vmem_limit_bytes=mebibytes << 20)


def cost(flops, moved):
    return pl.CostEstimate(flops=int(flops), bytes_accessed=int(moved), transcendentals=0)


def transposed_dot(left, right):
    return lax.dot_general(left, right, (((0,), (0,)), ((), ())), preferred_element_type=F32)


def build_words(index, q_rows, store):
    terms = index.shape[0]
    shift = q_rows.bit_length() - 1
    low = index & (q_rows - 1)
    one = jnp.left_shift(jnp.ones_like(index), (index >> shift) * 4)
    unit = one
    for other in range(1, terms):
        turned_low = jnp.concatenate([low[other:], low[:other]], axis=0)
        turned = jnp.concatenate([one[other:], one[:other]], axis=0)
        unit = unit + jnp.where(turned_low == low, turned, jnp.zeros_like(turned))
    tall = min(256, q_rows) // TILE
    shape = (tall, TILE, 128)
    place = lax.broadcasted_iota(jnp.int32, shape, 0) * TILE + lax.broadcasted_iota(jnp.int32, shape, 1)
    place = place.astype(I16)

    def tile(row):
        return jnp.broadcast_to(row, (TILE, 128)).astype(I16)[None]

    lows = [tile(low[k : k + 1, :]) for k in range(terms)]
    units = [tile(unit[k : k + 1, :]) for k in range(terms)]
    for top in range(0, q_rows // TILE, tall):
        word = jnp.zeros(shape, I16)
        for k in range(terms):
            word = jnp.where(place == lows[k] - I16(top * TILE), units[k], word)
        store(top, tall, word)


def unpack(word_ref, first, count_ref):
    tall = count_ref.shape[0] // 2
    for k in range(2):
        counts = (word_ref[...] >> (4 * (first + k))) & 15
        count_ref[k * tall : (k + 1) * tall, :] = counts.astype(BF16).reshape(tall, count_ref.shape[1])


def start_kernel(
    shard_bits, half_rows, place_ref, index_ref, feats_hbm, word_hbm, half_hbm, word_ref, sems
):
    own_shard, own_core = place_ref[0], place_ref[1]
    feats_rows = half_hbm.shape[0]
    here = pl.ds(pl.multiple_of(own_core * feats_rows, TILE), feats_rows)
    copies = [pltpu.make_async_copy(feats_hbm.at[here, :], half_hbm, sems.at[0])]
    copies[0].start()
    part_bits = shard_bits - 1
    parts = sems.shape[0] - 1
    wide = index_ref.shape[1] // parts
    for part in range(parts):

        @pl.loop(0, wide // 128)
        def _(tile, part=part):
            lanes = pl.ds(pl.multiple_of(part * wide + tile * 128, 128), 128)
            index = index_ref[:, lanes]
            row = index & ((1 << part_bits) - 1)
            half = ((index >> part_bits) & 1) ^ own_core ^ 1
            index = half * half_rows + (((index >> shard_bits) ^ own_shard) << part_bits) + row

            def store(top, tall, words):
                word_ref[top : top + tall, :, lanes] = words

            build_words(index, word_ref.shape[0] * TILE, store)

        lanes = slice(part * wide, (part + 1) * wide)
        copies.append(
            pltpu.make_async_copy(
                word_ref.at[:, :, lanes], word_hbm.at[:, :, lanes], sems.at[part + 1]
            )
        )
        copies[-1].start()
    for copy in copies:
        copy.wait()


def start(place, index, hot_feats, hot_total):
    rows = index.shape[1]
    shard_rows, d_in = hot_feats.shape
    deep = hot_total // FIELDS // TILE
    return pl.pallas_call(
        functools.partial(start_kernel, shard_rows.bit_length() - 1, hot_total // 2),
        in_specs=[scalars(), whole(), pl.BlockSpec(memory_space=pltpu.HBM)],
        out_specs=[in_place()] * 2,
        out_shape=[
            jax.ShapeDtypeStruct((deep, TILE, rows), I16),
            jax.ShapeDtypeStruct((shard_rows // 2, d_in), BF16),
        ],
        scratch_shapes=[
            pltpu.VMEM((deep, TILE, rows), I16),
            pltpu.SemaphoreType.DMA((5,)),
        ],
        compiler_params=params(START_MIB),
        cost_estimate=cost(10**10, 10**8),
        name="start",
    )(place, index, hot_feats)


def rows_kernel(
    chunks, place_ref, count_ref, out_grad_hbm, pre_act_hbm, layer_two_hbm,
    row_grad_ref, own_ref, send_ref,
    out_grad_ref, pre_act_ref, layer_two_ref, sems,
):
    rows = out_grad_ref.shape[0] // chunks
    blocks = [slice(chunk * rows, (chunk + 1) * rows) for chunk in range(chunks)]
    fetch_layer = pltpu.make_async_copy(layer_two_hbm, layer_two_ref, sems.at[2 * chunks])
    fetches = []
    for chunk, block in enumerate(blocks):
        pair = []
        for at, (source, target) in enumerate(((out_grad_hbm, out_grad_ref), (pre_act_hbm, pre_act_ref))):
            fetch = pltpu.make_async_copy(
                source.at[block, :], target.at[block, :], sems.at[2 * chunk + at]
            )
            fetch.start()
            pair.append(fetch)
        fetches.append(pair)
        if chunk == 0:
            fetch_layer.start()
    for chunk, block in enumerate(blocks):
        for fetch in fetches[chunk]:
            fetch.wait()
        if chunk == 0:
            fetch_layer.wait()
        live = count_ref[0] - chunk * rows

        @pl.when(live < rows)
        def _(block=block, live=live):
            out_grad = out_grad_ref[block, :].astype(F32)
            place = lax.broadcasted_iota(jnp.int32, out_grad.shape, 0)
            masked = jnp.where(place < live, out_grad, jnp.zeros_like(out_grad))
            out_grad_ref[block, :] = masked.astype(BF16)

        back = lax.dot_general(
            out_grad_ref[block, :],
            layer_two_ref[...],
            (((1,), (1,)), ((), ())),
            preferred_element_type=F32,
        )
        pre_act = pre_act_ref[block, :]
        row_grad_ref[block, :] = jnp.where(
            pre_act.astype(F32) > 0, back, jnp.zeros_like(back)
        ).astype(BF16)
        pre_act_ref[block, :] = jnp.maximum(pre_act, jnp.zeros_like(pre_act))
    total = transposed_dot(pre_act_ref[...], out_grad_ref[...]).astype(BF16)
    store_halves(total, slice(None), place_ref[1], own_ref, send_ref)


def store_halves(total, rows, own_core, own_ref, send_ref):
    wide = own_ref.shape[1]
    first, second = total[:, :wide], total[:, wide:]

    @pl.when(own_core == 0)
    def _():
        own_ref[rows, :] = first
        send_ref[rows, :] = second

    @pl.when(own_core == 1)
    def _():
        own_ref[rows, :] = second
        send_ref[rows, :] = first


def row_gradients(place, batch_count, out_grad, pre_act, layer_two):
    rows, d_out = out_grad.shape
    d_h = pre_act.shape[1]
    chunks = 4
    half = jax.ShapeDtypeStruct((d_h, d_out // 2), BF16)
    return pl.pallas_call(
        functools.partial(rows_kernel, chunks),
        in_specs=[scalars(), scalars()] + [pl.BlockSpec(memory_space=pltpu.HBM)] * 3,
        out_specs=[whole()] * 3,
        out_shape=[jax.ShapeDtypeStruct((rows, d_h), BF16), half, half],
        scratch_shapes=[
            pltpu.VMEM((rows, d_out), BF16),
            pltpu.VMEM((rows, d_h), BF16),
            pltpu.VMEM((d_h, d_out), BF16),
            pltpu.SemaphoreType.DMA((2 * chunks + 1,)),
        ],
        compiler_params=params(ROWS_MIB),
        cost_estimate=cost(10**10, 10**8),
        name="row_gradients",
    )(place, batch_count, out_grad, pre_act, layer_two)


def hot_kernel(
    scale, word_ref, row_grad_ref, index_ref, send_ref, keep_ref, cold_word_ref, *counts
):
    tiles = row_grad_ref.shape[0] // 128 // 2
    unpack(word_ref, 0, counts[0])
    for turn, out_ref in enumerate((send_ref, keep_ref)):
        found = jnp.dot(counts[turn][...], row_grad_ref[...], preferred_element_type=F32)
        out_ref[...] = (found * scale).astype(BF16)
        if turn == 0:
            unpack(word_ref, 2, counts[1])
        for tile in range(turn * tiles, (turn + 1) * tiles):
            lanes = slice(tile * 128, (tile + 1) * 128)

            def store(top, deep, words, lanes=lanes):
                cold_word_ref[top : top + deep, :, lanes] = words

            build_words(index_ref[:, lanes], cold_word_ref.shape[0] * TILE, store)


def hot_sums(words, row_grad, cold_index, cold_rows, fanout):
    rows, d_h = row_grad.shape
    q_rows = words.shape[0] * TILE
    half = jax.ShapeDtypeStruct((q_rows * FIELDS // 2, d_h), BF16)
    return pl.pallas_call(
        functools.partial(hot_kernel, 1.0 / fanout),
        in_specs=[whole(), whole(), whole()],
        out_specs=[whole()] * 3,
        out_shape=[
            half,
            half,
            jax.ShapeDtypeStruct((cold_rows // FIELDS // TILE, TILE, rows), I16),
        ],
        scratch_shapes=[pltpu.VMEM((2 * q_rows, rows), BF16)] * 2,
        compiler_params=params(40),
        cost_estimate=cost(10**10, 10**8),
        name="hot_sums",
    )(words, row_grad, cold_index)


def cold_kernel(scale, word_ref, row_grad_ref, feats_ref, grad_ref, sums_ref, held_ref, sem, *counts):
    fetch = pltpu.make_async_copy(feats_ref, held_ref, sem)
    fetch.start()
    tall = counts[0].shape[0]
    unpack(word_ref, 0, counts[0])
    for turn in range(2):
        rows = slice(turn * tall, (turn + 1) * tall)
        found = jnp.dot(counts[turn][...], row_grad_ref[...], preferred_element_type=F32)
        sums_ref[rows, :] = (found * scale).astype(BF16)
        if turn == 0:
            unpack(word_ref, 2, counts[1])
            fetch.wait()
        part = transposed_dot(held_ref[rows, :], sums_ref[rows, :])
        grad_ref[...] = part if turn == 0 else grad_ref[...] + part


def cold_grad(words, row_grad, feats, fanout):
    rows, d_h = row_grad.shape
    cold_rows, d_in = feats.shape
    q_rows = cold_rows // FIELDS
    return pl.pallas_call(
        functools.partial(cold_kernel, 1.0 / fanout),
        in_specs=[whole(), whole(), in_place()],
        out_specs=whole(),
        out_shape=jax.ShapeDtypeStruct((d_in, d_h), F32),
        scratch_shapes=[
            pltpu.VMEM((cold_rows, d_h), BF16),
            pltpu.VMEM((cold_rows, d_in), BF16),
            pltpu.SemaphoreType.DMA,
            pltpu.VMEM((2 * q_rows, rows), BF16),
            pltpu.VMEM((2 * q_rows, rows), BF16),
        ],
        compiler_params=params(40),
        cost_estimate=cost(10**10, 10**8),
        name="cold_grad",
    )(words, row_grad, feats)


def join_kernel(parts, place_ref, cold_ref, keep_ref, other_ref, two_ref, fetched_ref, *rest):
    feats, (own_ref, send_ref, pair_ref) = rest[:parts], rest[parts:]
    own_core = place_ref[1]
    d_in, d_h = cold_ref.shape
    sums = (keep_ref[...].astype(F32) + other_ref[...].astype(F32)).astype(BF16)
    for left in range(0, d_in, 256):
        rows = slice(left, left + 256)
        part = jnp.concatenate([part[:, rows] for part in feats], axis=0)
        total = (cold_ref[rows, :] + transposed_dot(part, sums)).astype(BF16)
        store_halves(total, rows, own_core, own_ref, send_ref)

    pair_ref[...] = (two_ref[...].astype(F32) + fetched_ref[...].astype(F32)).astype(BF16)


def join(place, cold, keep, other, two, fetched_two, feats):
    d_in, d_h = cold.shape
    half = jax.ShapeDtypeStruct((d_in, d_h // 2), BF16)
    return pl.pallas_call(
        functools.partial(join_kernel, len(feats)),
        in_specs=[scalars()] + [whole()] * (5 + len(feats)),
        out_specs=[whole()] * 3,
        out_shape=[half, half, jax.ShapeDtypeStruct(two.shape, BF16)],
        compiler_params=params(32),
        cost_estimate=cost(2 * keep.shape[0] * d_h * d_in, 4 * d_in * d_h),
        name="join",
    )(place, cold, keep, other, two, fetched_two, *feats)


def share_rows(rows, members, place_ref, core, turn):
    size = rows // members
    partner = turn
    if members == 4 and turn == 1:
        partner = 3
    elif members == 4 and turn > 1:
        partner = jnp.where(core == 0, turn - 1, 4 - turn)
    return pl.ds(pl.multiple_of((place_ref[0] ^ partner) * size, TILE), size)


def pair_kernel(place_ref, one_ref, other_ref, two_ref, *out_refs):
    members = len(out_refs)
    for k, out_ref in enumerate(out_refs):
        here = share_rows(one_ref.shape[0], members, place_ref, place_ref[1], k)
        total = one_ref[here, :].astype(F32) + other_ref[here, :].astype(F32)
        out_ref[: here.size, :] = total.astype(BF16)
        base = here.size
        here = share_rows(two_ref.shape[0], members, place_ref, place_ref[1], k)
        out_ref[base : base + here.size, :] = two_ref[here, :]


def pair_sums(place, one, other, two, members):
    wide = one.shape[1]
    rows = one.shape[0] + two.shape[0]
    share = jax.ShapeDtypeStruct((rows // members, wide), BF16)
    return pl.pallas_call(
        pair_kernel,
        in_specs=[scalars()] + [whole()] * 3,
        out_specs=[whole()] * members,
        out_shape=[share] * members,
        compiler_params=params(16),
        cost_estimate=cost(0, 6 * rows * wide),
        name="pair_sums",
    )(place, one, other, two)


def laid_turns(members):
    return [0, members - 1, *range(1, members - 1)]


def lay_kernel(members, parts, twin, place_ref, *refs):
    halves_in, refs = refs[:parts], refs[parts:]
    refs = refs[2:] if twin else refs
    outs, held, sems = refs[:2], refs[2:4], refs[4]
    core = 1 - place_ref[1] if twin else place_ref[1]
    wide = halves_in[0].shape[1]
    lanes = pl.ds(pl.multiple_of(core * wide, wide), wide)
    each = members // parts
    copies = []
    for k, turn in enumerate(laid_turns(members)):
        base = k % each * (halves_in[0].shape[0] // each)
        for at, (out_ref, held_ref) in enumerate(zip(outs, held)):
            here = share_rows(out_ref.shape[0], members, place_ref, core, turn)
            held_ref[here, :] = halves_in[k // each][base : base + here.size, :].astype(F32)
            copy = pltpu.make_async_copy(
                held_ref.at[here, :], out_ref.at[here, lanes], sems.at[2 * k + at]
            )
            copy.start()
            copies.append(copy)
            base += here.size
    for copy in copies:
        copy.wait()


def lay(place, parts, members, rows_of, before=()):
    wide = parts[0].shape[1]
    count = 1 + len(parts)
    return pl.pallas_call(
        functools.partial(lay_kernel, members, len(parts), bool(before)),
        in_specs=[scalars()] + [whole()] * len(parts) + [in_place()] * len(before),
        out_specs=[in_place()] * len(rows_of),
        out_shape=[jax.ShapeDtypeStruct((rows, 2 * wide), F32) for rows in rows_of],
        input_output_aliases={count + at: at for at in range(len(before))},
        scratch_shapes=[pltpu.VMEM((rows, wide), F32) for rows in rows_of]
        + [pltpu.SemaphoreType.DMA((2 * members,))],
        compiler_params=params(16),
        cost_estimate=cost(10**10, 10**8),
        name="lay",
    )(place, *parts, *before)


def exchange(array, axis, step):
    size = lax.axis_size(axis)
    return lax.ppermute(array, axis, [(source, source ^ step) for source in range(size)])


def added(*arrays):
    total = arrays[0].astype(F32)
    for array in arrays[1:]:
        total = total + array.astype(F32)
    return total.astype(BF16)


def route_of(n_clique, n_copy, turn):
    moves = [(0, 0), (3, 3), (1, 2), (2, 1)][turn] if n_clique == 4 else (turn, turn)
    return [
        (i * n_copy + j, (i ^ moves[j & 1]) * n_copy + j)
        for i in range(n_clique)
        for j in range(n_copy)
    ]


def trade(arrays):
    n_clique, n_copy = lax.axis_size("clique"), lax.axis_size("copy")
    return [arrays[0]] + [
        lax.ppermute(arrays[turn], ("clique", "copy"), route_of(n_clique, n_copy, turn))
        for turn in range(1, n_clique)
    ]


def sum_over_slice(shares):
    own = added(*trade(shares))
    n_copy = lax.axis_size("copy")
    steps = [2 << bit for bit in range((n_copy // 2).bit_length() - 1)]
    for near, far in zip(steps, reversed(steps)):
        route = [(j, j ^ (far if j & 1 else near)) for j in range(n_copy)]
        own = added(own, lax.ppermute(own, "copy", route))
    return trade([own] * len(shares))


def gather_feats(own):
    members = lax.axis_size("clique")
    if members != 4:
        return [own] + [exchange(own, "clique", k) for k in range(1, members)]
    one, two = exchange(own, "clique", 1), exchange(own, "clique", 2)
    middle = own.shape[0] // 2
    top = exchange(two[:middle], "clique", 1)
    bottom = exchange(one[middle:], "clique", 2)
    return [own, one, two, top, bottom]


def on_device(
    out_grad, pre_act, batch_count, layer_two, hot_slots, cold_index, hot_feats, cold_feats
):
    n_clique = lax.axis_size("clique")
    shard_rows, d_in = hot_feats.shape
    d_h = pre_act.shape[1]
    cold_rows = cold_feats.shape[0]
    fanout = hot_slots.shape[1] + cold_index.shape[1]
    copy_at = lax.axis_index("copy")
    place = jnp.stack([lax.axis_index("clique"), copy_at & 1]).astype(jnp.int32)

    words, half_feats = start(place, hot_slots.T, hot_feats, shard_rows * n_clique)
    feats = gather_feats(half_feats)
    row_grad, own_two, twin_two = row_gradients(place, batch_count, out_grad, pre_act, layer_two)
    fetched_two = exchange(twin_two, "copy", 1)
    send, keep, words = hot_sums(words, row_grad, cold_index.T, cold_rows, fanout)
    other = exchange(send, "copy", 1)
    cold = cold_grad(words, row_grad, cold_feats, fanout)
    own_one, twin_one, two = join(place, cold, keep, other, own_two, fetched_two, feats)
    shares = pair_sums(place, own_one, exchange(twin_one, "copy", 1), two, n_clique)
    shares = sum_over_slice(shares)
    middle = n_clique // 2
    shares = [shares[turn] for turn in laid_turns(n_clique)]
    parts = [jnp.concatenate(part, axis=0) for part in (shares[:middle], shares[middle:])]
    others = [exchange(part, "copy", 1) for part in parts]
    rows_of = (d_in, d_h)
    own = lay(place, parts, n_clique, rows_of)
    return tuple(lay(place, others, n_clique, rows_of, own))


def solution(mesh):
    placed = (
        P(("clique", "copy"), None),
        P(("clique", "copy"), None),
        P(("clique", "copy")),
        P(),
        P(("clique", "copy"), None),
        P(("clique", "copy"), None),
        P("clique", None),
        P(("clique", "copy"), None),
    )
    return jax.shard_map(
        on_device, mesh=mesh, in_specs=placed, out_specs=(P(), P()), check_vma=False
    )
```

```python
import functools

import jax
import jax.numpy as jnp
from jax import lax
from jax.experimental import pallas as pl
from jax.experimental.pallas import tpu as pltpu
from jax.sharding import PartitionSpec as P

F32 = jnp.float32
BF16 = jnp.bfloat16
I16 = jnp.int16
FIELDS = 4
TILE = 16
HALF_MIB = 60
ROWS_MIB = 48


def whole():
    return pl.BlockSpec(memory_space=pltpu.VMEM)


def scalars():
    return pl.BlockSpec(memory_space=pltpu.SMEM)


def in_place():
    return pl.BlockSpec(memory_space=pl.ANY)


def params(mebibytes):
    return pltpu.CompilerParams(vmem_limit_bytes=mebibytes << 20)


def cost(flops, moved):
    return pl.CostEstimate(flops=int(flops), bytes_accessed=int(moved), transcendentals=0)


def transposed_dot(left, right):
    return lax.dot_general(left, right, (((0,), (0,)), ((), ())), preferred_element_type=F32)


def half_kernel(place_ref, feats_hbm, half_hbm, sem):
    rows = half_hbm.shape[0]
    here = pl.ds(pl.multiple_of(place_ref[1] * rows, TILE), rows)
    copy = pltpu.make_async_copy(feats_hbm.at[here, :], half_hbm, sem)
    copy.start()
    copy.wait()


def half_of(place, feats):
    rows, d_in = feats.shape
    return pl.pallas_call(
        half_kernel,
        in_specs=[scalars(), in_place()],
        out_specs=in_place(),
        out_shape=jax.ShapeDtypeStruct((rows // 2, d_in), BF16),
        scratch_shapes=[pltpu.SemaphoreType.DMA],
        compiler_params=params(HALF_MIB),
        cost_estimate=cost(10**10, 10**8),
        name="half_of",
    )(place, feats)


def halves(total_ref, own_ref, send_ref, own_shard, own_core, members):
    wide = own_ref.shape[1]
    mine = pl.ds(pl.multiple_of(own_core * wide, wide), wide)
    twin = pl.ds(pl.multiple_of((1 - own_core) * wide, wide), wide)
    rows = own_ref.shape[0] // members
    for member in range(members):
        here = slice(member * rows, (member + 1) * rows)
        there = pl.ds(pl.multiple_of((member ^ own_shard) * rows, TILE), rows)
        own_ref[there, :] = total_ref[here, mine].astype(BF16)
        send_ref[there, :] = total_ref[here, twin].astype(BF16)


def build_words(index, q_rows, store):
    terms = index.shape[0]
    shift = q_rows.bit_length() - 1
    low = index & (q_rows - 1)
    one = jnp.left_shift(jnp.ones_like(index), (index >> shift) * 4)
    unit = one
    for other in range(1, terms):
        turned_low = jnp.concatenate([low[other:], low[:other]], axis=0)
        turned = jnp.concatenate([one[other:], one[:other]], axis=0)
        unit = unit + jnp.where(turned_low == low, turned, jnp.zeros_like(turned))
    tall = min(256, q_rows) // TILE
    shape = (tall, TILE, 128)
    place = lax.broadcasted_iota(jnp.int32, shape, 0) * TILE + lax.broadcasted_iota(jnp.int32, shape, 1)
    place = place.astype(I16)

    def tile(row):
        return jnp.broadcast_to(row, (TILE, 128)).astype(I16)[None]

    lows = [tile(low[k : k + 1, :]) for k in range(terms)]
    units = [tile(unit[k : k + 1, :]) for k in range(terms)]
    for top in range(0, q_rows // TILE, tall):
        word = jnp.zeros(shape, I16)
        for k in range(terms):
            word = jnp.where(place == lows[k] - I16(top * TILE), units[k], word)
        store(top, tall, word)


def unpack(word_ref, field, count_ref):
    if field < FIELDS - 1:
        counts = word_ref[...] & (15 << (4 * field))
    else:
        counts = (word_ref[...] >> (4 * field)) & 15
    count_ref[...] = counts.astype(BF16).reshape(count_ref.shape)


def unpacked_scale(field):
    return 16.0**field if field < FIELDS - 1 else 1.0


def rows_kernel(
    shard_bits, half_rows, chunks, members,
    place_ref, count_ref, index_ref, out_grad_hbm, pre_act_hbm, layer_two_hbm,
    row_grad_ref, own_ref, send_ref, word_ref,
    out_grad_ref, pre_act_ref, layer_two_ref, sum_ref, sems,
):
    rows = out_grad_ref.shape[0] // chunks
    blocks = [slice(chunk * rows, (chunk + 1) * rows) for chunk in range(chunks)]
    fetch_layer = pltpu.make_async_copy(layer_two_hbm, layer_two_ref, sems.at[2 * chunks])
    fetches = []
    for chunk, block in enumerate(blocks):
        pair = []
        for at, (source, target) in enumerate(((out_grad_hbm, out_grad_ref), (pre_act_hbm, pre_act_ref))):
            fetch = pltpu.make_async_copy(
                source.at[block, :], target.at[block, :], sems.at[2 * chunk + at]
            )
            fetch.start()
            pair.append(fetch)
        fetches.append(pair)
        if chunk == 0:
            fetch_layer.start()

    own_shard, own_core = place_ref[0], place_ref[1]
    part_bits = shard_bits - 1

    def build(tile):
        lanes = slice(tile * 128, (tile + 1) * 128)
        index = index_ref[:, lanes]
        row = index & ((1 << part_bits) - 1)
        half = ((index >> part_bits) & 1) ^ own_core ^ 1
        index = half * half_rows + (((index >> shard_bits) ^ own_shard) << part_bits) + row

        def store(top, tall, words):
            word_ref[top : top + tall, :, lanes] = words

        build_words(index, word_ref.shape[0] * TILE, store)

    tiles = row_grad_ref.shape[0] // 128
    first = tiles // 4
    for tile in range(first):
        build(tile)
    ends = [first + (tiles - first) * chunk // chunks for chunk in range(chunks + 1)]
    for chunk, block in enumerate(blocks):
        for fetch in fetches[chunk]:
            fetch.wait()
        if chunk == 0:
            fetch_layer.wait()
        live = count_ref[0] - chunk * rows

        @pl.when(live < rows)
        def _(block=block, live=live):
            out_grad = out_grad_ref[block, :].astype(F32)
            place = lax.broadcasted_iota(jnp.int32, out_grad.shape, 0)
            masked = jnp.where(place < live, out_grad, jnp.zeros_like(out_grad))
            out_grad_ref[block, :] = masked.astype(BF16)

        masked = out_grad_ref[block, :]
        pre_act = pre_act_ref[block, :]
        back = lax.dot_general(
            masked, layer_two_ref[...], (((1,), (1,)), ((), ())), preferred_element_type=F32
        )
        row_grad_ref[block, :] = jnp.where(
            pre_act.astype(F32) > 0, back, jnp.zeros_like(back)
        ).astype(BF16)
        activ = jnp.maximum(pre_act, jnp.zeros_like(pre_act))
        part = transposed_dot(activ, masked)
        sum_ref[...] = part if chunk == 0 else sum_ref[...] + part
        for tile in range(ends[chunk], ends[chunk + 1]):
            build(tile)
    halves(sum_ref, own_ref, send_ref, own_shard, own_core, members)


def row_gradients(place, batch_count, out_grad, pre_act, layer_two, index, hot_total, shard_rows):
    rows, d_out = out_grad.shape
    d_h = pre_act.shape[1]
    chunks = 4
    deep = hot_total // FIELDS // TILE
    half = jax.ShapeDtypeStruct((d_h, d_out // 2), BF16)
    return pl.pallas_call(
        functools.partial(
            rows_kernel,
            shard_rows.bit_length() - 1,
            hot_total // 2,
            chunks,
            hot_total // shard_rows,
        ),
        in_specs=[scalars(), scalars(), whole()] + [pl.BlockSpec(memory_space=pltpu.HBM)] * 3,
        out_specs=[whole()] * 4,
        out_shape=[
            jax.ShapeDtypeStruct((rows, d_h), BF16),
            half,
            half,
            jax.ShapeDtypeStruct((deep, TILE, rows), I16),
        ],
        scratch_shapes=[
            pltpu.VMEM((rows, d_out), BF16),
            pltpu.VMEM((rows, d_h), BF16),
            pltpu.VMEM((d_h, d_out), BF16),
            pltpu.VMEM((d_h, d_out), F32),
            pltpu.SemaphoreType.DMA((2 * chunks + 1,)),
        ],
        compiler_params=params(ROWS_MIB),
        cost_estimate=cost(10**10, 10**8),
        name="row_gradients",
    )(place, batch_count, index, out_grad, pre_act, layer_two)


def hot_kernel(
    scale, word_ref, row_grad_ref, index_ref, send_ref, keep_ref, cold_word_ref, *counts
):
    tall, rows = counts[0].shape
    tiles = rows // 128 // FIELDS
    unpack(word_ref, 0, counts[0])
    for field in range(FIELDS):
        found = jnp.dot(counts[field % 2][...], row_grad_ref[...], preferred_element_type=F32)
        out_ref = (send_ref, keep_ref)[field // 2]
        out_ref[field % 2 * tall : (field % 2 + 1) * tall, :] = (
            found * (scale / unpacked_scale(field))
        ).astype(BF16)
        if field + 1 < FIELDS:
            unpack(word_ref, field + 1, counts[(field + 1) % 2])
        for tile in range(field * tiles, (field + 1) * tiles):
            lanes = slice(tile * 128, (tile + 1) * 128)

            def store(top, deep, words, lanes=lanes):
                cold_word_ref[top : top + deep, :, lanes] = words

            build_words(index_ref[:, lanes], cold_word_ref.shape[0] * TILE, store)


def hot_sums(words, row_grad, cold_index, cold_rows, fanout):
    rows, d_h = row_grad.shape
    q_rows = words.shape[0] * TILE
    half = jax.ShapeDtypeStruct((q_rows * FIELDS // 2, d_h), BF16)
    return pl.pallas_call(
        functools.partial(hot_kernel, 1.0 / fanout),
        in_specs=[whole(), whole(), whole()],
        out_specs=[whole()] * 3,
        out_shape=[
            half,
            half,
            jax.ShapeDtypeStruct((cold_rows // FIELDS // TILE, TILE, rows), I16),
        ],
        scratch_shapes=[pltpu.VMEM((q_rows, rows), BF16)] * 2,
        compiler_params=params(40),
        cost_estimate=cost(10**10, 10**8),
        name="hot_sums",
    )(words, row_grad, cold_index)


def cold_kernel(scale, word_ref, row_grad_ref, feats_ref, grad_ref, sums_ref, held_ref, sem, *counts):
    fetch = pltpu.make_async_copy(feats_ref, held_ref, sem)
    fetch.start()
    tall = counts[0].shape[0]

    def add_product(field):
        rows = slice(field * tall, (field + 1) * tall)
        part = transposed_dot(held_ref[rows, :], sums_ref[rows, :])
        grad_ref[...] = part if field == 0 else grad_ref[...] + part

    unpack(word_ref, 0, counts[0])
    for field in range(FIELDS):
        found = jnp.dot(counts[field % 2][...], row_grad_ref[...], preferred_element_type=F32)
        sums_ref[field * tall : (field + 1) * tall, :] = (
            found * (scale / unpacked_scale(field))
        ).astype(BF16)
        if field + 1 < FIELDS:
            unpack(word_ref, field + 1, counts[(field + 1) % 2])
        if field == 1:
            fetch.wait()
        if field > 0:
            add_product(field - 1)
    add_product(FIELDS - 1)


def cold_grad(words, row_grad, feats, fanout):
    rows, d_h = row_grad.shape
    cold_rows, d_in = feats.shape
    q_rows = cold_rows // FIELDS
    return pl.pallas_call(
        functools.partial(cold_kernel, 1.0 / fanout),
        in_specs=[whole(), whole(), in_place()],
        out_specs=whole(),
        out_shape=jax.ShapeDtypeStruct((d_in, d_h), F32),
        scratch_shapes=[
            pltpu.VMEM((cold_rows, d_h), BF16),
            pltpu.VMEM((cold_rows, d_in), BF16),
            pltpu.SemaphoreType.DMA,
            pltpu.VMEM((q_rows, rows), BF16),
            pltpu.VMEM((q_rows, rows), BF16),
        ],
        compiler_params=params(40),
        cost_estimate=cost(10**10, 10**8),
        name="cold_grad",
    )(words, row_grad, feats)


def join_kernel(parts, place_ref, cold_ref, keep_ref, other_ref, *rest):
    feats, (own_ref, send_ref) = rest[:parts], rest[parts:]
    own_core = place_ref[1]
    d_in, d_h = cold_ref.shape
    wide = d_h // 2
    sums = (keep_ref[...].astype(F32) + other_ref[...].astype(F32)).astype(BF16)
    for left in range(0, d_in, 256):
        rows = slice(left, left + 256)
        part = jnp.concatenate([part[:, rows] for part in feats], axis=0)
        total = (cold_ref[rows, :] + transposed_dot(part, sums)).astype(BF16)
        first, second = total[:, :wide], total[:, wide:]

        @pl.when(own_core == 0)
        def _(rows=rows, first=first, second=second):
            own_ref[rows, :] = first
            send_ref[rows, :] = second

        @pl.when(own_core == 1)
        def _(rows=rows, first=first, second=second):
            own_ref[rows, :] = second
            send_ref[rows, :] = first


def join(place, cold, keep, other, feats):
    d_in, d_h = cold.shape
    half = jax.ShapeDtypeStruct((d_in, d_h // 2), BF16)
    return pl.pallas_call(
        functools.partial(join_kernel, len(feats)),
        in_specs=[scalars()] + [whole()] * (3 + len(feats)),
        out_specs=[whole()] * 2,
        out_shape=[half, half],
        compiler_params=params(32),
        cost_estimate=cost(2 * keep.shape[0] * d_h * d_in, 4 * d_in * d_h),
        name="join",
    )(place, cold, keep, other, *feats)


def share_rows(rows, members, place_ref, core, turn):
    size = rows // members
    partner = turn
    if members == 4 and turn == 1:
        partner = 3
    elif members == 4 and turn > 1:
        partner = jnp.where(core == 0, turn - 1, 4 - turn)
    return pl.ds(pl.multiple_of((place_ref[0] ^ partner) * size, TILE), size)


def pair_kernel(place_ref, one_ref, other_ref, *out_refs):
    members = len(out_refs)
    for k, out_ref in enumerate(out_refs):
        here = share_rows(one_ref.shape[0], members, place_ref, place_ref[1], k)
        total = one_ref[here, :].astype(F32) + other_ref[here, :].astype(F32)
        out_ref[...] = total.astype(BF16)


def pair_sums(place, one, other, members):
    rows, wide = one.shape
    share = jax.ShapeDtypeStruct((rows // members, wide), BF16)
    return pl.pallas_call(
        pair_kernel,
        in_specs=[scalars()] + [whole()] * 2,
        out_specs=[whole()] * members,
        out_shape=[share] * members,
        compiler_params=params(16),
        cost_estimate=cost(0, 6 * rows * wide),
        name="pair_sums",
    )(place, one, other)


def laid_turns(members):
    return [0, members - 1, *range(1, members - 1)]


def lay_kernel(members, parts, twin, place_ref, *refs):
    halves_in, refs = refs[:parts], refs[parts:]
    refs = refs[2:] if twin else refs
    outs, held, sems = refs[:2], refs[2:4], refs[4]
    core = 1 - place_ref[1] if twin else place_ref[1]
    wide = halves_in[0].shape[1]
    lanes = pl.ds(pl.multiple_of(core * wide, wide), wide)
    each = members // parts
    copies = []
    for k, turn in enumerate(laid_turns(members)):
        base = k % each * (halves_in[0].shape[0] // each)
        for at, (out_ref, held_ref) in enumerate(zip(outs, held)):
            here = share_rows(out_ref.shape[0], members, place_ref, core, turn)
            held_ref[here, :] = halves_in[k // each][base : base + here.size, :].astype(F32)
            copy = pltpu.make_async_copy(
                held_ref.at[here, :], out_ref.at[here, lanes], sems.at[2 * k + at]
            )
            copy.start()
            copies.append(copy)
            base += here.size
    for copy in copies:
        copy.wait()


def lay(place, parts, members, rows_of, before=()):
    wide = parts[0].shape[1]
    count = 1 + len(parts)
    return pl.pallas_call(
        functools.partial(lay_kernel, members, len(parts), bool(before)),
        in_specs=[scalars()] + [whole()] * len(parts) + [in_place()] * len(before),
        out_specs=[in_place()] * len(rows_of),
        out_shape=[jax.ShapeDtypeStruct((rows, 2 * wide), F32) for rows in rows_of],
        input_output_aliases={count + at: at for at in range(len(before))},
        scratch_shapes=[pltpu.VMEM((rows, wide), F32) for rows in rows_of]
        + [pltpu.SemaphoreType.DMA((2 * members,))],
        compiler_params=params(16),
        cost_estimate=cost(10**10, 10**8),
        name="lay",
    )(place, *parts, *before)


def exchange(array, axis, step):
    size = lax.axis_size(axis)
    return lax.ppermute(array, axis, [(source, source ^ step) for source in range(size)])


def added(*arrays):
    total = arrays[0].astype(F32)
    for array in arrays[1:]:
        total = total + array.astype(F32)
    return total.astype(BF16)


def route_of(n_clique, n_copy, turn):
    moves = [(0, 0), (3, 3), (1, 2), (2, 1)][turn] if n_clique == 4 else (turn, turn)
    return [
        (i * n_copy + j, (i ^ moves[j & 1]) * n_copy + j)
        for i in range(n_clique)
        for j in range(n_copy)
    ]


def trade(arrays):
    n_clique, n_copy = lax.axis_size("clique"), lax.axis_size("copy")
    return [arrays[0]] + [
        lax.ppermute(arrays[turn], ("clique", "copy"), route_of(n_clique, n_copy, turn))
        for turn in range(1, n_clique)
    ]


def sum_over_slice(shares, two):
    own = jnp.concatenate([added(*trade(shares)), two], axis=0)
    n_copy = lax.axis_size("copy")
    steps = [2 << bit for bit in range((n_copy // 2).bit_length() - 1)]
    for near, far in zip(steps, reversed(steps)):
        route = [(j, j ^ (far if j & 1 else near)) for j in range(n_copy)]
        own = added(own, lax.ppermute(own, "copy", route))
    return trade([own] * len(shares))


def gather(own, two):
    members = lax.axis_size("clique")
    rows = two.shape[0] // members
    shares = [two[k * rows : (k + 1) * rows] for k in range(members)]
    middle, d_in = own.shape[0] // 2, own.shape[1]
    if members != 4 or rows != middle:
        feats = [own] + [exchange(own, "clique", k) for k in range(1, members)]
        got = shares[:1] + [exchange(shares[k], "clique", k) for k in range(1, members)]
        return feats, added(*got)
    one, other = exchange(own, "clique", 1), exchange(own, "clique", 2)
    top = exchange(jnp.concatenate([other[:middle], shares[1]], axis=1), "clique", 1)
    bottom = exchange(jnp.concatenate([one[middle:], shares[2]], axis=1), "clique", 2)
    far = exchange(shares[3], "clique", 3)
    total = added(shares[0], top[:, d_in:], bottom[:, d_in:], far)
    return [own, one, other, top, bottom], total


def on_device(
    out_grad, pre_act, batch_count, layer_two, hot_slots, cold_index, hot_feats, cold_feats
):
    n_clique = lax.axis_size("clique")
    shard_rows, d_in = hot_feats.shape
    d_h = pre_act.shape[1]
    cold_rows = cold_feats.shape[0]
    fanout = hot_slots.shape[1] + cold_index.shape[1]
    copy_at = lax.axis_index("copy")
    place = jnp.stack([lax.axis_index("clique"), copy_at & 1]).astype(jnp.int32)

    half_feats = half_of(place, hot_feats)
    row_grad, own_two, twin_two, words = row_gradients(
        place, batch_count, out_grad, pre_act, layer_two, hot_slots.T, shard_rows * n_clique, shard_rows
    )
    two = added(own_two, exchange(twin_two, "copy", 1))
    feats, two = gather(half_feats, two)
    send, keep, words = hot_sums(words, row_grad, cold_index.T, cold_rows, fanout)
    other = exchange(send, "copy", 1)
    cold = cold_grad(words, row_grad, cold_feats, fanout)
    own_one, twin_one = join(place, cold, keep, other, feats)
    shares = pair_sums(place, own_one, exchange(twin_one, "copy", 1), n_clique)
    shares = sum_over_slice(shares, two)
    middle = n_clique // 2
    shares = [shares[turn] for turn in laid_turns(n_clique)]
    parts = [jnp.concatenate(part, axis=0) for part in (shares[:middle], shares[middle:])]
    others = [exchange(part, "copy", 1) for part in parts]
    rows_of = (d_in, d_h)
    own = lay(place, parts, n_clique, rows_of)
    return tuple(lay(place, others, n_clique, rows_of, own))


def solution(mesh):
    placed = (
        P(("clique", "copy"), None),
        P(("clique", "copy"), None),
        P(("clique", "copy")),
        P(),
        P(("clique", "copy"), None),
        P(("clique", "copy"), None),
        P("clique", None),
        P(("clique", "copy"), None),
    )
    return jax.shard_map(
        on_device, mesh=mesh, in_specs=placed, out_specs=(P(), P()), check_vma=False
    )
```

```python
import functools

import jax
import jax.numpy as jnp
from jax import lax
from jax.experimental import pallas as pl
from jax.experimental.pallas import tpu as pltpu
from jax.sharding import PartitionSpec as P

F32 = jnp.float32
BF16 = jnp.bfloat16
I16 = jnp.int16
FIELDS = 4
TILE = 16
HALF_MIB = 60
ROWS_MIB = 48


def whole():
    return pl.BlockSpec(memory_space=pltpu.VMEM)


def scalars():
    return pl.BlockSpec(memory_space=pltpu.SMEM)


def in_place():
    return pl.BlockSpec(memory_space=pl.ANY)


def params(mebibytes):
    return pltpu.CompilerParams(vmem_limit_bytes=mebibytes << 20)


def cost(flops, moved):
    return pl.CostEstimate(flops=int(flops), bytes_accessed=int(moved), transcendentals=0)


def transposed_dot(left, right):
    return lax.dot_general(left, right, (((0,), (0,)), ((), ())), preferred_element_type=F32)


def half_kernel(place_ref, feats_ref, half_ref, sem):
    rows = half_ref.shape[0]
    here = pl.ds(pl.multiple_of(place_ref[1] * rows, TILE), rows)
    copy = pltpu.make_async_copy(feats_ref.at[here, :], half_ref, sem)
    copy.start()
    copy.wait()


def half_of(place, feats):
    rows, d_in = feats.shape
    return pl.pallas_call(
        half_kernel,
        in_specs=[scalars(), in_place()],
        out_specs=whole(),
        out_shape=jax.ShapeDtypeStruct((rows // 2, d_in), BF16),
        scratch_shapes=[pltpu.SemaphoreType.DMA],
        compiler_params=params(HALF_MIB),
        cost_estimate=cost(10**10, 10**8),
        name="half_of",
    )(place, feats)


def halves(total_ref, own_ref, send_ref, own_shard, own_core, members):
    wide = own_ref.shape[1]
    mine = pl.ds(pl.multiple_of(own_core * wide, wide), wide)
    twin = pl.ds(pl.multiple_of((1 - own_core) * wide, wide), wide)
    rows = own_ref.shape[0] // members
    for member in range(members):
        here = slice(member * rows, (member + 1) * rows)
        there = pl.ds(pl.multiple_of((member ^ own_shard) * rows, TILE), rows)
        own_ref[there, :] = total_ref[here, mine].astype(BF16)
        send_ref[there, :] = total_ref[here, twin].astype(BF16)


def build_words(index, q_rows, store):
    terms = index.shape[0]
    shift = q_rows.bit_length() - 1
    low = index & (q_rows - 1)
    one = jnp.left_shift(jnp.ones_like(index), (index >> shift) * 4)
    unit = one
    for other in range(1, terms):
        turned_low = jnp.concatenate([low[other:], low[:other]], axis=0)
        turned = jnp.concatenate([one[other:], one[:other]], axis=0)
        unit = unit + jnp.where(turned_low == low, turned, jnp.zeros_like(turned))
    tall = min(256, q_rows) // TILE
    shape = (tall, TILE, 128)
    place = lax.broadcasted_iota(jnp.int32, shape, 0) * TILE + lax.broadcasted_iota(jnp.int32, shape, 1)
    place = place.astype(I16)

    def tile(row):
        return jnp.broadcast_to(row, (TILE, 128)).astype(I16)[None]

    lows = [tile(low[k : k + 1, :]) for k in range(terms)]
    units = [tile(unit[k : k + 1, :]) for k in range(terms)]
    for top in range(0, q_rows // TILE, tall):
        word = jnp.zeros(shape, I16)
        for k in range(terms):
            word = jnp.where(place == lows[k] - I16(top * TILE), units[k], word)
        store(top, tall, word)


def unpack(word_ref, field, count_ref):
    if field < FIELDS - 1:
        counts = word_ref[...] & (15 << (4 * field))
    else:
        counts = (word_ref[...] >> (4 * field)) & 15
    count_ref[...] = counts.astype(BF16).reshape(count_ref.shape)


def unpacked_scale(field):
    return 16.0**field if field < FIELDS - 1 else 1.0


def rows_kernel(
    shard_bits, half_rows, chunks, members,
    place_ref, count_ref, index_ref, out_grad_hbm, pre_act_hbm, layer_two_hbm,
    row_grad_ref, own_ref, send_ref, word_ref,
    out_grad_ref, pre_act_ref, layer_two_ref, sum_ref, sems,
):
    rows = out_grad_ref.shape[0] // chunks
    blocks = [slice(chunk * rows, (chunk + 1) * rows) for chunk in range(chunks)]
    fetch_layer = pltpu.make_async_copy(layer_two_hbm, layer_two_ref, sems.at[2 * chunks])
    fetches = []
    for chunk, block in enumerate(blocks):
        pair = []
        for at, (source, target) in enumerate(((out_grad_hbm, out_grad_ref), (pre_act_hbm, pre_act_ref))):
            fetch = pltpu.make_async_copy(
                source.at[block, :], target.at[block, :], sems.at[2 * chunk + at]
            )
            fetch.start()
            pair.append(fetch)
        fetches.append(pair)
        if chunk == 0:
            fetch_layer.start()

    own_shard, own_core = place_ref[0], place_ref[1]
    part_bits = shard_bits - 1

    def build(tile):
        lanes = slice(tile * 128, (tile + 1) * 128)
        index = index_ref[:, lanes]
        row = index & ((1 << part_bits) - 1)
        half = ((index >> part_bits) & 1) ^ own_core ^ 1
        index = half * half_rows + (((index >> shard_bits) ^ own_shard) << part_bits) + row

        def store(top, tall, words):
            word_ref[top : top + tall, :, lanes] = words

        build_words(index, word_ref.shape[0] * TILE, store)

    tiles = row_grad_ref.shape[0] // 128
    first = tiles // 4
    for tile in range(first):
        build(tile)
    ends = [first + (tiles - first) * chunk // chunks for chunk in range(chunks + 1)]
    for chunk, block in enumerate(blocks):
        for fetch in fetches[chunk]:
            fetch.wait()
        if chunk == 0:
            fetch_layer.wait()
        live = count_ref[0] - chunk * rows

        @pl.when(live < rows)
        def _(block=block, live=live):
            out_grad = out_grad_ref[block, :].astype(F32)
            place = lax.broadcasted_iota(jnp.int32, out_grad.shape, 0)
            masked = jnp.where(place < live, out_grad, jnp.zeros_like(out_grad))
            out_grad_ref[block, :] = masked.astype(BF16)

        masked = out_grad_ref[block, :]
        pre_act = pre_act_ref[block, :]
        back = lax.dot_general(
            masked, layer_two_ref[...], (((1,), (1,)), ((), ())), preferred_element_type=F32
        )
        row_grad_ref[block, :] = jnp.where(
            pre_act.astype(F32) > 0, back, jnp.zeros_like(back)
        ).astype(BF16)
        activ = jnp.maximum(pre_act, jnp.zeros_like(pre_act))
        part = transposed_dot(activ, masked)
        sum_ref[...] = part if chunk == 0 else sum_ref[...] + part
        for tile in range(ends[chunk], ends[chunk + 1]):
            build(tile)
    halves(sum_ref, own_ref, send_ref, own_shard, own_core, members)


def row_gradients(place, batch_count, out_grad, pre_act, layer_two, index, hot_total, shard_rows):
    rows, d_out = out_grad.shape
    d_h = pre_act.shape[1]
    chunks = 4
    deep = hot_total // FIELDS // TILE
    half = jax.ShapeDtypeStruct((d_h, d_out // 2), BF16)
    return pl.pallas_call(
        functools.partial(
            rows_kernel,
            shard_rows.bit_length() - 1,
            hot_total // 2,
            chunks,
            hot_total // shard_rows,
        ),
        in_specs=[scalars(), scalars(), whole()] + [pl.BlockSpec(memory_space=pltpu.HBM)] * 3,
        out_specs=[whole()] * 4,
        out_shape=[
            jax.ShapeDtypeStruct((rows, d_h), BF16),
            half,
            half,
            jax.ShapeDtypeStruct((deep, TILE, rows), I16),
        ],
        scratch_shapes=[
            pltpu.VMEM((rows, d_out), BF16),
            pltpu.VMEM((rows, d_h), BF16),
            pltpu.VMEM((d_h, d_out), BF16),
            pltpu.VMEM((d_h, d_out), F32),
            pltpu.SemaphoreType.DMA((2 * chunks + 1,)),
        ],
        compiler_params=params(ROWS_MIB),
        cost_estimate=cost(10**10, 10**8),
        name="row_gradients",
    )(place, batch_count, index, out_grad, pre_act, layer_two)


def hot_kernel(
    scale, word_ref, row_grad_ref, index_ref, send_ref, keep_ref, cold_word_ref, *counts
):
    tall, rows = counts[0].shape
    tiles = rows // 128 // FIELDS
    unpack(word_ref, 0, counts[0])
    for field in range(FIELDS):
        found = jnp.dot(counts[field % 2][...], row_grad_ref[...], preferred_element_type=F32)
        out_ref = (send_ref, keep_ref)[field // 2]
        out_ref[field % 2 * tall : (field % 2 + 1) * tall, :] = (
            found * (scale / unpacked_scale(field))
        ).astype(BF16)
        if field + 1 < FIELDS:
            unpack(word_ref, field + 1, counts[(field + 1) % 2])
        for tile in range(field * tiles, (field + 1) * tiles):
            lanes = slice(tile * 128, (tile + 1) * 128)

            def store(top, deep, words, lanes=lanes):
                cold_word_ref[top : top + deep, :, lanes] = words

            build_words(index_ref[:, lanes], cold_word_ref.shape[0] * TILE, store)


def hot_sums(words, row_grad, cold_index, cold_rows, fanout):
    rows, d_h = row_grad.shape
    q_rows = words.shape[0] * TILE
    half = jax.ShapeDtypeStruct((q_rows * FIELDS // 2, d_h), BF16)
    return pl.pallas_call(
        functools.partial(hot_kernel, 1.0 / fanout),
        in_specs=[whole(), whole(), whole()],
        out_specs=[whole()] * 3,
        out_shape=[
            half,
            half,
            jax.ShapeDtypeStruct((cold_rows // FIELDS // TILE, TILE, rows), I16),
        ],
        scratch_shapes=[pltpu.VMEM((q_rows, rows), BF16)] * 2,
        compiler_params=params(40),
        cost_estimate=cost(10**10, 10**8),
        name="hot_sums",
    )(words, row_grad, cold_index)


def cold_kernel(scale, word_ref, row_grad_ref, feats_ref, grad_ref, sums_ref, held_ref, sem, *counts):
    fetch = pltpu.make_async_copy(feats_ref, held_ref, sem)
    fetch.start()
    tall = counts[0].shape[0]

    def add_product(field):
        rows = slice(field * tall, (field + 1) * tall)
        part = transposed_dot(held_ref[rows, :], sums_ref[rows, :])
        grad_ref[...] = part if field == 0 else grad_ref[...] + part

    unpack(word_ref, 0, counts[0])
    for field in range(FIELDS):
        found = jnp.dot(counts[field % 2][...], row_grad_ref[...], preferred_element_type=F32)
        sums_ref[field * tall : (field + 1) * tall, :] = (
            found * (scale / unpacked_scale(field))
        ).astype(BF16)
        if field + 1 < FIELDS:
            unpack(word_ref, field + 1, counts[(field + 1) % 2])
        if field == 1:
            fetch.wait()
        if field > 0:
            add_product(field - 1)
    add_product(FIELDS - 1)


def cold_grad(words, row_grad, feats, fanout):
    rows, d_h = row_grad.shape
    cold_rows, d_in = feats.shape
    q_rows = cold_rows // FIELDS
    return pl.pallas_call(
        functools.partial(cold_kernel, 1.0 / fanout),
        in_specs=[whole(), whole(), in_place()],
        out_specs=whole(),
        out_shape=jax.ShapeDtypeStruct((d_in, d_h), F32),
        scratch_shapes=[
            pltpu.VMEM((cold_rows, d_h), BF16),
            pltpu.VMEM((cold_rows, d_in), BF16),
            pltpu.SemaphoreType.DMA,
            pltpu.VMEM((q_rows, rows), BF16),
            pltpu.VMEM((q_rows, rows), BF16),
        ],
        compiler_params=params(40),
        cost_estimate=cost(10**10, 10**8),
        name="cold_grad",
    )(words, row_grad, feats)


def join_kernel(parts, place_ref, cold_ref, keep_ref, other_ref, *rest):
    feats, (own_ref, send_ref) = rest[:parts], rest[parts:]
    own_core = place_ref[1]
    d_in, d_h = cold_ref.shape
    wide = d_h // 2
    sums = (keep_ref[...].astype(F32) + other_ref[...].astype(F32)).astype(BF16)
    for left in range(0, d_in, 256):
        rows = slice(left, left + 256)
        part = jnp.concatenate([part[:, rows] for part in feats], axis=0)
        total = (cold_ref[rows, :] + transposed_dot(part, sums)).astype(BF16)
        first, second = total[:, :wide], total[:, wide:]

        @pl.when(own_core == 0)
        def _(rows=rows, first=first, second=second):
            own_ref[rows, :] = first
            send_ref[rows, :] = second

        @pl.when(own_core == 1)
        def _(rows=rows, first=first, second=second):
            own_ref[rows, :] = second
            send_ref[rows, :] = first


def join(place, cold, keep, other, feats):
    d_in, d_h = cold.shape
    half = jax.ShapeDtypeStruct((d_in, d_h // 2), BF16)
    return pl.pallas_call(
        functools.partial(join_kernel, len(feats)),
        in_specs=[scalars()] + [whole()] * (3 + len(feats)),
        out_specs=[whole()] * 2,
        out_shape=[half, half],
        compiler_params=params(32),
        cost_estimate=cost(2 * keep.shape[0] * d_h * d_in, 4 * d_in * d_h),
        name="join",
    )(place, cold, keep, other, *feats)


def share_rows(rows, members, place_ref, core, turn):
    size = rows // members
    partner = turn
    if members == 4 and turn == 1:
        partner = 3
    elif members == 4 and turn > 1:
        partner = jnp.where(core == 0, turn - 1, 4 - turn)
    return pl.ds(pl.multiple_of((place_ref[0] ^ partner) * size, TILE), size)


def pair_kernel(place_ref, one_ref, other_ref, *out_refs):
    members = len(out_refs)
    for k, out_ref in enumerate(out_refs):
        here = share_rows(one_ref.shape[0], members, place_ref, place_ref[1], k)
        total = one_ref[here, :].astype(F32) + other_ref[here, :].astype(F32)
        out_ref[...] = total.astype(BF16)


def pair_sums(place, one, other, members):
    rows, wide = one.shape
    share = jax.ShapeDtypeStruct((rows // members, wide), BF16)
    return pl.pallas_call(
        pair_kernel,
        in_specs=[scalars()] + [whole()] * 2,
        out_specs=[whole()] * members,
        out_shape=[share] * members,
        compiler_params=params(16),
        cost_estimate=cost(0, 6 * rows * wide),
        name="pair_sums",
    )(place, one, other)


def laid_turns(members):
    return [0, members - 1, *range(1, members - 1)]


def lay_kernel(members, parts, twin, place_ref, *refs):
    halves_in, refs = refs[:parts], refs[parts:]
    refs = refs[2:] if twin else refs
    outs, held, sems = refs[:2], refs[2:4], refs[4]
    core = 1 - place_ref[1] if twin else place_ref[1]
    wide = halves_in[0].shape[1]
    lanes = pl.ds(pl.multiple_of(core * wide, wide), wide)
    each = members // parts
    copies = []
    for k, turn in enumerate(laid_turns(members)):
        base = k % each * (halves_in[0].shape[0] // each)
        for at, (out_ref, held_ref) in enumerate(zip(outs, held)):
            here = share_rows(out_ref.shape[0], members, place_ref, core, turn)
            held_ref[here, :] = halves_in[k // each][base : base + here.size, :].astype(F32)
            copy = pltpu.make_async_copy(
                held_ref.at[here, :], out_ref.at[here, lanes], sems.at[2 * k + at]
            )
            copy.start()
            copies.append(copy)
            base += here.size
    for copy in copies:
        copy.wait()


def lay(place, parts, members, rows_of, before=()):
    wide = parts[0].shape[1]
    count = 1 + len(parts)
    return pl.pallas_call(
        functools.partial(lay_kernel, members, len(parts), bool(before)),
        in_specs=[scalars()] + [whole()] * len(parts) + [in_place()] * len(before),
        out_specs=[in_place()] * len(rows_of),
        out_shape=[jax.ShapeDtypeStruct((rows, 2 * wide), F32) for rows in rows_of],
        input_output_aliases={count + at: at for at in range(len(before))},
        scratch_shapes=[pltpu.VMEM((rows, wide), F32) for rows in rows_of]
        + [pltpu.SemaphoreType.DMA((2 * members,))],
        compiler_params=params(16),
        cost_estimate=cost(10**10, 10**8),
        name="lay",
    )(place, *parts, *before)


def exchange(array, axis, step):
    size = lax.axis_size(axis)
    return lax.ppermute(array, axis, [(source, source ^ step) for source in range(size)])


def added(*arrays):
    total = arrays[0].astype(F32)
    for array in arrays[1:]:
        total = total + array.astype(F32)
    return total.astype(BF16)


def route_of(n_clique, n_copy, turn):
    moves = [(0, 0), (3, 3), (1, 2), (2, 1)][turn] if n_clique == 4 else (turn, turn)
    return [
        (i * n_copy + j, (i ^ moves[j & 1]) * n_copy + j)
        for i in range(n_clique)
        for j in range(n_copy)
    ]


def trade(arrays):
    n_clique, n_copy = lax.axis_size("clique"), lax.axis_size("copy")
    return [arrays[0]] + [
        lax.ppermute(arrays[turn], ("clique", "copy"), route_of(n_clique, n_copy, turn))
        for turn in range(1, n_clique)
    ]


def sum_over_slice(shares, two):
    own = jnp.concatenate([added(*trade(shares)), two], axis=0)
    n_copy = lax.axis_size("copy")
    steps = [2 << bit for bit in range((n_copy // 2).bit_length() - 1)]
    for near, far in zip(steps, reversed(steps)):
        route = [(j, j ^ (far if j & 1 else near)) for j in range(n_copy)]
        own = added(own, lax.ppermute(own, "copy", route))
    return trade([own] * len(shares))


def gather(own, two):
    members = lax.axis_size("clique")
    rows = two.shape[0] // members
    shares = [two[k * rows : (k + 1) * rows] for k in range(members)]
    middle, d_in = own.shape[0] // 2, own.shape[1]
    if members != 4 or rows != middle:
        feats = [own] + [exchange(own, "clique", k) for k in range(1, members)]
        got = shares[:1] + [exchange(shares[k], "clique", k) for k in range(1, members)]
        return feats, added(*got)
    one, other = exchange(own, "clique", 1), exchange(own, "clique", 2)
    top = exchange(jnp.concatenate([other[:middle], shares[1]], axis=1), "clique", 1)
    bottom = exchange(jnp.concatenate([one[middle:], shares[2]], axis=1), "clique", 2)
    far = exchange(shares[3], "clique", 3)
    total = added(shares[0], top[:, d_in:], bottom[:, d_in:], far)
    return [own, one, other, top, bottom], total


def on_device(
    out_grad, pre_act, batch_count, layer_two, hot_slots, cold_index, hot_feats, cold_feats
):
    n_clique = lax.axis_size("clique")
    shard_rows, d_in = hot_feats.shape
    d_h = pre_act.shape[1]
    cold_rows = cold_feats.shape[0]
    fanout = hot_slots.shape[1] + cold_index.shape[1]
    copy_at = lax.axis_index("copy")
    place = jnp.stack([lax.axis_index("clique"), copy_at & 1]).astype(jnp.int32)

    half_feats = half_of(place, hot_feats)
    row_grad, own_two, twin_two, words = row_gradients(
        place, batch_count, out_grad, pre_act, layer_two, hot_slots.T, shard_rows * n_clique, shard_rows
    )
    two = added(own_two, exchange(twin_two, "copy", 1))
    feats, two = gather(half_feats, two)
    send, keep, words = hot_sums(words, row_grad, cold_index.T, cold_rows, fanout)
    other = exchange(send, "copy", 1)
    cold = cold_grad(words, row_grad, cold_feats, fanout)
    own_one, twin_one = join(place, cold, keep, other, feats)
    shares = pair_sums(place, own_one, exchange(twin_one, "copy", 1), n_clique)
    shares = sum_over_slice(shares, two)
    middle = n_clique // 2
    shares = [shares[turn] for turn in laid_turns(n_clique)]
    parts = [jnp.concatenate(part, axis=0) for part in (shares[:middle], shares[middle:])]
    others = [exchange(part, "copy", 1) for part in parts]
    rows_of = (d_in, d_h)
    own = lay(place, parts, n_clique, rows_of)
    return tuple(lay(place, others, n_clique, rows_of, own))


def solution(mesh):
    placed = (
        P(("clique", "copy"), None),
        P(("clique", "copy"), None),
        P(("clique", "copy")),
        P(),
        P(("clique", "copy"), None),
        P(("clique", "copy"), None),
        P("clique", None),
        P(("clique", "copy"), None),
    )
    return jax.shard_map(
        on_device, mesh=mesh, in_specs=placed, out_specs=(P(), P()), check_vma=False
    )
```

```python
import functools

import jax
import jax.numpy as jnp
from jax import lax
from jax.experimental import pallas as pl
from jax.experimental.pallas import tpu as pltpu
from jax.sharding import PartitionSpec as P

F32 = jnp.float32
BF16 = jnp.bfloat16
I16 = jnp.int16
FIELDS = 4
TILE = 16
HALF_MIB = 16
ROWS_MIB = 32


def whole():
    return pl.BlockSpec(memory_space=pltpu.VMEM)


def scalars():
    return pl.BlockSpec(memory_space=pltpu.SMEM)


def in_place():
    return pl.BlockSpec(memory_space=pl.ANY)


def params(mebibytes):
    return pltpu.CompilerParams(vmem_limit_bytes=mebibytes << 20)


def cost(flops, moved):
    return pl.CostEstimate(flops=int(flops), bytes_accessed=int(moved), transcendentals=0)


def transposed_dot(left, right):
    return lax.dot_general(left, right, (((0,), (0,)), ((), ())), preferred_element_type=F32)


def half_kernel(place_ref, feats_ref, half_ref):
    rows = half_ref.shape[0]
    here = pl.ds(pl.multiple_of(place_ref[1] * rows, TILE), rows)
    half_ref[...] = feats_ref[here, :]


def half_of(place, feats):
    rows, d_in = feats.shape
    return pl.pallas_call(
        half_kernel,
        in_specs=[scalars(), whole()],
        out_specs=whole(),
        out_shape=jax.ShapeDtypeStruct((rows // 2, d_in), BF16),
        compiler_params=params(HALF_MIB),
        cost_estimate=cost(10**10, 10**8),
        name="half_of",
    )(place, feats)


def halves(total_ref, own_ref, send_ref, own_shard, own_core, members):
    wide = own_ref.shape[1]
    mine = pl.ds(pl.multiple_of(own_core * wide, wide), wide)
    twin = pl.ds(pl.multiple_of((1 - own_core) * wide, wide), wide)
    rows = own_ref.shape[0] // members
    for member in range(members):
        here = slice(member * rows, (member + 1) * rows)
        there = pl.ds(pl.multiple_of((member ^ own_shard) * rows, TILE), rows)
        own_ref[there, :] = total_ref[here, mine].astype(BF16)
        send_ref[there, :] = total_ref[here, twin].astype(BF16)


def build_words(index, q_rows, store):
    terms = index.shape[0]
    shift = q_rows.bit_length() - 1
    low = index & (q_rows - 1)
    one = jnp.left_shift(jnp.ones_like(index), (index >> shift) * 4)
    unit = one
    for other in range(1, terms):
        turned_low = jnp.concatenate([low[other:], low[:other]], axis=0)
        turned = jnp.concatenate([one[other:], one[:other]], axis=0)
        unit = unit + jnp.where(turned_low == low, turned, jnp.zeros_like(turned))
    tall = min(256, q_rows) // TILE
    shape = (tall, TILE, 128)
    place = lax.broadcasted_iota(jnp.int32, shape, 0) * TILE + lax.broadcasted_iota(jnp.int32, shape, 1)
    place = place.astype(I16)

    def tile(row):
        return jnp.broadcast_to(row, (TILE, 128)).astype(I16)[None]

    lows = [tile(low[k : k + 1, :]) for k in range(terms)]
    units = [tile(unit[k : k + 1, :]) for k in range(terms)]
    for top in range(0, q_rows // TILE, tall):
        word = jnp.zeros(shape, I16)
        for k in range(terms):
            word = jnp.where(place == lows[k] - I16(top * TILE), units[k], word)
        store(top, tall, word)


def unpack(word_ref, field, count_ref, part=0, parts=1):
    deep = word_ref.shape[0] // parts
    words = word_ref[part * deep : (part + 1) * deep, :, :]
    if field < FIELDS - 1:
        counts = words & (15 << (4 * field))
    else:
        counts = (words >> (4 * field)) & 15
    rows = deep * TILE
    count_ref[part * rows : (part + 1) * rows, :] = counts.astype(BF16).reshape(rows, count_ref.shape[1])


def unpacked_scale(field):
    return 16.0**field if field < FIELDS - 1 else 1.0


def rows_kernel(
    shard_bits, half_rows, chunks, members,
    place_ref, count_ref, index_ref, out_grad_ref, pre_act_ref, layer_two_ref,
    row_grad_ref, own_ref, send_ref, word_ref,
    masked_ref, sum_ref,
):
    rows = out_grad_ref.shape[0] // chunks
    blocks = [slice(chunk * rows, (chunk + 1) * rows) for chunk in range(chunks)]
    own_shard, own_core = place_ref[0], place_ref[1]
    part_bits = shard_bits - 1

    def build(tile):
        lanes = slice(tile * 128, (tile + 1) * 128)
        index = index_ref[:, lanes]
        row = index & ((1 << part_bits) - 1)
        half = ((index >> part_bits) & 1) ^ own_core ^ 1
        index = half * half_rows + (((index >> shard_bits) ^ own_shard) << part_bits) + row

        def store(top, tall, words):
            word_ref[top : top + tall, :, lanes] = words

        build_words(index, word_ref.shape[0] * TILE, store)

    tiles = row_grad_ref.shape[0] // 128
    ends = [tiles * chunk // chunks for chunk in range(chunks + 1)]
    for chunk, block in enumerate(blocks):
        live = count_ref[0] - chunk * rows

        @pl.when(live >= rows)
        def _(block=block):
            masked_ref[block, :] = out_grad_ref[block, :]

        @pl.when(live < rows)
        def _(block=block, live=live):
            out_grad = out_grad_ref[block, :].astype(F32)
            place = lax.broadcasted_iota(jnp.int32, out_grad.shape, 0)
            masked = jnp.where(place < live, out_grad, jnp.zeros_like(out_grad))
            masked_ref[block, :] = masked.astype(BF16)

    for chunk, block in enumerate(blocks):
        masked = masked_ref[block, :]
        pre_act = pre_act_ref[block, :]
        back = lax.dot_general(
            masked, layer_two_ref[...], (((1,), (1,)), ((), ())), preferred_element_type=F32
        )
        row_grad_ref[block, :] = jnp.where(
            pre_act.astype(F32) > 0, back, jnp.zeros_like(back)
        ).astype(BF16)
        activ = jnp.maximum(pre_act, jnp.zeros_like(pre_act))
        part = transposed_dot(activ, masked)
        sum_ref[...] = part if chunk == 0 else sum_ref[...] + part
        for tile in range(ends[chunk], ends[chunk + 1]):
            build(tile)
    halves(sum_ref, own_ref, send_ref, own_shard, own_core, members)


def row_gradients(place, batch_count, out_grad, pre_act, layer_two, index, hot_total, shard_rows):
    rows, d_out = out_grad.shape
    d_h = pre_act.shape[1]
    chunks = 4
    deep = hot_total // FIELDS // TILE
    half = jax.ShapeDtypeStruct((d_h, d_out // 2), BF16)
    return pl.pallas_call(
        functools.partial(
            rows_kernel,
            shard_rows.bit_length() - 1,
            hot_total // 2,
            chunks,
            hot_total // shard_rows,
        ),
        in_specs=[scalars(), scalars()] + [whole()] * 4,
        out_specs=[whole()] * 4,
        out_shape=[
            jax.ShapeDtypeStruct((rows, d_h), BF16),
            half,
            half,
            jax.ShapeDtypeStruct((deep, TILE, rows), I16),
        ],
        scratch_shapes=[
            pltpu.VMEM((rows, d_out), BF16),
            pltpu.VMEM((d_h, d_out), F32),
        ],
        compiler_params=params(ROWS_MIB),
        cost_estimate=cost(10**10, 10**8),
        name="row_gradients",
    )(place, batch_count, index, out_grad, pre_act, layer_two)


def sums_of_field(counts, row_grad_ref, field, scale, out_ref, top, beside):
    tall = counts[0].shape[0]
    wide = row_grad_ref.shape[1] // 2
    for half in range(2):
        lanes = slice(half * wide, (half + 1) * wide)
        found = jnp.dot(
            counts[field % 2][...], row_grad_ref[:, lanes], preferred_element_type=F32
        )
        found = found * (scale / unpacked_scale(field))
        out_ref[top : top + tall, lanes] = found.astype(BF16)
        beside(half)


def hot_kernel(
    scale, word_ref, row_grad_ref, index_ref, send_ref, keep_ref, cold_word_ref, *counts
):
    tall, rows = counts[0].shape
    tiles = rows // 128 // FIELDS // 2
    unpack(word_ref, 0, counts[0])
    for field in range(FIELDS):

        def beside(half, field=field):
            if field + 1 < FIELDS:
                unpack(word_ref, field + 1, counts[(field + 1) % 2], half, 2)
            first = (2 * field + half) * tiles
            for tile in range(first, first + tiles):
                lanes = slice(tile * 128, (tile + 1) * 128)

                def store(top, deep, words, lanes=lanes):
                    cold_word_ref[top : top + deep, :, lanes] = words

                build_words(index_ref[:, lanes], cold_word_ref.shape[0] * TILE, store)

        out_ref = (send_ref, keep_ref)[field // 2]
        sums_of_field(counts, row_grad_ref, field, scale, out_ref, field % 2 * tall, beside)


def hot_sums(words, row_grad, cold_index, cold_rows, fanout):
    rows, d_h = row_grad.shape
    q_rows = words.shape[0] * TILE
    half = jax.ShapeDtypeStruct((q_rows * FIELDS // 2, d_h), BF16)
    return pl.pallas_call(
        functools.partial(hot_kernel, 1.0 / fanout),
        in_specs=[whole(), whole(), whole()],
        out_specs=[whole()] * 3,
        out_shape=[
            half,
            half,
            jax.ShapeDtypeStruct((cold_rows // FIELDS // TILE, TILE, rows), I16),
        ],
        scratch_shapes=[pltpu.VMEM((q_rows, rows), BF16)] * 2,
        compiler_params=params(40),
        cost_estimate=cost(10**10, 10**8),
        name="hot_sums",
    )(words, row_grad, cold_index)


def cold_kernel(scale, word_ref, row_grad_ref, feats_ref, grad_ref, sums_ref, held_ref, sem, *counts):
    fetch = pltpu.make_async_copy(feats_ref, held_ref, sem)
    fetch.start()
    tall = counts[0].shape[0]
    wide = held_ref.shape[1] // 2

    def add_product(field, half):
        rows, lanes = slice(field * tall, (field + 1) * tall), slice(half * wide, (half + 1) * wide)
        part = transposed_dot(held_ref[rows, lanes], sums_ref[rows, :])
        grad_ref[lanes, :] = part if field == 0 else grad_ref[lanes, :] + part

    unpack(word_ref, 0, counts[0])
    for field in range(FIELDS):
        if field == 1:
            fetch.wait()

        def beside(half, field=field):
            if field + 1 < FIELDS:
                unpack(word_ref, field + 1, counts[(field + 1) % 2], half, 2)
            if field > 0:
                add_product(field - 1, half)

        sums_of_field(counts, row_grad_ref, field, scale, sums_ref, field * tall, beside)
    for half in range(2):
        add_product(FIELDS - 1, half)


def cold_grad(words, row_grad, feats, fanout):
    rows, d_h = row_grad.shape
    cold_rows, d_in = feats.shape
    q_rows = cold_rows // FIELDS
    return pl.pallas_call(
        functools.partial(cold_kernel, 1.0 / fanout),
        in_specs=[whole(), whole(), in_place()],
        out_specs=whole(),
        out_shape=jax.ShapeDtypeStruct((d_in, d_h), F32),
        scratch_shapes=[
            pltpu.VMEM((cold_rows, d_h), BF16),
            pltpu.VMEM((cold_rows, d_in), BF16),
            pltpu.SemaphoreType.DMA,
            pltpu.VMEM((q_rows, rows), BF16),
            pltpu.VMEM((q_rows, rows), BF16),
        ],
        compiler_params=params(40),
        cost_estimate=cost(10**10, 10**8),
        name="cold_grad",
    )(words, row_grad, feats)


def join_kernel(parts, place_ref, cold_ref, keep_ref, other_ref, *rest):
    feats, (own_ref, send_ref) = rest[:parts], rest[parts:]
    own_core = place_ref[1]
    d_in, d_h = cold_ref.shape
    wide = d_h // 2
    sums = (keep_ref[...].astype(F32) + other_ref[...].astype(F32)).astype(BF16)
    for left in range(0, d_in, 256):
        rows = slice(left, left + 256)
        part = jnp.concatenate([part[:, rows] for part in feats], axis=0)
        total = (cold_ref[rows, :] + transposed_dot(part, sums)).astype(BF16)
        first, second = total[:, :wide], total[:, wide:]

        @pl.when(own_core == 0)
        def _(rows=rows, first=first, second=second):
            own_ref[rows, :] = first
            send_ref[rows, :] = second

        @pl.when(own_core == 1)
        def _(rows=rows, first=first, second=second):
            own_ref[rows, :] = second
            send_ref[rows, :] = first


def join(place, cold, keep, other, feats):
    d_in, d_h = cold.shape
    half = jax.ShapeDtypeStruct((d_in, d_h // 2), BF16)
    return pl.pallas_call(
        functools.partial(join_kernel, len(feats)),
        in_specs=[scalars()] + [whole()] * (3 + len(feats)),
        out_specs=[whole()] * 2,
        out_shape=[half, half],
        compiler_params=params(32),
        cost_estimate=cost(2 * keep.shape[0] * d_h * d_in, 4 * d_in * d_h),
        name="join",
    )(place, cold, keep, other, *feats)


def share_rows(rows, members, place_ref, core, turn):
    size = rows // members
    partner = turn
    if members == 4 and turn == 1:
        partner = 3
    elif members == 4 and turn > 1:
        partner = jnp.where(core == 0, turn - 1, 4 - turn)
    return pl.ds(pl.multiple_of((place_ref[0] ^ partner) * size, TILE), size)


def pair_kernel(place_ref, one_ref, other_ref, *out_refs):
    members = len(out_refs)
    for k, out_ref in enumerate(out_refs):
        here = share_rows(one_ref.shape[0], members, place_ref, place_ref[1], k)
        total = one_ref[here, :].astype(F32) + other_ref[here, :].astype(F32)
        out_ref[...] = total.astype(BF16)


def pair_sums(place, one, other, members):
    rows, wide = one.shape
    share = jax.ShapeDtypeStruct((rows // members, wide), BF16)
    return pl.pallas_call(
        pair_kernel,
        in_specs=[scalars()] + [whole()] * 2,
        out_specs=[whole()] * members,
        out_shape=[share] * members,
        compiler_params=params(16),
        cost_estimate=cost(0, 6 * rows * wide),
        name="pair_sums",
    )(place, one, other)


def laid_turns(members):
    return [0, members - 1, *range(1, members - 1)]


def lay_kernel(members, parts, twin, place_ref, *refs):
    halves_in, refs = refs[:parts], refs[parts:]
    refs = refs[2:] if twin else refs
    outs, held, sems = refs[:2], refs[2:4], refs[4]
    core = 1 - place_ref[1] if twin else place_ref[1]
    wide = halves_in[0].shape[1]
    lanes = pl.ds(pl.multiple_of(core * wide, wide), wide)
    each = members // parts
    copies = []
    for k, turn in enumerate(laid_turns(members)):
        base = k % each * (halves_in[0].shape[0] // each)
        for at, (out_ref, held_ref) in enumerate(zip(outs, held)):
            here = share_rows(out_ref.shape[0], members, place_ref, core, turn)
            held_ref[here, :] = halves_in[k // each][base : base + here.size, :].astype(F32)
            copy = pltpu.make_async_copy(
                held_ref.at[here, :], out_ref.at[here, lanes], sems.at[2 * k + at]
            )
            copy.start()
            copies.append(copy)
            base += here.size
    for copy in copies:
        copy.wait()


def lay(place, parts, members, rows_of, before=()):
    wide = parts[0].shape[1]
    count = 1 + len(parts)
    return pl.pallas_call(
        functools.partial(lay_kernel, members, len(parts), bool(before)),
        in_specs=[scalars()] + [whole()] * len(parts) + [in_place()] * len(before),
        out_specs=[in_place()] * len(rows_of),
        out_shape=[jax.ShapeDtypeStruct((rows, 2 * wide), F32) for rows in rows_of],
        input_output_aliases={count + at: at for at in range(len(before))},
        scratch_shapes=[pltpu.VMEM((rows, wide), F32) for rows in rows_of]
        + [pltpu.SemaphoreType.DMA((2 * members,))],
        compiler_params=params(16),
        cost_estimate=cost(10**10, 10**8),
        name="lay",
    )(place, *parts, *before)


def exchange(array, axis, step):
    size = lax.axis_size(axis)
    return lax.ppermute(array, axis, [(source, source ^ step) for source in range(size)])


def added(*arrays):
    total = arrays[0].astype(F32)
    for array in arrays[1:]:
        total = total + array.astype(F32)
    return total.astype(BF16)


def route_of(n_clique, n_copy, turn):
    moves = [(0, 0), (3, 3), (1, 2), (2, 1)][turn] if n_clique == 4 else (turn, turn)
    return [
        (i * n_copy + j, (i ^ moves[j & 1]) * n_copy + j)
        for i in range(n_clique)
        for j in range(n_copy)
    ]


def trade(arrays):
    n_clique, n_copy = lax.axis_size("clique"), lax.axis_size("copy")
    return [arrays[0]] + [
        lax.ppermute(arrays[turn], ("clique", "copy"), route_of(n_clique, n_copy, turn))
        for turn in range(1, n_clique)
    ]


def sum_over_slice(shares, two):
    own = jnp.concatenate([added(*trade(shares)), two], axis=0)
    n_copy = lax.axis_size("copy")
    steps = [2 << bit for bit in range((n_copy // 2).bit_length() - 1)]
    for near, far in zip(steps, reversed(steps)):
        route = [(j, j ^ (far if j & 1 else near)) for j in range(n_copy)]
        own = added(own, lax.ppermute(own, "copy", route))
    return trade([own] * len(shares))


def gather(own, two):
    members = lax.axis_size("clique")
    rows = two.shape[0] // members
    shares = [two[k * rows : (k + 1) * rows] for k in range(members)]
    middle, d_in = own.shape[0] // 2, own.shape[1]
    if members != 4 or rows != middle:
        feats = [own] + [exchange(own, "clique", k) for k in range(1, members)]
        got = shares[:1] + [exchange(shares[k], "clique", k) for k in range(1, members)]
        return feats, added(*got)
    one, other = exchange(own, "clique", 1), exchange(own, "clique", 2)
    top = exchange(jnp.concatenate([other[:middle], shares[1]], axis=1), "clique", 1)
    bottom = exchange(jnp.concatenate([one[middle:], shares[2]], axis=1), "clique", 2)
    far = exchange(shares[3], "clique", 3)
    total = added(shares[0], top[:, d_in:], bottom[:, d_in:], far)
    return [own, one, other, top, bottom], total


def on_device(
    out_grad, pre_act, batch_count, layer_two, hot_slots, cold_index, hot_feats, cold_feats
):
    n_clique = lax.axis_size("clique")
    shard_rows, d_in = hot_feats.shape
    d_h = pre_act.shape[1]
    cold_rows = cold_feats.shape[0]
    fanout = hot_slots.shape[1] + cold_index.shape[1]
    copy_at = lax.axis_index("copy")
    place = jnp.stack([lax.axis_index("clique"), copy_at & 1]).astype(jnp.int32)

    half_feats = half_of(place, hot_feats)
    row_grad, own_two, twin_two, words = row_gradients(
        place, batch_count, out_grad, pre_act, layer_two, hot_slots.T, shard_rows * n_clique, shard_rows
    )
    two = added(own_two, exchange(twin_two, "copy", 1))
    feats, two = gather(half_feats, two)
    send, keep, words = hot_sums(words, row_grad, cold_index.T, cold_rows, fanout)
    other = exchange(send, "copy", 1)
    cold = cold_grad(words, row_grad, cold_feats, fanout)
    own_one, twin_one = join(place, cold, keep, other, feats)
    shares = pair_sums(place, own_one, exchange(twin_one, "copy", 1), n_clique)
    shares = sum_over_slice(shares, two)
    middle = n_clique // 2
    shares = [shares[turn] for turn in laid_turns(n_clique)]
    parts = [jnp.concatenate(part, axis=0) for part in (shares[:middle], shares[middle:])]
    others = [exchange(part, "copy", 1) for part in parts]
    rows_of = (d_in, d_h)
    own = lay(place, parts, n_clique, rows_of)
    return tuple(lay(place, others, n_clique, rows_of, own))


def solution(mesh):
    placed = (
        P(("clique", "copy"), None),
        P(("clique", "copy"), None),
        P(("clique", "copy")),
        P(),
        P(("clique", "copy"), None),
        P(("clique", "copy"), None),
        P("clique", None),
        P(("clique", "copy"), None),
    )
    return jax.shard_map(
        on_device, mesh=mesh, in_specs=placed, out_specs=(P(), P()), check_vma=False
    )
```

```python
import functools

import jax
import jax.numpy as jnp
from jax import lax
from jax.experimental import pallas as pl
from jax.experimental.pallas import tpu as pltpu
from jax.sharding import PartitionSpec as P

F32 = jnp.float32
BF16 = jnp.bfloat16
I16 = jnp.int16
FIELDS = 4
TILE = 16
HALF_MIB = 16
ROWS_MIB = 32


def whole():
    return pl.BlockSpec(memory_space=pltpu.VMEM)


def scalars():
    return pl.BlockSpec(memory_space=pltpu.SMEM)


def in_place():
    return pl.BlockSpec(memory_space=pl.ANY)


def params(mebibytes):
    return pltpu.CompilerParams(vmem_limit_bytes=mebibytes << 20)


def cost(flops, moved):
    return pl.CostEstimate(flops=int(flops), bytes_accessed=int(moved), transcendentals=0)


def transposed_dot(left, right):
    return lax.dot_general(left, right, (((0,), (0,)), ((), ())), preferred_element_type=F32)


def half_kernel(place_ref, feats_ref, half_ref):
    rows = half_ref.shape[0]
    here = pl.ds(pl.multiple_of(place_ref[1] * rows, TILE), rows)
    half_ref[...] = feats_ref[here, :]


def half_of(place, feats):
    rows, d_in = feats.shape
    return pl.pallas_call(
        half_kernel,
        in_specs=[scalars(), whole()],
        out_specs=whole(),
        out_shape=jax.ShapeDtypeStruct((rows // 2, d_in), BF16),
        compiler_params=params(HALF_MIB),
        cost_estimate=cost(10**10, 10**8),
        name="half_of",
    )(place, feats)


def halves(total_ref, own_ref, send_ref, own_shard, own_core, members):
    wide = own_ref.shape[1]
    mine = pl.ds(pl.multiple_of(own_core * wide, wide), wide)
    twin = pl.ds(pl.multiple_of((1 - own_core) * wide, wide), wide)
    rows = own_ref.shape[0] // members
    for member in range(members):
        here = slice(member * rows, (member + 1) * rows)
        there = pl.ds(pl.multiple_of((member ^ own_shard) * rows, TILE), rows)
        own_ref[there, :] = total_ref[here, mine].astype(BF16)
        send_ref[there, :] = total_ref[here, twin].astype(BF16)


def build_words(index, q_rows, store):
    terms = index.shape[0]
    shift = q_rows.bit_length() - 1
    low = index & (q_rows - 1)
    one = jnp.left_shift(jnp.ones_like(index), (index >> shift) * 4)
    unit = one
    for other in range(1, terms):
        turned_low = jnp.concatenate([low[other:], low[:other]], axis=0)
        turned = jnp.concatenate([one[other:], one[:other]], axis=0)
        unit = unit + jnp.where(turned_low == low, turned, jnp.zeros_like(turned))
    tall = min(256, q_rows) // TILE
    shape = (tall, TILE, 128)
    place = lax.broadcasted_iota(jnp.int32, shape, 0) * TILE + lax.broadcasted_iota(jnp.int32, shape, 1)
    place = place.astype(I16)

    def tile(row):
        return jnp.broadcast_to(row, (TILE, 128)).astype(I16)[None]

    lows = [tile(low[k : k + 1, :]) for k in range(terms)]
    units = [tile(unit[k : k + 1, :]) for k in range(terms)]
    for top in range(0, q_rows // TILE, tall):
        word = jnp.zeros(shape, I16)
        for k in range(terms):
            word = jnp.where(place == lows[k] - I16(top * TILE), units[k], word)
        store(top, tall, word)


def unpack(word_ref, field, count_ref, part=0, parts=1):
    deep = word_ref.shape[0] // parts
    words = word_ref[part * deep : (part + 1) * deep, :, :]
    if field < FIELDS - 1:
        counts = words & (15 << (4 * field))
    else:
        counts = (words >> (4 * field)) & 15
    rows = deep * TILE
    count_ref[part * rows : (part + 1) * rows, :] = counts.astype(BF16).reshape(rows, count_ref.shape[1])


def unpacked_scale(field):
    return 16.0**field if field < FIELDS - 1 else 1.0


def rows_kernel(
    shard_bits, half_rows, chunks, members,
    place_ref, count_ref, index_ref, out_grad_ref, pre_act_ref, layer_two_ref,
    row_grad_ref, own_ref, send_ref, word_ref,
    masked_ref, sum_ref,
):
    rows = out_grad_ref.shape[0] // chunks
    blocks = [slice(chunk * rows, (chunk + 1) * rows) for chunk in range(chunks)]
    own_shard, own_core = place_ref[0], place_ref[1]
    part_bits = shard_bits - 1

    def build(tile):
        lanes = slice(tile * 128, (tile + 1) * 128)
        index = index_ref[:, lanes]
        row = index & ((1 << part_bits) - 1)
        half = ((index >> part_bits) & 1) ^ own_core ^ 1
        index = half * half_rows + (((index >> shard_bits) ^ own_shard) << part_bits) + row

        def store(top, tall, words):
            word_ref[top : top + tall, :, lanes] = words

        build_words(index, word_ref.shape[0] * TILE, store)

    tiles = row_grad_ref.shape[0] // 128
    ends = [tiles * chunk // chunks for chunk in range(chunks + 1)]
    for chunk, block in enumerate(blocks):
        live = count_ref[0] - chunk * rows

        @pl.when(live >= rows)
        def _(block=block):
            masked_ref[block, :] = out_grad_ref[block, :]

        @pl.when(live < rows)
        def _(block=block, live=live):
            out_grad = out_grad_ref[block, :].astype(F32)
            place = lax.broadcasted_iota(jnp.int32, out_grad.shape, 0)
            masked = jnp.where(place < live, out_grad, jnp.zeros_like(out_grad))
            masked_ref[block, :] = masked.astype(BF16)

    for chunk, block in enumerate(blocks):
        masked = masked_ref[block, :]
        pre_act = pre_act_ref[block, :]
        back = lax.dot_general(
            masked, layer_two_ref[...], (((1,), (1,)), ((), ())), preferred_element_type=F32
        )
        row_grad_ref[block, :] = jnp.where(
            pre_act.astype(F32) > 0, back, jnp.zeros_like(back)
        ).astype(BF16)
        activ = jnp.maximum(pre_act, jnp.zeros_like(pre_act))
        part = transposed_dot(activ, masked)
        sum_ref[...] = part if chunk == 0 else sum_ref[...] + part
        for tile in range(ends[chunk], ends[chunk + 1]):
            build(tile)
    halves(sum_ref, own_ref, send_ref, own_shard, own_core, members)


def row_gradients(place, batch_count, out_grad, pre_act, layer_two, index, hot_total, shard_rows):
    rows, d_out = out_grad.shape
    d_h = pre_act.shape[1]
    chunks = 4
    deep = hot_total // FIELDS // TILE
    half = jax.ShapeDtypeStruct((d_h, d_out // 2), BF16)
    return pl.pallas_call(
        functools.partial(
            rows_kernel,
            shard_rows.bit_length() - 1,
            hot_total // 2,
            chunks,
            hot_total // shard_rows,
        ),
        in_specs=[scalars(), scalars()] + [whole()] * 4,
        out_specs=[whole()] * 4,
        out_shape=[
            jax.ShapeDtypeStruct((rows, d_h), BF16),
            half,
            half,
            jax.ShapeDtypeStruct((deep, TILE, rows), I16),
        ],
        scratch_shapes=[
            pltpu.VMEM((rows, d_out), BF16),
            pltpu.VMEM((d_h, d_out), F32),
        ],
        compiler_params=params(ROWS_MIB),
        cost_estimate=cost(10**10, 10**8),
        name="row_gradients",
    )(place, batch_count, index, out_grad, pre_act, layer_two)


def sums_of_field(counts, row_grad_ref, field, scale, out_ref, top, beside):
    tall = counts[0].shape[0]
    wide = row_grad_ref.shape[1] // 2
    for half in range(2):
        lanes = slice(half * wide, (half + 1) * wide)
        found = jnp.dot(
            counts[field % 2][...], row_grad_ref[:, lanes], preferred_element_type=F32
        )
        found = found * (scale / unpacked_scale(field))
        out_ref[top : top + tall, lanes] = found.astype(BF16)
        beside(half)


def hot_kernel(
    scale, word_in, row_grad_in, index_in, send_ref, keep_ref, cold_word_out,
    word_ref, row_grad_ref, index_ref, sums_ref, cold_word_ref, *counts
):
    word_ref[...] = word_in[...]
    row_grad_ref[...] = row_grad_in[...]
    index_ref[...] = index_in[...]
    tall, rows = counts[0].shape
    tiles = rows // 128 // FIELDS // 2
    unpack(word_ref, 0, counts[0])
    for field in range(FIELDS):

        def beside(half, field=field):
            if field + 1 < FIELDS:
                unpack(word_ref, field + 1, counts[(field + 1) % 2], half, 2)
            first = (2 * field + half) * tiles
            for tile in range(first, first + tiles):
                lanes = slice(tile * 128, (tile + 1) * 128)

                def store(top, deep, words, lanes=lanes):
                    cold_word_ref[top : top + deep, :, lanes] = words

                build_words(index_ref[:, lanes], cold_word_ref.shape[0] * TILE, store)

        sums_of_field(counts, row_grad_ref, field, scale, sums_ref, field * tall, beside)
    send_ref[...] = sums_ref[: 2 * tall, :]
    keep_ref[...] = sums_ref[2 * tall :, :]
    cold_word_out[...] = cold_word_ref[...]


def hot_sums(words, row_grad, cold_index, cold_rows, fanout):
    rows, d_h = row_grad.shape
    q_rows = words.shape[0] * TILE
    half = jax.ShapeDtypeStruct((q_rows * FIELDS // 2, d_h), BF16)
    return pl.pallas_call(
        functools.partial(hot_kernel, 1.0 / fanout),
        in_specs=[whole(), whole(), whole()],
        out_specs=[whole()] * 3,
        out_shape=[
            half,
            half,
            jax.ShapeDtypeStruct((cold_rows // FIELDS // TILE, TILE, rows), I16),
        ],
        scratch_shapes=[
            pltpu.VMEM(words.shape, I16),
            pltpu.VMEM(row_grad.shape, BF16),
            pltpu.VMEM(cold_index.shape, jnp.int32),
            pltpu.VMEM((q_rows * FIELDS, d_h), BF16),
            pltpu.VMEM((cold_rows // FIELDS // TILE, TILE, rows), I16),
            pltpu.VMEM((q_rows, rows), BF16),
            pltpu.VMEM((q_rows, rows), BF16),
        ],
        compiler_params=params(40),
        cost_estimate=cost(10**10, 10**8),
        name="hot_sums",
    )(words, row_grad, cold_index)


def cold_kernel(
    scale, word_in, row_grad_in, feats_ref, grad_out,
    word_ref, row_grad_ref, grad_ref, sums_ref, held_ref, sem, *counts
):
    fetch = pltpu.make_async_copy(feats_ref, held_ref, sem)
    fetch.start()
    word_ref[...] = word_in[...]
    row_grad_ref[...] = row_grad_in[...]
    tall = counts[0].shape[0]
    wide = held_ref.shape[1] // 2

    def add_product(field, half):
        rows, lanes = slice(field * tall, (field + 1) * tall), slice(half * wide, (half + 1) * wide)
        part = transposed_dot(held_ref[rows, lanes], sums_ref[rows, :])
        grad_ref[lanes, :] = part if field == 0 else grad_ref[lanes, :] + part

    unpack(word_ref, 0, counts[0])
    for field in range(FIELDS):
        if field == 1:
            fetch.wait()

        def beside(half, field=field):
            if field + 1 < FIELDS:
                unpack(word_ref, field + 1, counts[(field + 1) % 2], half, 2)
            if field > 0:
                add_product(field - 1, half)

        sums_of_field(counts, row_grad_ref, field, scale, sums_ref, field * tall, beside)
    for half in range(2):
        add_product(FIELDS - 1, half)
    grad_out[...] = grad_ref[...]


def cold_grad(words, row_grad, feats, fanout):
    rows, d_h = row_grad.shape
    cold_rows, d_in = feats.shape
    q_rows = cold_rows // FIELDS
    return pl.pallas_call(
        functools.partial(cold_kernel, 1.0 / fanout),
        in_specs=[whole(), whole(), in_place()],
        out_specs=whole(),
        out_shape=jax.ShapeDtypeStruct((d_in, d_h), F32),
        scratch_shapes=[
            pltpu.VMEM(words.shape, I16),
            pltpu.VMEM(row_grad.shape, BF16),
            pltpu.VMEM((d_in, d_h), F32),
            pltpu.VMEM((cold_rows, d_h), BF16),
            pltpu.VMEM((cold_rows, d_in), BF16),
            pltpu.SemaphoreType.DMA,
            pltpu.VMEM((q_rows, rows), BF16),
            pltpu.VMEM((q_rows, rows), BF16),
        ],
        compiler_params=params(40),
        cost_estimate=cost(10**10, 10**8),
        name="cold_grad",
    )(words, row_grad, feats)


def join_kernel(parts, place_ref, cold_ref, keep_ref, other_ref, *rest):
    feats, (own_ref, send_ref) = rest[:parts], rest[parts:]
    own_core = place_ref[1]
    d_in, d_h = cold_ref.shape
    wide = d_h // 2
    sums = (keep_ref[...].astype(F32) + other_ref[...].astype(F32)).astype(BF16)
    for left in range(0, d_in, 256):
        rows = slice(left, left + 256)
        part = jnp.concatenate([part[:, rows] for part in feats], axis=0)
        total = (cold_ref[rows, :] + transposed_dot(part, sums)).astype(BF16)
        first, second = total[:, :wide], total[:, wide:]

        @pl.when(own_core == 0)
        def _(rows=rows, first=first, second=second):
            own_ref[rows, :] = first
            send_ref[rows, :] = second

        @pl.when(own_core == 1)
        def _(rows=rows, first=first, second=second):
            own_ref[rows, :] = second
            send_ref[rows, :] = first


def join(place, cold, keep, other, feats):
    d_in, d_h = cold.shape
    half = jax.ShapeDtypeStruct((d_in, d_h // 2), BF16)
    return pl.pallas_call(
        functools.partial(join_kernel, len(feats)),
        in_specs=[scalars()] + [whole()] * (3 + len(feats)),
        out_specs=[whole()] * 2,
        out_shape=[half, half],
        compiler_params=params(32),
        cost_estimate=cost(2 * keep.shape[0] * d_h * d_in, 4 * d_in * d_h),
        name="join",
    )(place, cold, keep, other, *feats)


def share_rows(rows, members, place_ref, core, turn):
    size = rows // members
    partner = turn
    if members == 4 and turn == 1:
        partner = 3
    elif members == 4 and turn > 1:
        partner = jnp.where(core == 0, turn - 1, 4 - turn)
    return pl.ds(pl.multiple_of((place_ref[0] ^ partner) * size, TILE), size)


def pair_kernel(place_ref, one_ref, other_ref, *out_refs):
    members = len(out_refs)
    for k, out_ref in enumerate(out_refs):
        here = share_rows(one_ref.shape[0], members, place_ref, place_ref[1], k)
        total = one_ref[here, :].astype(F32) + other_ref[here, :].astype(F32)
        out_ref[...] = total.astype(BF16)


def pair_sums(place, one, other, members):
    rows, wide = one.shape
    share = jax.ShapeDtypeStruct((rows // members, wide), BF16)
    return pl.pallas_call(
        pair_kernel,
        in_specs=[scalars()] + [whole()] * 2,
        out_specs=[whole()] * members,
        out_shape=[share] * members,
        compiler_params=params(16),
        cost_estimate=cost(0, 6 * rows * wide),
        name="pair_sums",
    )(place, one, other)


def laid_turns(members):
    return [0, members - 1, *range(1, members - 1)]


def lay_kernel(members, parts, twin, place_ref, *refs):
    halves_in, refs = refs[:parts], refs[parts:]
    refs = refs[2:] if twin else refs
    outs, held, sems = refs[:2], refs[2:4], refs[4]
    core = 1 - place_ref[1] if twin else place_ref[1]
    wide = halves_in[0].shape[1]
    lanes = pl.ds(pl.multiple_of(core * wide, wide), wide)
    each = members // parts
    copies = []
    for k, turn in enumerate(laid_turns(members)):
        base = k % each * (halves_in[0].shape[0] // each)
        for at, (out_ref, held_ref) in enumerate(zip(outs, held)):
            here = share_rows(out_ref.shape[0], members, place_ref, core, turn)
            held_ref[here, :] = halves_in[k // each][base : base + here.size, :].astype(F32)
            copy = pltpu.make_async_copy(
                held_ref.at[here, :], out_ref.at[here, lanes], sems.at[2 * k + at]
            )
            copy.start()
            copies.append(copy)
            base += here.size
    for copy in copies:
        copy.wait()


def lay(place, parts, members, rows_of, before=()):
    wide = parts[0].shape[1]
    count = 1 + len(parts)
    return pl.pallas_call(
        functools.partial(lay_kernel, members, len(parts), bool(before)),
        in_specs=[scalars()] + [whole()] * len(parts) + [in_place()] * len(before),
        out_specs=[in_place()] * len(rows_of),
        out_shape=[jax.ShapeDtypeStruct((rows, 2 * wide), F32) for rows in rows_of],
        input_output_aliases={count + at: at for at in range(len(before))},
        scratch_shapes=[pltpu.VMEM((rows, wide), F32) for rows in rows_of]
        + [pltpu.SemaphoreType.DMA((2 * members,))],
        compiler_params=params(16),
        cost_estimate=cost(10**10, 10**8),
        name="lay",
    )(place, *parts, *before)


def exchange(array, axis, step):
    size = lax.axis_size(axis)
    return lax.ppermute(array, axis, [(source, source ^ step) for source in range(size)])


def added(*arrays):
    total = arrays[0].astype(F32)
    for array in arrays[1:]:
        total = total + array.astype(F32)
    return total.astype(BF16)


def route_of(n_clique, n_copy, turn):
    moves = [(0, 0), (3, 3), (1, 2), (2, 1)][turn] if n_clique == 4 else (turn, turn)
    return [
        (i * n_copy + j, (i ^ moves[j & 1]) * n_copy + j)
        for i in range(n_clique)
        for j in range(n_copy)
    ]


def trade(arrays):
    n_clique, n_copy = lax.axis_size("clique"), lax.axis_size("copy")
    return [arrays[0]] + [
        lax.ppermute(arrays[turn], ("clique", "copy"), route_of(n_clique, n_copy, turn))
        for turn in range(1, n_clique)
    ]


def sum_over_slice(shares, two):
    own = jnp.concatenate([added(*trade(shares)), two], axis=0)
    n_copy = lax.axis_size("copy")
    steps = [2 << bit for bit in range((n_copy // 2).bit_length() - 1)]
    for near, far in zip(steps, reversed(steps)):
        route = [(j, j ^ (far if j & 1 else near)) for j in range(n_copy)]
        own = added(own, lax.ppermute(own, "copy", route))
    return trade([own] * len(shares))


def gather(own, two):
    members = lax.axis_size("clique")
    rows = two.shape[0] // members
    shares = [two[k * rows : (k + 1) * rows] for k in range(members)]
    middle, d_in = own.shape[0] // 2, own.shape[1]
    if members != 4 or rows != middle:
        feats = [own] + [exchange(own, "clique", k) for k in range(1, members)]
        got = shares[:1] + [exchange(shares[k], "clique", k) for k in range(1, members)]
        return feats, added(*got)
    one, other = exchange(own, "clique", 1), exchange(own, "clique", 2)
    top = exchange(jnp.concatenate([other[:middle], shares[1]], axis=1), "clique", 1)
    bottom = exchange(jnp.concatenate([one[middle:], shares[2]], axis=1), "clique", 2)
    far = exchange(shares[3], "clique", 3)
    total = added(shares[0], top[:, d_in:], bottom[:, d_in:], far)
    return [own, one, other, top, bottom], total


def on_device(
    out_grad, pre_act, batch_count, layer_two, hot_slots, cold_index, hot_feats, cold_feats
):
    n_clique = lax.axis_size("clique")
    shard_rows, d_in = hot_feats.shape
    d_h = pre_act.shape[1]
    cold_rows = cold_feats.shape[0]
    fanout = hot_slots.shape[1] + cold_index.shape[1]
    copy_at = lax.axis_index("copy")
    place = jnp.stack([lax.axis_index("clique"), copy_at & 1]).astype(jnp.int32)

    half_feats = half_of(place, hot_feats)
    row_grad, own_two, twin_two, words = row_gradients(
        place, batch_count, out_grad, pre_act, layer_two, hot_slots.T, shard_rows * n_clique, shard_rows
    )
    two = added(own_two, exchange(twin_two, "copy", 1))
    feats, two = gather(half_feats, two)
    send, keep, words = hot_sums(words, row_grad, cold_index.T, cold_rows, fanout)
    other = exchange(send, "copy", 1)
    cold = cold_grad(words, row_grad, cold_feats, fanout)
    own_one, twin_one = join(place, cold, keep, other, feats)
    shares = pair_sums(place, own_one, exchange(twin_one, "copy", 1), n_clique)
    shares = sum_over_slice(shares, two)
    middle = n_clique // 2
    shares = [shares[turn] for turn in laid_turns(n_clique)]
    parts = [jnp.concatenate(part, axis=0) for part in (shares[:middle], shares[middle:])]
    others = [exchange(part, "copy", 1) for part in parts]
    rows_of = (d_in, d_h)
    own = lay(place, parts, n_clique, rows_of)
    return tuple(lay(place, others, n_clique, rows_of, own))


def solution(mesh):
    placed = (
        P(("clique", "copy"), None),
        P(("clique", "copy"), None),
        P(("clique", "copy")),
        P(),
        P(("clique", "copy"), None),
        P(("clique", "copy"), None),
        P("clique", None),
        P(("clique", "copy"), None),
    )
    return jax.shard_map(
        on_device, mesh=mesh, in_specs=placed, out_specs=(P(), P()), check_vma=False
    )
```

```python
import functools

import jax
import jax.numpy as jnp
from jax import lax
from jax.experimental import pallas as pl
from jax.experimental.pallas import tpu as pltpu
from jax.sharding import PartitionSpec as P

F32 = jnp.float32
BF16 = jnp.bfloat16
I16 = jnp.int16
FIELDS = 4
TILE = 16
HALF_MIB = 16
ROWS_MIB = 32


def whole():
    return pl.BlockSpec(memory_space=pltpu.VMEM)


def scalars():
    return pl.BlockSpec(memory_space=pltpu.SMEM)


def in_place():
    return pl.BlockSpec(memory_space=pl.ANY)


def params(mebibytes):
    return pltpu.CompilerParams(vmem_limit_bytes=mebibytes << 20)


def cost(flops, moved):
    return pl.CostEstimate(flops=int(flops), bytes_accessed=int(moved), transcendentals=0)


def transposed_dot(left, right):
    return lax.dot_general(left, right, (((0,), (0,)), ((), ())), preferred_element_type=F32)


def half_kernel(place_ref, feats_ref, half_ref):
    rows = half_ref.shape[0]
    here = pl.ds(pl.multiple_of(place_ref[1] * rows, TILE), rows)
    half_ref[...] = feats_ref[here, :]


def half_of(place, feats):
    rows, d_in = feats.shape
    return pl.pallas_call(
        half_kernel,
        in_specs=[scalars(), whole()],
        out_specs=whole(),
        out_shape=jax.ShapeDtypeStruct((rows // 2, d_in), BF16),
        compiler_params=params(HALF_MIB),
        cost_estimate=cost(10**10, 10**8),
        name="half_of",
    )(place, feats)


def halves(total_ref, own_ref, send_ref, own_shard, own_core, members):
    wide = own_ref.shape[1]
    mine = pl.ds(pl.multiple_of(own_core * wide, wide), wide)
    twin = pl.ds(pl.multiple_of((1 - own_core) * wide, wide), wide)
    rows = own_ref.shape[0] // members
    for member in range(members):
        here = slice(member * rows, (member + 1) * rows)
        there = pl.ds(pl.multiple_of((member ^ own_shard) * rows, TILE), rows)
        own_ref[there, :] = total_ref[here, mine].astype(BF16)
        send_ref[there, :] = total_ref[here, twin].astype(BF16)


def build_words(index, q_rows, store):
    terms = index.shape[0]
    shift = q_rows.bit_length() - 1
    low = index & (q_rows - 1)
    one = jnp.left_shift(jnp.ones_like(index), (index >> shift) * 4)
    unit = one
    for other in range(1, terms):
        turned_low = jnp.concatenate([low[other:], low[:other]], axis=0)
        turned = jnp.concatenate([one[other:], one[:other]], axis=0)
        unit = unit + jnp.where(turned_low == low, turned, jnp.zeros_like(turned))
    tall = min(256, q_rows) // TILE
    shape = (tall, TILE, 128)
    place = lax.broadcasted_iota(jnp.int32, shape, 0) * TILE + lax.broadcasted_iota(jnp.int32, shape, 1)
    place = place.astype(I16)

    def tile(row):
        return jnp.broadcast_to(row, (TILE, 128)).astype(I16)[None]

    lows = [tile(low[k : k + 1, :]) for k in range(terms)]
    units = [tile(unit[k : k + 1, :]) for k in range(terms)]
    for top in range(0, q_rows // TILE, tall):
        word = jnp.zeros(shape, I16)
        for k in range(terms):
            word = jnp.where(place == lows[k] - I16(top * TILE), units[k], word)
        store(top, tall, word)


def unpack(word_ref, field, count_ref, part=0, parts=1):
    deep = word_ref.shape[0] // parts
    words = word_ref[part * deep : (part + 1) * deep, :, :]
    if field < FIELDS - 1:
        counts = words & (15 << (4 * field))
    else:
        counts = (words >> (4 * field)) & 15
    rows = deep * TILE
    count_ref[part * rows : (part + 1) * rows, :] = counts.astype(BF16).reshape(rows, count_ref.shape[1])


def unpacked_scale(field):
    return 16.0**field if field < FIELDS - 1 else 1.0


def rows_kernel(
    shard_bits, half_rows, chunks, members,
    place_ref, count_ref, index_in, out_grad_ref, pre_act_in, layer_two_in,
    row_grad_out, own_ref, send_ref, word_out,
    index_ref, masked_ref, pre_act_ref, layer_two_ref, row_grad_ref, word_ref, sum_ref,
):
    index_ref[...] = index_in[...]
    pre_act_ref[...] = pre_act_in[...]
    layer_two_ref[...] = layer_two_in[...]
    rows = out_grad_ref.shape[0] // chunks
    blocks = [slice(chunk * rows, (chunk + 1) * rows) for chunk in range(chunks)]
    own_shard, own_core = place_ref[0], place_ref[1]
    part_bits = shard_bits - 1

    def build(tile):
        lanes = slice(tile * 128, (tile + 1) * 128)
        index = index_ref[:, lanes]
        row = index & ((1 << part_bits) - 1)
        half = ((index >> part_bits) & 1) ^ own_core ^ 1
        index = half * half_rows + (((index >> shard_bits) ^ own_shard) << part_bits) + row

        def store(top, tall, words):
            word_ref[top : top + tall, :, lanes] = words

        build_words(index, word_ref.shape[0] * TILE, store)

    tiles = row_grad_ref.shape[0] // 128
    ends = [tiles * chunk // chunks for chunk in range(chunks + 1)]
    for chunk, block in enumerate(blocks):
        live = count_ref[0] - chunk * rows

        @pl.when(live >= rows)
        def _(block=block):
            masked_ref[block, :] = out_grad_ref[block, :]

        @pl.when(live < rows)
        def _(block=block, live=live):
            out_grad = out_grad_ref[block, :].astype(F32)
            place = lax.broadcasted_iota(jnp.int32, out_grad.shape, 0)
            masked = jnp.where(place < live, out_grad, jnp.zeros_like(out_grad))
            masked_ref[block, :] = masked.astype(BF16)

    for chunk, block in enumerate(blocks):
        masked = masked_ref[block, :]
        pre_act = pre_act_ref[block, :]
        back = lax.dot_general(
            masked, layer_two_ref[...], (((1,), (1,)), ((), ())), preferred_element_type=F32
        )
        row_grad_ref[block, :] = jnp.where(
            pre_act.astype(F32) > 0, back, jnp.zeros_like(back)
        ).astype(BF16)
        activ = jnp.maximum(pre_act, jnp.zeros_like(pre_act))
        part = transposed_dot(activ, masked)
        sum_ref[...] = part if chunk == 0 else sum_ref[...] + part
        for tile in range(ends[chunk], ends[chunk + 1]):
            build(tile)
    row_grad_out[...] = row_grad_ref[...]
    word_out[...] = word_ref[...]
    halves(sum_ref, own_ref, send_ref, own_shard, own_core, members)


def row_gradients(place, batch_count, out_grad, pre_act, layer_two, index, hot_total, shard_rows):
    rows, d_out = out_grad.shape
    d_h = pre_act.shape[1]
    chunks = 4
    deep = hot_total // FIELDS // TILE
    half = jax.ShapeDtypeStruct((d_h, d_out // 2), BF16)
    return pl.pallas_call(
        functools.partial(
            rows_kernel,
            shard_rows.bit_length() - 1,
            hot_total // 2,
            chunks,
            hot_total // shard_rows,
        ),
        in_specs=[scalars(), scalars()] + [whole()] * 4,
        out_specs=[whole()] * 4,
        out_shape=[
            jax.ShapeDtypeStruct((rows, d_h), BF16),
            half,
            half,
            jax.ShapeDtypeStruct((deep, TILE, rows), I16),
        ],
        scratch_shapes=[
            pltpu.VMEM(index.shape, jnp.int32),
            pltpu.VMEM((rows, d_out), BF16),
            pltpu.VMEM((rows, d_h), BF16),
            pltpu.VMEM((d_h, d_out), BF16),
            pltpu.VMEM((rows, d_h), BF16),
            pltpu.VMEM((deep, TILE, rows), I16),
            pltpu.VMEM((d_h, d_out), F32),
        ],
        compiler_params=params(ROWS_MIB),
        cost_estimate=cost(10**10, 10**8),
        name="row_gradients",
    )(place, batch_count, index, out_grad, pre_act, layer_two)


def sums_of_field(counts, row_grad_ref, field, scale, out_ref, top, beside):
    tall = counts[0].shape[0]
    wide = row_grad_ref.shape[1] // 2
    for half in range(2):
        lanes = slice(half * wide, (half + 1) * wide)
        found = jnp.dot(
            counts[field % 2][...], row_grad_ref[:, lanes], preferred_element_type=F32
        )
        found = found * (scale / unpacked_scale(field))
        out_ref[top : top + tall, lanes] = found.astype(BF16)
        beside(half)


def hot_kernel(
    scale, word_in, row_grad_in, index_in, send_ref, keep_ref, cold_word_out,
    word_ref, row_grad_ref, index_ref, sums_ref, cold_word_ref, *counts
):
    word_ref[...] = word_in[...]
    row_grad_ref[...] = row_grad_in[...]
    index_ref[...] = index_in[...]
    tall, rows = counts[0].shape
    tiles = rows // 128 // FIELDS // 2
    unpack(word_ref, 0, counts[0])
    for field in range(FIELDS):

        def beside(half, field=field):
            if field + 1 < FIELDS:
                unpack(word_ref, field + 1, counts[(field + 1) % 2], half, 2)
            first = (2 * field + half) * tiles
            for tile in range(first, first + tiles):
                lanes = slice(tile * 128, (tile + 1) * 128)

                def store(top, deep, words, lanes=lanes):
                    cold_word_ref[top : top + deep, :, lanes] = words

                build_words(index_ref[:, lanes], cold_word_ref.shape[0] * TILE, store)

        sums_of_field(counts, row_grad_ref, field, scale, sums_ref, field * tall, beside)
    send_ref[...] = sums_ref[: 2 * tall, :]
    keep_ref[...] = sums_ref[2 * tall :, :]
    cold_word_out[...] = cold_word_ref[...]


def hot_sums(words, row_grad, cold_index, cold_rows, fanout):
    rows, d_h = row_grad.shape
    q_rows = words.shape[0] * TILE
    half = jax.ShapeDtypeStruct((q_rows * FIELDS // 2, d_h), BF16)
    return pl.pallas_call(
        functools.partial(hot_kernel, 1.0 / fanout),
        in_specs=[whole(), whole(), whole()],
        out_specs=[whole()] * 3,
        out_shape=[
            half,
            half,
            jax.ShapeDtypeStruct((cold_rows // FIELDS // TILE, TILE, rows), I16),
        ],
        scratch_shapes=[
            pltpu.VMEM(words.shape, I16),
            pltpu.VMEM(row_grad.shape, BF16),
            pltpu.VMEM(cold_index.shape, jnp.int32),
            pltpu.VMEM((q_rows * FIELDS, d_h), BF16),
            pltpu.VMEM((cold_rows // FIELDS // TILE, TILE, rows), I16),
            pltpu.VMEM((q_rows, rows), BF16),
            pltpu.VMEM((q_rows, rows), BF16),
        ],
        compiler_params=params(40),
        cost_estimate=cost(10**10, 10**8),
        name="hot_sums",
    )(words, row_grad, cold_index)


def cold_kernel(
    scale, word_in, row_grad_in, feats_ref, grad_out,
    word_ref, row_grad_ref, grad_ref, sums_ref, held_ref, sem, *counts
):
    fetch = pltpu.make_async_copy(feats_ref, held_ref, sem)
    fetch.start()
    word_ref[...] = word_in[...]
    row_grad_ref[...] = row_grad_in[...]
    tall = counts[0].shape[0]
    wide = held_ref.shape[1] // 2

    def add_product(field, half):
        rows, lanes = slice(field * tall, (field + 1) * tall), slice(half * wide, (half + 1) * wide)
        part = transposed_dot(held_ref[rows, lanes], sums_ref[rows, :])
        grad_ref[lanes, :] = part if field == 0 else grad_ref[lanes, :] + part

    unpack(word_ref, 0, counts[0])
    for field in range(FIELDS):
        if field == 1:
            fetch.wait()

        def beside(half, field=field):
            if field + 1 < FIELDS:
                unpack(word_ref, field + 1, counts[(field + 1) % 2], half, 2)
            if field > 0:
                add_product(field - 1, half)

        sums_of_field(counts, row_grad_ref, field, scale, sums_ref, field * tall, beside)
    for half in range(2):
        add_product(FIELDS - 1, half)
    grad_out[...] = grad_ref[...]


def cold_grad(words, row_grad, feats, fanout):
    rows, d_h = row_grad.shape
    cold_rows, d_in = feats.shape
    q_rows = cold_rows // FIELDS
    return pl.pallas_call(
        functools.partial(cold_kernel, 1.0 / fanout),
        in_specs=[whole(), whole(), in_place()],
        out_specs=whole(),
        out_shape=jax.ShapeDtypeStruct((d_in, d_h), F32),
        scratch_shapes=[
            pltpu.VMEM(words.shape, I16),
            pltpu.VMEM(row_grad.shape, BF16),
            pltpu.VMEM((d_in, d_h), F32),
            pltpu.VMEM((cold_rows, d_h), BF16),
            pltpu.VMEM((cold_rows, d_in), BF16),
            pltpu.SemaphoreType.DMA,
            pltpu.VMEM((q_rows, rows), BF16),
            pltpu.VMEM((q_rows, rows), BF16),
        ],
        compiler_params=params(40),
        cost_estimate=cost(10**10, 10**8),
        name="cold_grad",
    )(words, row_grad, feats)


def join_kernel(parts, place_ref, cold_ref, keep_ref, other_ref, *rest):
    feats, (own_ref, send_ref, sums_ref, held_ref, total_ref) = rest[:parts], rest[parts:]
    d_in, wide = own_ref.shape
    sums = keep_ref[...].astype(F32) + other_ref[...].astype(F32)
    sums_ref[...] = sums.astype(BF16)
    base = 0
    for part in feats:
        held_ref[base : base + part.shape[0], :] = part[:, :d_in]
        base += part.shape[0]
    total_ref[...] = cold_ref[...]
    for left in range(0, d_in, 256):
        rows = slice(left, left + 256)
        total_ref[rows, :] += transposed_dot(held_ref[:, rows], sums_ref[...])
    total = total_ref[...].astype(BF16)
    store_halves(total, slice(None), place_ref[1], own_ref, send_ref)


def store_halves(total, rows, own_core, own_ref, send_ref):
    wide = own_ref.shape[1]
    first, second = total[:, :wide], total[:, wide:]

    @pl.when(own_core == 0)
    def _():
        own_ref[rows, :] = first
        send_ref[rows, :] = second

    @pl.when(own_core == 1)
    def _():
        own_ref[rows, :] = second
        send_ref[rows, :] = first


def join(place, cold, keep, other, feats):
    d_in, d_h = cold.shape
    half = jax.ShapeDtypeStruct((d_in, d_h // 2), BF16)
    return pl.pallas_call(
        functools.partial(join_kernel, len(feats)),
        in_specs=[scalars()] + [whole()] * (3 + len(feats)),
        out_specs=[whole()] * 2,
        out_shape=[half, half],
        scratch_shapes=[
            pltpu.VMEM(keep.shape, BF16),
            pltpu.VMEM((keep.shape[0], d_in), BF16),
            pltpu.VMEM((d_in, d_h), F32),
        ],
        compiler_params=params(32),
        cost_estimate=cost(2 * keep.shape[0] * d_h * d_in, 4 * d_in * d_h),
        name="join",
    )(place, cold, keep, other, *feats)


def share_rows(rows, members, place_ref, core, turn):
    size = rows // members
    partner = turn
    if members == 4 and turn == 1:
        partner = 3
    elif members == 4 and turn > 1:
        partner = jnp.where(core == 0, turn - 1, 4 - turn)
    return pl.ds(pl.multiple_of((place_ref[0] ^ partner) * size, TILE), size)


def pair_kernel(place_ref, one_ref, other_ref, *out_refs):
    members = len(out_refs)
    for k, out_ref in enumerate(out_refs):
        here = share_rows(one_ref.shape[0], members, place_ref, place_ref[1], k)
        total = one_ref[here, :].astype(F32) + other_ref[here, :].astype(F32)
        out_ref[...] = total.astype(BF16)


def pair_sums(place, one, other, members):
    rows, wide = one.shape
    share = jax.ShapeDtypeStruct((rows // members, wide), BF16)
    return pl.pallas_call(
        pair_kernel,
        in_specs=[scalars()] + [whole()] * 2,
        out_specs=[whole()] * members,
        out_shape=[share] * members,
        compiler_params=params(16),
        cost_estimate=cost(0, 6 * rows * wide),
        name="pair_sums",
    )(place, one, other)


def laid_turns(members):
    return [0, members - 1, *range(1, members - 1)]


def lay_kernel(members, parts, twin, place_ref, *refs):
    halves_in, refs = refs[:parts], refs[parts:]
    refs = refs[2:] if twin else refs
    outs, held, sems = refs[:2], refs[2:4], refs[4]
    core = 1 - place_ref[1] if twin else place_ref[1]
    wide = halves_in[0].shape[1]
    lanes = pl.ds(pl.multiple_of(core * wide, wide), wide)
    each = members // parts
    copies = []
    for k, turn in enumerate(laid_turns(members)):
        base = k % each * (halves_in[0].shape[0] // each)
        for at, (out_ref, held_ref) in enumerate(zip(outs, held)):
            here = share_rows(out_ref.shape[0], members, place_ref, core, turn)
            held_ref[here, :] = halves_in[k // each][base : base + here.size, :].astype(F32)
            copy = pltpu.make_async_copy(
                held_ref.at[here, :], out_ref.at[here, lanes], sems.at[2 * k + at]
            )
            copy.start()
            copies.append(copy)
            base += here.size
    for copy in copies:
        copy.wait()


def lay(place, parts, members, rows_of, before=()):
    wide = parts[0].shape[1]
    count = 1 + len(parts)
    return pl.pallas_call(
        functools.partial(lay_kernel, members, len(parts), bool(before)),
        in_specs=[scalars()] + [whole()] * len(parts) + [in_place()] * len(before),
        out_specs=[in_place()] * len(rows_of),
        out_shape=[jax.ShapeDtypeStruct((rows, 2 * wide), F32) for rows in rows_of],
        input_output_aliases={count + at: at for at in range(len(before))},
        scratch_shapes=[pltpu.VMEM((rows, wide), F32) for rows in rows_of]
        + [pltpu.SemaphoreType.DMA((2 * members,))],
        compiler_params=params(16),
        cost_estimate=cost(10**10, 10**8),
        name="lay",
    )(place, *parts, *before)


def exchange(array, axis, step):
    size = lax.axis_size(axis)
    return lax.ppermute(array, axis, [(source, source ^ step) for source in range(size)])


def added(*arrays):
    total = arrays[0].astype(F32)
    for array in arrays[1:]:
        total = total + array.astype(F32)
    return total.astype(BF16)


def route_of(n_clique, n_copy, turn):
    moves = [(0, 0), (3, 3), (1, 2), (2, 1)][turn] if n_clique == 4 else (turn, turn)
    return [
        (i * n_copy + j, (i ^ moves[j & 1]) * n_copy + j)
        for i in range(n_clique)
        for j in range(n_copy)
    ]


def trade(arrays):
    n_clique, n_copy = lax.axis_size("clique"), lax.axis_size("copy")
    return [arrays[0]] + [
        lax.ppermute(arrays[turn], ("clique", "copy"), route_of(n_clique, n_copy, turn))
        for turn in range(1, n_clique)
    ]


def sum_over_slice(shares, two):
    own = jnp.concatenate([added(*trade(shares)), two], axis=0)
    n_copy = lax.axis_size("copy")
    steps = [2 << bit for bit in range((n_copy // 2).bit_length() - 1)]
    for near, far in zip(steps, reversed(steps)):
        route = [(j, j ^ (far if j & 1 else near)) for j in range(n_copy)]
        own = added(own, lax.ppermute(own, "copy", route))
    return trade([own] * len(shares))


def gather(own, two):
    members = lax.axis_size("clique")
    rows = two.shape[0] // members
    shares = [two[k * rows : (k + 1) * rows] for k in range(members)]
    middle, d_in = own.shape[0] // 2, own.shape[1]
    if members != 4 or rows != middle:
        feats = [own] + [exchange(own, "clique", k) for k in range(1, members)]
        got = shares[:1] + [exchange(shares[k], "clique", k) for k in range(1, members)]
        return feats, added(*got)
    one, other = exchange(own, "clique", 1), exchange(own, "clique", 2)
    top = exchange(jnp.concatenate([other[:middle], shares[1]], axis=1), "clique", 1)
    bottom = exchange(jnp.concatenate([one[middle:], shares[2]], axis=1), "clique", 2)
    far = exchange(shares[3], "clique", 3)
    total = added(shares[0], top[:, d_in:], bottom[:, d_in:], far)
    return [own, one, other, top, bottom], total


def on_device(
    out_grad, pre_act, batch_count, layer_two, hot_slots, cold_index, hot_feats, cold_feats
):
    n_clique = lax.axis_size("clique")
    shard_rows, d_in = hot_feats.shape
    d_h = pre_act.shape[1]
    cold_rows = cold_feats.shape[0]
    fanout = hot_slots.shape[1] + cold_index.shape[1]
    copy_at = lax.axis_index("copy")
    place = jnp.stack([lax.axis_index("clique"), copy_at & 1]).astype(jnp.int32)

    half_feats = half_of(place, hot_feats)
    row_grad, own_two, twin_two, words = row_gradients(
        place, batch_count, out_grad, pre_act, layer_two, hot_slots.T, shard_rows * n_clique, shard_rows
    )
    two = added(own_two, exchange(twin_two, "copy", 1))
    feats, two = gather(half_feats, two)
    send, keep, words = hot_sums(words, row_grad, cold_index.T, cold_rows, fanout)
    other = exchange(send, "copy", 1)
    cold = cold_grad(words, row_grad, cold_feats, fanout)
    own_one, twin_one = join(place, cold, keep, other, feats)
    shares = pair_sums(place, own_one, exchange(twin_one, "copy", 1), n_clique)
    shares = sum_over_slice(shares, two)
    middle = n_clique // 2
    shares = [shares[turn] for turn in laid_turns(n_clique)]
    parts = [jnp.concatenate(part, axis=0) for part in (shares[:middle], shares[middle:])]
    others = [exchange(part, "copy", 1) for part in parts]
    rows_of = (d_in, d_h)
    own = lay(place, parts, n_clique, rows_of)
    return tuple(lay(place, others, n_clique, rows_of, own))


def solution(mesh):
    placed = (
        P(("clique", "copy"), None),
        P(("clique", "copy"), None),
        P(("clique", "copy")),
        P(),
        P(("clique", "copy"), None),
        P(("clique", "copy"), None),
        P("clique", None),
        P(("clique", "copy"), None),
    )
    return jax.shard_map(
        on_device, mesh=mesh, in_specs=placed, out_specs=(P(), P()), check_vma=False
    )
```

```python
import functools

import jax
import jax.numpy as jnp
from jax import lax
from jax.experimental import pallas as pl
from jax.experimental.pallas import tpu as pltpu
from jax.sharding import PartitionSpec as P

F32 = jnp.float32
BF16 = jnp.bfloat16
I16 = jnp.int16
FIELDS = 4
TILE = 16
HALF_MIB = 16
ROWS_MIB = 32


def whole():
    return pl.BlockSpec(memory_space=pltpu.VMEM)


def scalars():
    return pl.BlockSpec(memory_space=pltpu.SMEM)


def in_place():
    return pl.BlockSpec(memory_space=pl.ANY)


def params(mebibytes):
    return pltpu.CompilerParams(vmem_limit_bytes=mebibytes << 20)


def cost(flops, moved):
    return pl.CostEstimate(flops=int(flops), bytes_accessed=int(moved), transcendentals=0)


def transposed_dot(left, right):
    return lax.dot_general(left, right, (((0,), (0,)), ((), ())), preferred_element_type=F32)


def half_kernel(place_ref, feats_ref, half_ref):
    rows = half_ref.shape[0]
    here = pl.ds(pl.multiple_of(place_ref[1] * rows, TILE), rows)
    half_ref[...] = feats_ref[here, :]


def half_of(place, feats):
    rows, d_in = feats.shape
    return pl.pallas_call(
        half_kernel,
        in_specs=[scalars(), whole()],
        out_specs=whole(),
        out_shape=jax.ShapeDtypeStruct((rows // 2, d_in), BF16),
        compiler_params=params(HALF_MIB),
        cost_estimate=cost(10**10, 10**8),
        name="half_of",
    )(place, feats)


def halves(total_ref, own_ref, send_ref, own_shard, own_core, members):
    wide = own_ref.shape[1]
    mine = pl.ds(pl.multiple_of(own_core * wide, wide), wide)
    twin = pl.ds(pl.multiple_of((1 - own_core) * wide, wide), wide)
    rows = own_ref.shape[0] // members
    for member in range(members):
        here = slice(member * rows, (member + 1) * rows)
        there = pl.ds(pl.multiple_of((member ^ own_shard) * rows, TILE), rows)
        own_ref[there, :] = total_ref[here, mine].astype(BF16)
        send_ref[there, :] = total_ref[here, twin].astype(BF16)


def build_words(index, q_rows, store):
    terms = index.shape[0]
    shift = q_rows.bit_length() - 1
    low = index & (q_rows - 1)
    one = jnp.left_shift(jnp.ones_like(index), (index >> shift) * 4)
    spare = -terms % 8
    low = jnp.concatenate([low, jnp.full((spare, 128), -1, jnp.int32)], axis=0)
    one = jnp.concatenate([one, jnp.zeros((spare, 128), jnp.int32)], axis=0)
    unit = one
    for other in range(1, terms + spare):
        same = pltpu.roll(low, other, 0) == low
        unit = unit + jnp.where(same, pltpu.roll(one, other, 0), jnp.zeros_like(one))
    tall = min(256, q_rows) // TILE
    shape = (tall, TILE, 128)
    place = lax.broadcasted_iota(jnp.int32, shape, 0) * TILE + lax.broadcasted_iota(jnp.int32, shape, 1)
    place = place.astype(I16)

    def tile(row):
        return jnp.broadcast_to(row, (TILE, 128)).astype(I16)[None]

    lows = [tile(low[k : k + 1, :]) for k in range(terms)]
    units = [tile(unit[k : k + 1, :]) for k in range(terms)]
    for top in range(0, q_rows // TILE, tall):
        word = jnp.zeros(shape, I16)
        for k in range(terms):
            word = jnp.where(place == lows[k] - I16(top * TILE), units[k], word)
        store(top, tall, word)


def unpack(word_ref, field, lanes, count_ref):
    words = word_ref[:, :, lanes]
    if field < FIELDS - 1:
        counts = words & (15 << (4 * field))
    else:
        counts = (words >> (4 * field)) & 15
    count_ref[...] = counts.astype(BF16).reshape(count_ref.shape)


def unpacked_scale(field):
    return 16.0**field if field < FIELDS - 1 else 1.0


def rows_kernel(
    shard_bits, half_rows, chunks, members,
    place_ref, count_ref, index_ref, out_grad_ref, pre_act_ref, layer_two_ref,
    row_grad_ref, own_ref, send_ref, word_ref,
    masked_ref, sum_ref,
):
    rows = out_grad_ref.shape[0] // chunks
    blocks = [slice(chunk * rows, (chunk + 1) * rows) for chunk in range(chunks)]
    own_shard, own_core = place_ref[0], place_ref[1]
    part_bits = shard_bits - 1

    def build(tile):
        lanes = slice(tile * 128, (tile + 1) * 128)
        index = index_ref[:, lanes]
        row = index & ((1 << part_bits) - 1)
        half = ((index >> part_bits) & 1) ^ own_core ^ 1
        index = half * half_rows + (((index >> shard_bits) ^ own_shard) << part_bits) + row

        def store(top, tall, words):
            word_ref[top : top + tall, :, lanes] = words

        build_words(index, word_ref.shape[0] * TILE, store)

    tiles = row_grad_ref.shape[0] // 128
    ends = [tiles * chunk // chunks for chunk in range(chunks + 1)]
    for chunk, block in enumerate(blocks):
        live = count_ref[0] - chunk * rows

        @pl.when(live >= rows)
        def _(block=block):
            masked_ref[block, :] = out_grad_ref[block, :]

        @pl.when(live < rows)
        def _(block=block, live=live):
            out_grad = out_grad_ref[block, :].astype(F32)
            place = lax.broadcasted_iota(jnp.int32, out_grad.shape, 0)
            masked = jnp.where(place < live, out_grad, jnp.zeros_like(out_grad))
            masked_ref[block, :] = masked.astype(BF16)

    for chunk, block in enumerate(blocks):
        masked = masked_ref[block, :]
        pre_act = pre_act_ref[block, :]
        back = lax.dot_general(
            masked, layer_two_ref[...], (((1,), (1,)), ((), ())), preferred_element_type=F32
        )
        row_grad_ref[block, :] = jnp.where(
            pre_act.astype(F32) > 0, back, jnp.zeros_like(back)
        ).astype(BF16)
        activ = jnp.maximum(pre_act, jnp.zeros_like(pre_act))
        part = transposed_dot(activ, masked)
        sum_ref[...] = part if chunk == 0 else sum_ref[...] + part
        for tile in range(ends[chunk], ends[chunk + 1]):
            build(tile)
    halves(sum_ref, own_ref, send_ref, own_shard, own_core, members)


def row_gradients(place, batch_count, out_grad, pre_act, layer_two, index, hot_total, shard_rows):
    rows, d_out = out_grad.shape
    d_h = pre_act.shape[1]
    chunks = 4
    deep = hot_total // FIELDS // TILE
    half = jax.ShapeDtypeStruct((d_h, d_out // 2), BF16)
    return pl.pallas_call(
        functools.partial(
            rows_kernel,
            shard_rows.bit_length() - 1,
            hot_total // 2,
            chunks,
            hot_total // shard_rows,
        ),
        in_specs=[scalars(), scalars()] + [whole()] * 4,
        out_specs=[whole()] * 4,
        out_shape=[
            jax.ShapeDtypeStruct((rows, d_h), BF16),
            half,
            half,
            jax.ShapeDtypeStruct((deep, TILE, rows), I16),
        ],
        scratch_shapes=[
            pltpu.VMEM((rows, d_out), BF16),
            pltpu.VMEM((d_h, d_out), F32),
        ],
        compiler_params=params(ROWS_MIB),
        cost_estimate=cost(10**10, 10**8),
        name="row_gradients",
    )(place, batch_count, index, out_grad, pre_act, layer_two)


def build_tiles(index_ref, word_ref, first, count, word_first):
    for tile in range(count):
        here = slice((first + tile) * 128, (first + tile + 1) * 128)
        lanes = slice((word_first + tile) * 128, (word_first + tile + 1) * 128)

        def store(top, deep, words, lanes=lanes):
            word_ref[top : top + deep, :, lanes] = words

        build_words(index_ref[:, here], word_ref.shape[0] * TILE, store)


def hot_kernel(
    scale, word_in, row_grad_in, index_in, send_ref, keep_ref, cold_word_out,
    word_ref, row_grad_ref, index_ref, sums_ref, cold_word_ref, *counts
):
    word_ref[...] = word_in[...]
    row_grad_ref[...] = row_grad_in[...]
    index_ref[...] = index_in[...]
    tall, rows = counts[0].shape
    tiles = rows // 128 // 2 // FIELDS
    unpack(word_ref, 0, slice(None), counts[0])
    for field in range(FIELDS):
        found = jnp.dot(counts[field % 2][...], row_grad_ref[...], preferred_element_type=F32)
        found = found * (scale / unpacked_scale(field))
        sums_ref[field * tall : (field + 1) * tall, :] = found.astype(BF16)
        if field + 1 < FIELDS:
            unpack(word_ref, field + 1, slice(None), counts[(field + 1) % 2])
        build_tiles(index_ref, cold_word_ref, field * tiles, tiles, field * tiles)
    send_ref[...] = sums_ref[: 2 * tall, :]
    keep_ref[...] = sums_ref[2 * tall :, :]
    cold_word_out[...] = cold_word_ref[...]


def hot_sums(words, row_grad, cold_index, cold_rows, fanout):
    rows, d_h = row_grad.shape
    q_rows = words.shape[0] * TILE
    half = jax.ShapeDtypeStruct((q_rows * FIELDS // 2, d_h), BF16)
    return pl.pallas_call(
        functools.partial(hot_kernel, 1.0 / fanout),
        in_specs=[whole(), whole(), whole()],
        out_specs=[whole()] * 3,
        out_shape=[
            half,
            half,
            jax.ShapeDtypeStruct((cold_rows // FIELDS // TILE, TILE, rows // 2), I16),
        ],
        scratch_shapes=[
            pltpu.VMEM(words.shape, I16),
            pltpu.VMEM(row_grad.shape, BF16),
            pltpu.VMEM(cold_index.shape, jnp.int32),
            pltpu.VMEM((q_rows * FIELDS, d_h), BF16),
            pltpu.VMEM((cold_rows // FIELDS // TILE, TILE, rows // 2), I16),
            pltpu.VMEM((q_rows, rows), BF16),
            pltpu.VMEM((q_rows, rows), BF16),
        ],
        compiler_params=params(40),
        cost_estimate=cost(10**10, 10**8),
        name="hot_sums",
    )(words, row_grad, cold_index)


def cold_kernel(
    scale, word_in, index_in, row_grad_in, feats_ref, grad_out,
    word_ref, index_ref, row_grad_ref, grad_ref, part_ref, sums_ref, held_ref, sem, *counts
):
    fetch = pltpu.make_async_copy(feats_ref, held_ref, sem)
    fetch.start()
    tall, half = counts[0].shape
    word_ref[:, :, :half] = word_in[...]
    index_ref[...] = index_in[...]
    row_grad_ref[...] = row_grad_in[...]
    tiles = half // 128 // FIELDS

    def add_product(field):
        rows = slice(field * tall, (field + 1) * tall)
        part = transposed_dot(held_ref[rows, :], sums_ref[rows, :])
        grad_ref[...] = part if field == 0 else grad_ref[...] + part

    steps = [(k, field) for k in range(2) for field in range(FIELDS)]
    unpack(word_ref, 0, slice(half), counts[0])
    for step, (k, field) in enumerate(steps):
        depth, rows = slice(k * half, (k + 1) * half), slice(field * tall, (field + 1) * tall)
        found = jnp.dot(counts[step % 2][...], row_grad_ref[depth, :], preferred_element_type=F32)
        if k == 0:
            part_ref[rows, :] = found
            first = half // 128 + field * tiles
            build_tiles(index_ref, word_ref, first, tiles, first)
        else:
            found = (part_ref[rows, :] + found) * (scale / unpacked_scale(field))
            sums_ref[rows, :] = found.astype(BF16)
        if step + 1 < len(steps):
            ahead, next_field = steps[step + 1]
            lanes = slice(ahead * half, (ahead + 1) * half)
            unpack(word_ref, next_field, lanes, counts[(step + 1) % 2])
        if k == 1 and field == 0:
            fetch.wait()
        if k == 1 and field > 0:
            add_product(field - 1)
    add_product(FIELDS - 1)
    grad_out[...] = grad_ref[...]


def cold_grad(words, index, row_grad, feats, fanout):
    rows, d_h = row_grad.shape
    cold_rows, d_in = feats.shape
    q_rows = cold_rows // FIELDS
    return pl.pallas_call(
        functools.partial(cold_kernel, 1.0 / fanout),
        in_specs=[whole(), whole(), whole(), in_place()],
        out_specs=whole(),
        out_shape=jax.ShapeDtypeStruct((d_in, d_h), F32),
        scratch_shapes=[
            pltpu.VMEM((q_rows // TILE, TILE, rows), I16),
            pltpu.VMEM(index.shape, jnp.int32),
            pltpu.VMEM(row_grad.shape, BF16),
            pltpu.VMEM((d_in, d_h), F32),
            pltpu.VMEM((cold_rows, d_h), F32),
            pltpu.VMEM((cold_rows, d_h), BF16),
            pltpu.VMEM((cold_rows, d_in), BF16),
            pltpu.SemaphoreType.DMA,
            pltpu.VMEM((q_rows, rows // 2), BF16),
            pltpu.VMEM((q_rows, rows // 2), BF16),
        ],
        compiler_params=params(40),
        cost_estimate=cost(10**10, 10**8),
        name="cold_grad",
    )(words, index, row_grad, feats)


def join_kernel(parts, place_ref, cold_ref, keep_ref, other_ref, *rest):
    feats, (own_ref, send_ref, sums_ref, held_ref, total_ref) = rest[:parts], rest[parts:]
    d_in, wide = own_ref.shape
    sums = keep_ref[...].astype(F32) + other_ref[...].astype(F32)
    sums_ref[...] = sums.astype(BF16)
    base = 0
    for part in feats:
        held_ref[base : base + part.shape[0], :] = part[:, :d_in]
        base += part.shape[0]
    total_ref[...] = cold_ref[...]
    for left in range(0, d_in, 256):
        rows = slice(left, left + 256)
        total_ref[rows, :] += transposed_dot(held_ref[:, rows], sums_ref[...])
    total = total_ref[...].astype(BF16)
    store_halves(total, slice(None), place_ref[1], own_ref, send_ref)


def store_halves(total, rows, own_core, own_ref, send_ref):
    wide = own_ref.shape[1]
    first, second = total[:, :wide], total[:, wide:]

    @pl.when(own_core == 0)
    def _():
        own_ref[rows, :] = first
        send_ref[rows, :] = second

    @pl.when(own_core == 1)
    def _():
        own_ref[rows, :] = second
        send_ref[rows, :] = first


def join(place, cold, keep, other, feats):
    d_in, d_h = cold.shape
    half = jax.ShapeDtypeStruct((d_in, d_h // 2), BF16)
    return pl.pallas_call(
        functools.partial(join_kernel, len(feats)),
        in_specs=[scalars()] + [whole()] * (3 + len(feats)),
        out_specs=[whole()] * 2,
        out_shape=[half, half],
        scratch_shapes=[
            pltpu.VMEM(keep.shape, BF16),
            pltpu.VMEM((keep.shape[0], d_in), BF16),
            pltpu.VMEM((d_in, d_h), F32),
        ],
        compiler_params=params(32),
        cost_estimate=cost(2 * keep.shape[0] * d_h * d_in, 4 * d_in * d_h),
        name="join",
    )(place, cold, keep, other, *feats)


def share_rows(rows, members, place_ref, core, turn):
    size = rows // members
    partner = turn
    if members == 4 and turn == 1:
        partner = 3
    elif members == 4 and turn > 1:
        partner = jnp.where(core == 0, turn - 1, 4 - turn)
    return pl.ds(pl.multiple_of((place_ref[0] ^ partner) * size, TILE), size)


def pair_kernel(place_ref, one_ref, other_ref, *out_refs):
    members = len(out_refs)
    for k, out_ref in enumerate(out_refs):
        here = share_rows(one_ref.shape[0], members, place_ref, place_ref[1], k)
        total = one_ref[here, :].astype(F32) + other_ref[here, :].astype(F32)
        out_ref[...] = total.astype(BF16)


def pair_sums(place, one, other, members):
    rows, wide = one.shape
    share = jax.ShapeDtypeStruct((rows // members, wide), BF16)
    return pl.pallas_call(
        pair_kernel,
        in_specs=[scalars()] + [whole()] * 2,
        out_specs=[whole()] * members,
        out_shape=[share] * members,
        compiler_params=params(16),
        cost_estimate=cost(0, 6 * rows * wide),
        name="pair_sums",
    )(place, one, other)


def laid_turns(members):
    return [0, members - 1, *range(1, members - 1)]


def lay_kernel(members, parts, twin, place_ref, *refs):
    halves_in, refs = refs[:parts], refs[parts:]
    refs = refs[2:] if twin else refs
    outs, held, sems = refs[:2], refs[2:4], refs[4]
    core = 1 - place_ref[1] if twin else place_ref[1]
    wide = halves_in[0].shape[1]
    lanes = pl.ds(pl.multiple_of(core * wide, wide), wide)
    each = members // parts
    copies = []
    for k, turn in enumerate(laid_turns(members)):
        base = k % each * (halves_in[0].shape[0] // each)
        for at, (out_ref, held_ref) in enumerate(zip(outs, held)):
            here = share_rows(out_ref.shape[0], members, place_ref, core, turn)
            held_ref[here, :] = halves_in[k // each][base : base + here.size, :].astype(F32)
            copy = pltpu.make_async_copy(
                held_ref.at[here, :], out_ref.at[here, lanes], sems.at[2 * k + at]
            )
            copy.start()
            copies.append(copy)
            base += here.size
    for copy in copies:
        copy.wait()


def lay(place, parts, members, rows_of, before=()):
    wide = parts[0].shape[1]
    count = 1 + len(parts)
    return pl.pallas_call(
        functools.partial(lay_kernel, members, len(parts), bool(before)),
        in_specs=[scalars()] + [whole()] * len(parts) + [in_place()] * len(before),
        out_specs=[in_place()] * len(rows_of),
        out_shape=[jax.ShapeDtypeStruct((rows, 2 * wide), F32) for rows in rows_of],
        input_output_aliases={count + at: at for at in range(len(before))},
        scratch_shapes=[pltpu.VMEM((rows, wide), F32) for rows in rows_of]
        + [pltpu.SemaphoreType.DMA((2 * members,))],
        compiler_params=params(16),
        cost_estimate=cost(10**10, 10**8),
        name="lay",
    )(place, *parts, *before)


def exchange(array, axis, step):
    size = lax.axis_size(axis)
    return lax.ppermute(array, axis, [(source, source ^ step) for source in range(size)])


def added(*arrays):
    total = arrays[0].astype(F32)
    for array in arrays[1:]:
        total = total + array.astype(F32)
    return total.astype(BF16)


def route_of(n_clique, n_copy, turn):
    moves = [(0, 0), (3, 3), (1, 2), (2, 1)][turn] if n_clique == 4 else (turn, turn)
    return [
        (i * n_copy + j, (i ^ moves[j & 1]) * n_copy + j)
        for i in range(n_clique)
        for j in range(n_copy)
    ]


def trade(arrays):
    n_clique, n_copy = lax.axis_size("clique"), lax.axis_size("copy")
    return [arrays[0]] + [
        lax.ppermute(arrays[turn], ("clique", "copy"), route_of(n_clique, n_copy, turn))
        for turn in range(1, n_clique)
    ]


def sum_over_slice(shares, two):
    own = jnp.concatenate([added(*trade(shares)), two], axis=0)
    n_copy = lax.axis_size("copy")
    steps = [2 << bit for bit in range((n_copy // 2).bit_length() - 1)]
    for near, far in zip(steps, reversed(steps)):
        route = [(j, j ^ (far if j & 1 else near)) for j in range(n_copy)]
        own = added(own, lax.ppermute(own, "copy", route))
    return trade([own] * len(shares))


def gather(own, two):
    members = lax.axis_size("clique")
    rows = two.shape[0] // members
    shares = [two[k * rows : (k + 1) * rows] for k in range(members)]
    middle, d_in = own.shape[0] // 2, own.shape[1]
    if members != 4 or rows != middle:
        feats = [own] + [exchange(own, "clique", k) for k in range(1, members)]
        got = shares[:1] + [exchange(shares[k], "clique", k) for k in range(1, members)]
        return feats, added(*got)
    one, other = exchange(own, "clique", 1), exchange(own, "clique", 2)
    top = exchange(jnp.concatenate([other[:middle], shares[1]], axis=1), "clique", 1)
    bottom = exchange(jnp.concatenate([one[middle:], shares[2]], axis=1), "clique", 2)
    far = exchange(shares[3], "clique", 3)
    total = added(shares[0], top[:, d_in:], bottom[:, d_in:], far)
    return [own, one, other, top, bottom], total


def on_device(
    out_grad, pre_act, batch_count, layer_two, hot_slots, cold_index, hot_feats, cold_feats
):
    n_clique = lax.axis_size("clique")
    shard_rows, d_in = hot_feats.shape
    d_h = pre_act.shape[1]
    cold_rows = cold_feats.shape[0]
    fanout = hot_slots.shape[1] + cold_index.shape[1]
    copy_at = lax.axis_index("copy")
    place = jnp.stack([lax.axis_index("clique"), copy_at & 1]).astype(jnp.int32)

    half_feats = half_of(place, hot_feats)
    row_grad, own_two, twin_two, words = row_gradients(
        place, batch_count, out_grad, pre_act, layer_two, hot_slots.T, shard_rows * n_clique, shard_rows
    )
    two = added(own_two, exchange(twin_two, "copy", 1))
    feats, two = gather(half_feats, two)
    send, keep, words = hot_sums(words, row_grad, cold_index.T, cold_rows, fanout)
    other = exchange(send, "copy", 1)
    cold = cold_grad(words, cold_index.T, row_grad, cold_feats, fanout)
    own_one, twin_one = join(place, cold, keep, other, feats)
    shares = pair_sums(place, own_one, exchange(twin_one, "copy", 1), n_clique)
    shares = sum_over_slice(shares, two)
    middle = n_clique // 2
    shares = [shares[turn] for turn in laid_turns(n_clique)]
    parts = [jnp.concatenate(part, axis=0) for part in (shares[:middle], shares[middle:])]
    others = [exchange(part, "copy", 1) for part in parts]
    rows_of = (d_in, d_h)
    own = lay(place, parts, n_clique, rows_of)
    return tuple(lay(place, others, n_clique, rows_of, own))


def solution(mesh):
    placed = (
        P(("clique", "copy"), None),
        P(("clique", "copy"), None),
        P(("clique", "copy")),
        P(),
        P(("clique", "copy"), None),
        P(("clique", "copy"), None),
        P("clique", None),
        P(("clique", "copy"), None),
    )
    return jax.shard_map(
        on_device, mesh=mesh, in_specs=placed, out_specs=(P(), P()), check_vma=False
    )
```

```python
import functools

import jax
import jax.numpy as jnp
from jax import lax
from jax.experimental import pallas as pl
from jax.experimental.pallas import tpu as pltpu
from jax.sharding import PartitionSpec as P

F32 = jnp.float32
BF16 = jnp.bfloat16
I16 = jnp.int16
FIELDS = 4
TILE = 16
HALF_MIB = 16
ROWS_MIB = 32


def whole():
    return pl.BlockSpec(memory_space=pltpu.VMEM)


def scalars():
    return pl.BlockSpec(memory_space=pltpu.SMEM)


def in_place():
    return pl.BlockSpec(memory_space=pl.ANY)


def params(mebibytes):
    return pltpu.CompilerParams(vmem_limit_bytes=mebibytes << 20)


def cost(flops, moved):
    return pl.CostEstimate(flops=int(flops), bytes_accessed=int(moved), transcendentals=0)


def transposed_dot(left, right):
    return lax.dot_general(left, right, (((0,), (0,)), ((), ())), preferred_element_type=F32)


def half_kernel(place_ref, feats_ref, half_ref):
    rows = half_ref.shape[0]
    here = pl.ds(pl.multiple_of(place_ref[1] * rows, TILE), rows)
    half_ref[...] = feats_ref[here, :]


def half_of(place, feats):
    rows, d_in = feats.shape
    return pl.pallas_call(
        half_kernel,
        in_specs=[scalars(), whole()],
        out_specs=whole(),
        out_shape=jax.ShapeDtypeStruct((rows // 2, d_in), BF16),
        compiler_params=params(HALF_MIB),
        cost_estimate=cost(10**10, 10**8),
        name="half_of",
    )(place, feats)


def halves(total_ref, own_ref, send_ref, own_shard, own_core, members):
    wide = own_ref.shape[1]
    mine = pl.ds(pl.multiple_of(own_core * wide, wide), wide)
    twin = pl.ds(pl.multiple_of((1 - own_core) * wide, wide), wide)
    rows = own_ref.shape[0] // members
    for member in range(members):
        here = slice(member * rows, (member + 1) * rows)
        there = pl.ds(pl.multiple_of((member ^ own_shard) * rows, TILE), rows)
        own_ref[there, :] = total_ref[here, mine].astype(BF16)
        send_ref[there, :] = total_ref[here, twin].astype(BF16)


def build_words(index, q_rows, store):
    terms = index.shape[0]
    shift = q_rows.bit_length() - 1
    low = index & (q_rows - 1)
    one = jnp.left_shift(jnp.ones_like(index), (index >> shift) * 4)
    spare = -terms % 8 if -terms % 8 < 3 else 0
    if spare == 0 and terms % 8:
        turn = lambda array, by: jnp.concatenate([array[by:], array[:by]], axis=0)
    else:
        turn = lambda array, by: pltpu.roll(array, by, 0)
    if spare:
        low = jnp.concatenate([low, jnp.full((spare, 128), -1, jnp.int32)], axis=0)
        one = jnp.concatenate([one, jnp.zeros((spare, 128), jnp.int32)], axis=0)
    unit = one
    for other in range(1, terms + spare):
        unit = unit + jnp.where(turn(low, other) == low, turn(one, other), jnp.zeros_like(one))
    tall = min(256, q_rows) // TILE
    shape = (tall, TILE, 128)
    place = lax.broadcasted_iota(jnp.int32, shape, 0) * TILE + lax.broadcasted_iota(jnp.int32, shape, 1)
    place = place.astype(I16)

    def tile(row):
        return jnp.broadcast_to(row, (TILE, 128)).astype(I16)[None]

    lows = [tile(low[k : k + 1, :]) for k in range(terms)]
    units = [tile(unit[k : k + 1, :]) for k in range(terms)]
    for top in range(0, q_rows // TILE, tall):
        word = jnp.zeros(shape, I16)
        for k in range(terms):
            word = jnp.where(place == lows[k] - I16(top * TILE), units[k], word)
        store(top, tall, word)


def unpack(word_ref, field, lanes, count_ref, part=0, parts=1):
    deep = word_ref.shape[0] // parts
    words = word_ref[part * deep : (part + 1) * deep, :, lanes]
    if field < FIELDS - 1:
        counts = words & (15 << (4 * field))
    else:
        counts = (words >> (4 * field)) & 15
    rows = slice(part * deep * TILE, (part + 1) * deep * TILE)
    count_ref[rows, :] = counts.astype(BF16).reshape(deep * TILE, count_ref.shape[1])


def unpacked_scale(field):
    return 16.0**field if field < FIELDS - 1 else 1.0


def rows_kernel(
    shard_bits, half_rows, chunks, members,
    place_ref, count_ref, index_ref, out_grad_ref, pre_act_ref, layer_two_ref,
    row_grad_ref, own_ref, send_ref, word_ref,
    masked_ref, sum_ref,
):
    rows = out_grad_ref.shape[0] // chunks
    blocks = [slice(chunk * rows, (chunk + 1) * rows) for chunk in range(chunks)]
    own_shard, own_core = place_ref[0], place_ref[1]
    part_bits = shard_bits - 1

    def build(tile):
        lanes = slice(tile * 128, (tile + 1) * 128)
        index = index_ref[:, lanes]
        row = index & ((1 << part_bits) - 1)
        half = ((index >> part_bits) & 1) ^ own_core ^ 1
        index = half * half_rows + (((index >> shard_bits) ^ own_shard) << part_bits) + row

        def store(top, tall, words):
            word_ref[top : top + tall, :, lanes] = words

        build_words(index, word_ref.shape[0] * TILE, store)

    tiles = row_grad_ref.shape[0] // 128
    ends = [tiles * chunk // chunks for chunk in range(chunks + 1)]
    for chunk, block in enumerate(blocks):
        live = count_ref[0] - chunk * rows

        @pl.when(live >= rows)
        def _(block=block):
            masked_ref[block, :] = out_grad_ref[block, :]

        @pl.when(live < rows)
        def _(block=block, live=live):
            out_grad = out_grad_ref[block, :].astype(F32)
            place = lax.broadcasted_iota(jnp.int32, out_grad.shape, 0)
            masked = jnp.where(place < live, out_grad, jnp.zeros_like(out_grad))
            masked_ref[block, :] = masked.astype(BF16)

    for chunk, block in enumerate(blocks):
        masked = masked_ref[block, :]
        pre_act = pre_act_ref[block, :]
        back = lax.dot_general(
            masked, layer_two_ref[...], (((1,), (1,)), ((), ())), preferred_element_type=F32
        )
        row_grad_ref[block, :] = jnp.where(
            pre_act.astype(F32) > 0, back, jnp.zeros_like(back)
        ).astype(BF16)
        activ = jnp.maximum(pre_act, jnp.zeros_like(pre_act))
        part = transposed_dot(activ, masked)
        sum_ref[...] = part if chunk == 0 else sum_ref[...] + part
        for tile in range(ends[chunk], ends[chunk + 1]):
            build(tile)
    halves(sum_ref, own_ref, send_ref, own_shard, own_core, members)


def row_gradients(place, batch_count, out_grad, pre_act, layer_two, index, hot_total, shard_rows):
    rows, d_out = out_grad.shape
    d_h = pre_act.shape[1]
    chunks = 4
    deep = hot_total // FIELDS // TILE
    half = jax.ShapeDtypeStruct((d_h, d_out // 2), BF16)
    return pl.pallas_call(
        functools.partial(
            rows_kernel,
            shard_rows.bit_length() - 1,
            hot_total // 2,
            chunks,
            hot_total // shard_rows,
        ),
        in_specs=[scalars(), scalars()] + [whole()] * 4,
        out_specs=[whole()] * 4,
        out_shape=[
            jax.ShapeDtypeStruct((rows, d_h), BF16),
            half,
            half,
            jax.ShapeDtypeStruct((deep, TILE, rows), I16),
        ],
        scratch_shapes=[
            pltpu.VMEM((rows, d_out), BF16),
            pltpu.VMEM((d_h, d_out), F32),
        ],
        compiler_params=params(ROWS_MIB),
        cost_estimate=cost(10**10, 10**8),
        name="row_gradients",
    )(place, batch_count, index, out_grad, pre_act, layer_two)


def build_tiles(index_ref, word_ref, first, count, word_first):
    for tile in range(count):
        here = slice((first + tile) * 128, (first + tile + 1) * 128)
        lanes = slice((word_first + tile) * 128, (word_first + tile + 1) * 128)

        def store(top, deep, words, lanes=lanes):
            word_ref[top : top + deep, :, lanes] = words

        build_words(index_ref[:, here], word_ref.shape[0] * TILE, store)


def hot_kernel(
    scale, word_in, row_grad_in, index_in, send_ref, keep_ref, cold_word_out,
    word_ref, row_grad_ref, index_ref, sums_ref, cold_word_ref, *counts
):
    word_ref[...] = word_in[...]
    row_grad_ref[...] = row_grad_in[...]
    index_ref[...] = index_in[...]
    tall, rows = counts[0].shape
    tiles = rows // 128 // 2 // FIELDS // 2
    wide = row_grad_ref.shape[1] // 2
    unpack(word_ref, 0, slice(None), counts[0])
    for field in range(FIELDS):
        for part in range(2):
            lanes = slice(part * wide, (part + 1) * wide)
            found = jnp.dot(
                counts[field % 2][...], row_grad_ref[:, lanes], preferred_element_type=F32
            )
            found = found * (scale / unpacked_scale(field))
            sums_ref[field * tall : (field + 1) * tall, lanes] = found.astype(BF16)
            if field + 1 < FIELDS:
                unpack(word_ref, field + 1, slice(None), counts[(field + 1) % 2], part, 2)
            first = (2 * field + part) * tiles
            build_tiles(index_ref, cold_word_ref, first, tiles, first)
    send_ref[...] = sums_ref[: 2 * tall, :]
    keep_ref[...] = sums_ref[2 * tall :, :]
    cold_word_out[...] = cold_word_ref[...]


def hot_sums(words, row_grad, cold_index, cold_rows, fanout):
    rows, d_h = row_grad.shape
    q_rows = words.shape[0] * TILE
    half = jax.ShapeDtypeStruct((q_rows * FIELDS // 2, d_h), BF16)
    return pl.pallas_call(
        functools.partial(hot_kernel, 1.0 / fanout),
        in_specs=[whole(), whole(), whole()],
        out_specs=[whole()] * 3,
        out_shape=[
            half,
            half,
            jax.ShapeDtypeStruct((cold_rows // FIELDS // TILE, TILE, rows // 2), I16),
        ],
        scratch_shapes=[
            pltpu.VMEM(words.shape, I16),
            pltpu.VMEM(row_grad.shape, BF16),
            pltpu.VMEM(cold_index.shape, jnp.int32),
            pltpu.VMEM((q_rows * FIELDS, d_h), BF16),
            pltpu.VMEM((cold_rows // FIELDS // TILE, TILE, rows // 2), I16),
            pltpu.VMEM((q_rows, rows), BF16),
            pltpu.VMEM((q_rows, rows), BF16),
        ],
        compiler_params=params(40),
        cost_estimate=cost(10**10, 10**8),
        name="hot_sums",
    )(words, row_grad, cold_index)


def cold_kernel(
    scale, word_in, index_in, row_grad_in, feats_ref, grad_out,
    word_ref, index_ref, row_grad_ref, grad_ref, part_ref, sums_ref, held_ref, sem, *counts
):
    fetch = pltpu.make_async_copy(feats_ref, held_ref, sem)
    fetch.start()
    tall, half = counts[0].shape
    word_ref[:, :, :half] = word_in[...]
    index_ref[...] = index_in[...]
    row_grad_ref[...] = row_grad_in[...]
    tiles = half // 128 // FIELDS // 2
    wide, deep = row_grad_ref.shape[1] // 2, held_ref.shape[1] // 2

    def add_product(field, part):
        rows, lanes = slice(field * tall, (field + 1) * tall), slice(part * deep, (part + 1) * deep)
        found = transposed_dot(held_ref[rows, lanes], sums_ref[rows, :])
        grad_ref[lanes, :] = found if field == 0 else grad_ref[lanes, :] + found

    steps = [(k, field) for k in range(2) for field in range(FIELDS)]
    unpack(word_ref, 0, slice(half), counts[0])
    for step, (k, field) in enumerate(steps):
        if step == FIELDS + 1:
            fetch.wait()
        depth, rows = slice(k * half, (k + 1) * half), slice(field * tall, (field + 1) * tall)
        for part in range(2):
            lanes = slice(part * wide, (part + 1) * wide)
            found = jnp.dot(
                counts[step % 2][...], row_grad_ref[depth, lanes], preferred_element_type=F32
            )
            if k == 0:
                part_ref[rows, lanes] = found
                first = half // 128 + (2 * field + part) * tiles
                build_tiles(index_ref, word_ref, first, tiles, first)
            else:
                found = (part_ref[rows, lanes] + found) * (scale / unpacked_scale(field))
                sums_ref[rows, lanes] = found.astype(BF16)
            if step + 1 < len(steps) and (step + 1 != FIELDS or part == 1):
                ahead, next_field = steps[step + 1]
                there = slice(ahead * half, (ahead + 1) * half)
                at = (0, 1) if step + 1 == FIELDS else (part, 2)
                unpack(word_ref, next_field, there, counts[(step + 1) % 2], *at)
            if k == 1 and field > 0:
                add_product(field - 1, part)
    for part in range(2):
        add_product(FIELDS - 1, part)
    grad_out[...] = grad_ref[...]


def cold_grad(words, index, row_grad, feats, fanout):
    rows, d_h = row_grad.shape
    cold_rows, d_in = feats.shape
    q_rows = cold_rows // FIELDS
    return pl.pallas_call(
        functools.partial(cold_kernel, 1.0 / fanout),
        in_specs=[whole(), whole(), whole(), in_place()],
        out_specs=whole(),
        out_shape=jax.ShapeDtypeStruct((d_in, d_h), F32),
        scratch_shapes=[
            pltpu.VMEM((q_rows // TILE, TILE, rows), I16),
            pltpu.VMEM(index.shape, jnp.int32),
            pltpu.VMEM(row_grad.shape, BF16),
            pltpu.VMEM((d_in, d_h), F32),
            pltpu.VMEM((cold_rows, d_h), F32),
            pltpu.VMEM((cold_rows, d_h), BF16),
            pltpu.VMEM((cold_rows, d_in), BF16),
            pltpu.SemaphoreType.DMA,
            pltpu.VMEM((q_rows, rows // 2), BF16),
            pltpu.VMEM((q_rows, rows // 2), BF16),
        ],
        compiler_params=params(40),
        cost_estimate=cost(10**10, 10**8),
        name="cold_grad",
    )(words, index, row_grad, feats)


def join_kernel(parts, place_ref, cold_ref, keep_ref, other_ref, *rest):
    feats, (own_ref, send_ref, sums_ref, held_ref, total_ref) = rest[:parts], rest[-5:]
    d_in, wide = own_ref.shape
    sums = keep_ref[...].astype(F32) + other_ref[...].astype(F32)
    sums_ref[...] = sums.astype(BF16)
    base = 0
    for part in feats:
        held_ref[base : base + part.shape[0], :] = part[:, :d_in]
        base += part.shape[0]
    total_ref[...] = cold_ref[...]
    for left in range(0, d_in, 256):
        rows = slice(left, left + 256)
        total_ref[rows, :] += transposed_dot(held_ref[:, rows], sums_ref[...])
    total = total_ref[...].astype(BF16)
    store_halves(total, slice(None), place_ref[1], own_ref, send_ref)


def store_halves(total, rows, own_core, own_ref, send_ref):
    wide = own_ref.shape[1]
    first, second = total[:, :wide], total[:, wide:]

    @pl.when(own_core == 0)
    def _():
        own_ref[rows, :] = first
        send_ref[rows, :] = second

    @pl.when(own_core == 1)
    def _():
        own_ref[rows, :] = second
        send_ref[rows, :] = first


def join(place, cold, keep, other, feats, arrived):
    d_in, d_h = cold.shape
    half = jax.ShapeDtypeStruct((d_in, d_h // 2), BF16)
    return pl.pallas_call(
        functools.partial(join_kernel, len(feats)),
        in_specs=[scalars()] + [whole()] * (3 + len(feats)) + [in_place()],
        out_specs=[whole()] * 2,
        out_shape=[half, half],
        scratch_shapes=[
            pltpu.VMEM(keep.shape, BF16),
            pltpu.VMEM((keep.shape[0], d_in), BF16),
            pltpu.VMEM((d_in, d_h), F32),
        ],
        compiler_params=params(32),
        cost_estimate=cost(2 * keep.shape[0] * d_h * d_in, 4 * d_in * d_h),
        name="join",
    )(place, cold, keep, other, *feats, arrived)


def share_rows(rows, members, place_ref, core, turn):
    size = rows // members
    partner = turn
    if members == 4 and turn == 1:
        partner = 3
    elif members == 4 and turn > 1:
        partner = jnp.where(core == 0, turn - 1, 4 - turn)
    return pl.ds(pl.multiple_of((place_ref[0] ^ partner) * size, TILE), size)


def pair_kernel(place_ref, one_ref, other_ref, *out_refs):
    members = len(out_refs)
    for k, out_ref in enumerate(out_refs):
        here = share_rows(one_ref.shape[0], members, place_ref, place_ref[1], k)
        total = one_ref[here, :].astype(F32) + other_ref[here, :].astype(F32)
        out_ref[...] = total.astype(BF16)


def pair_sums(place, one, other, members):
    rows, wide = one.shape
    share = jax.ShapeDtypeStruct((rows // members, wide), BF16)
    return pl.pallas_call(
        pair_kernel,
        in_specs=[scalars()] + [whole()] * 2,
        out_specs=[whole()] * members,
        out_shape=[share] * members,
        compiler_params=params(16),
        cost_estimate=cost(0, 6 * rows * wide),
        name="pair_sums",
    )(place, one, other)


def laid_turns(members):
    return [0, members - 1, *range(1, members - 1)]


def lay_kernel(members, parts, twin, place_ref, *refs):
    halves_in, refs = refs[:parts], refs[parts:]
    refs = refs[2:] if twin else refs
    outs, held, sems = refs[:2], refs[2:4], refs[4]
    core = 1 - place_ref[1] if twin else place_ref[1]
    wide = halves_in[0].shape[1]
    lanes = pl.ds(pl.multiple_of(core * wide, wide), wide)
    each = members // parts
    copies = []
    for k, turn in enumerate(laid_turns(members)):
        base = k % each * (halves_in[0].shape[0] // each)
        for at, (out_ref, held_ref) in enumerate(zip(outs, held)):
            here = share_rows(out_ref.shape[0], members, place_ref, core, turn)
            held_ref[here, :] = halves_in[k // each][base : base + here.size, :].astype(F32)
            copy = pltpu.make_async_copy(
                held_ref.at[here, :], out_ref.at[here, lanes], sems.at[2 * k + at]
            )
            copy.start()
            copies.append(copy)
            base += here.size
    for copy in copies:
        copy.wait()


def lay(place, parts, members, rows_of, before=()):
    wide = parts[0].shape[1]
    count = 1 + len(parts)
    return pl.pallas_call(
        functools.partial(lay_kernel, members, len(parts), bool(before)),
        in_specs=[scalars()] + [whole()] * len(parts) + [in_place()] * len(before),
        out_specs=[in_place()] * len(rows_of),
        out_shape=[jax.ShapeDtypeStruct((rows, 2 * wide), F32) for rows in rows_of],
        input_output_aliases={count + at: at for at in range(len(before))},
        scratch_shapes=[pltpu.VMEM((rows, wide), F32) for rows in rows_of]
        + [pltpu.SemaphoreType.DMA((2 * members,))],
        compiler_params=params(16),
        cost_estimate=cost(10**10, 10**8),
        name="lay",
    )(place, *parts, *before)


def exchange(array, axis, step):
    size = lax.axis_size(axis)
    return lax.ppermute(array, axis, [(source, source ^ step) for source in range(size)])


def added(*arrays):
    total = arrays[0].astype(F32)
    for array in arrays[1:]:
        total = total + array.astype(F32)
    return total.astype(BF16)


def route_of(n_clique, n_copy, turn):
    moves = [(0, 0), (3, 3), (1, 2), (2, 1)][turn] if n_clique == 4 else (turn, turn)
    return [
        (i * n_copy + j, (i ^ moves[j & 1]) * n_copy + j)
        for i in range(n_clique)
        for j in range(n_copy)
    ]


def trade(arrays):
    n_clique, n_copy = lax.axis_size("clique"), lax.axis_size("copy")
    return [arrays[0]] + [
        lax.ppermute(arrays[turn], ("clique", "copy"), route_of(n_clique, n_copy, turn))
        for turn in range(1, n_clique)
    ]


def sum_over_slice(shares, two):
    own = jnp.concatenate([added(*trade(shares)), two], axis=0)
    n_copy = lax.axis_size("copy")
    steps = [2 << bit for bit in range((n_copy // 2).bit_length() - 1)]
    for near, far in zip(steps, reversed(steps)):
        route = [(j, j ^ (far if j & 1 else near)) for j in range(n_copy)]
        own = added(own, lax.ppermute(own, "copy", route))
    return trade([own] * len(shares))


def gather(own, two):
    members = lax.axis_size("clique")
    rows = two.shape[0] // members
    shares = [two[k * rows : (k + 1) * rows] for k in range(members)]
    middle, d_in = own.shape[0] // 2, own.shape[1]
    if members != 4 or rows != middle:
        feats = [own] + [exchange(own, "clique", k) for k in range(1, members)]
        got = shares[:1] + [exchange(shares[k], "clique", k) for k in range(1, members)]
        return feats, added(*got)
    one, other = exchange(own, "clique", 1), exchange(own, "clique", 2)
    top = exchange(jnp.concatenate([other[:middle], shares[1]], axis=1), "clique", 1)
    bottom = exchange(jnp.concatenate([one[middle:], shares[2]], axis=1), "clique", 2)
    far = exchange(shares[3], "clique", 3)
    total = added(shares[0], top[:, d_in:], bottom[:, d_in:], far)
    return [own, one, other, top, bottom], total


def on_device(
    out_grad, pre_act, batch_count, layer_two, hot_slots, cold_index, hot_feats, cold_feats
):
    n_clique = lax.axis_size("clique")
    shard_rows, d_in = hot_feats.shape
    d_h = pre_act.shape[1]
    cold_rows = cold_feats.shape[0]
    fanout = hot_slots.shape[1] + cold_index.shape[1]
    copy_at = lax.axis_index("copy")
    place = jnp.stack([lax.axis_index("clique"), copy_at & 1]).astype(jnp.int32)

    half_feats = half_of(place, hot_feats)
    row_grad, own_two, twin_two, words = row_gradients(
        place, batch_count, out_grad, pre_act, layer_two, hot_slots.T, shard_rows * n_clique, shard_rows
    )
    two = added(own_two, exchange(twin_two, "copy", 1))
    feats, two = gather(half_feats, two)
    send, keep, words = hot_sums(words, row_grad, cold_index.T, cold_rows, fanout)
    other = exchange(send, "copy", 1)
    cold = cold_grad(words, cold_index.T, row_grad, cold_feats, fanout)
    own_one, twin_one = join(place, cold, keep, other, feats, two)
    shares = pair_sums(place, own_one, exchange(twin_one, "copy", 1), n_clique)
    shares = sum_over_slice(shares, two)
    middle = n_clique // 2
    shares = [shares[turn] for turn in laid_turns(n_clique)]
    parts = [jnp.concatenate(part, axis=0) for part in (shares[:middle], shares[middle:])]
    others = [exchange(part, "copy", 1) for part in parts]
    rows_of = (d_in, d_h)
    own = lay(place, parts, n_clique, rows_of)
    return tuple(lay(place, others, n_clique, rows_of, own))


def solution(mesh):
    placed = (
        P(("clique", "copy"), None),
        P(("clique", "copy"), None),
        P(("clique", "copy")),
        P(),
        P(("clique", "copy"), None),
        P(("clique", "copy"), None),
        P("clique", None),
        P(("clique", "copy"), None),
    )
    return jax.shard_map(
        on_device, mesh=mesh, in_specs=placed, out_specs=(P(), P()), check_vma=False
    )
```

```python
import functools

import jax
import jax.numpy as jnp
from jax import lax
from jax.experimental import pallas as pl
from jax.experimental.pallas import tpu as pltpu
from jax.sharding import PartitionSpec as P

F32 = jnp.float32
BF16 = jnp.bfloat16
I16 = jnp.int16
FIELDS = 4
TILE = 16
HALF_MIB = 16
ROWS_MIB = 32


def whole():
    return pl.BlockSpec(memory_space=pltpu.VMEM)


def scalars():
    return pl.BlockSpec(memory_space=pltpu.SMEM)


def in_place():
    return pl.BlockSpec(memory_space=pl.ANY)


def params(mebibytes):
    return pltpu.CompilerParams(vmem_limit_bytes=mebibytes << 20)


def cost(flops, moved):
    return pl.CostEstimate(flops=int(flops), bytes_accessed=int(moved), transcendentals=0)


def transposed_dot(left, right):
    return lax.dot_general(left, right, (((0,), (0,)), ((), ())), preferred_element_type=F32)


def half_kernel(place_ref, feats_ref, half_ref):
    rows = half_ref.shape[0]
    here = pl.ds(pl.multiple_of(place_ref[1] * rows, TILE), rows)
    half_ref[...] = feats_ref[here, :]


def half_of(place, feats):
    rows, d_in = feats.shape
    return pl.pallas_call(
        half_kernel,
        in_specs=[scalars(), whole()],
        out_specs=whole(),
        out_shape=jax.ShapeDtypeStruct((rows // 2, d_in), BF16),
        compiler_params=params(HALF_MIB),
        cost_estimate=cost(10**10, 10**8),
        name="half_of",
    )(place, feats)


def halves(total_ref, own_ref, send_ref, own_shard, own_core, members):
    wide = own_ref.shape[1]
    mine = pl.ds(pl.multiple_of(own_core * wide, wide), wide)
    twin = pl.ds(pl.multiple_of((1 - own_core) * wide, wide), wide)
    rows = own_ref.shape[0] // members
    for member in range(members):
        here = slice(member * rows, (member + 1) * rows)
        there = pl.ds(pl.multiple_of((member ^ own_shard) * rows, TILE), rows)
        own_ref[there, :] = total_ref[here, mine].astype(BF16)
        send_ref[there, :] = total_ref[here, twin].astype(BF16)


def build_words(index, q_rows, store):
    terms = index.shape[0]
    shift = q_rows.bit_length() - 1
    low = index & (q_rows - 1)
    one = jnp.left_shift(jnp.ones_like(index), (index >> shift) * 4)
    spare = -terms % 8
    low = jnp.concatenate([low, jnp.full((spare, 128), -1, jnp.int32)], axis=0)
    one = jnp.concatenate([one, jnp.zeros((spare, 128), jnp.int32)], axis=0)
    unit = one
    for other in range(1, terms + spare):
        same = pltpu.roll(low, other, 0) == low
        unit = unit + jnp.where(same, pltpu.roll(one, other, 0), jnp.zeros_like(one))
    tall = min(256, q_rows) // TILE
    shape = (tall, TILE, 128)
    place = lax.broadcasted_iota(jnp.int32, shape, 0) * TILE + lax.broadcasted_iota(jnp.int32, shape, 1)
    place = place.astype(I16)

    def tile(row):
        return jnp.broadcast_to(row, (TILE, 128)).astype(I16)[None]

    lows = [tile(low[k : k + 1, :]) for k in range(terms)]
    units = [tile(unit[k : k + 1, :]) for k in range(terms)]
    for top in range(0, q_rows // TILE, tall):
        word = jnp.zeros(shape, I16)
        for k in range(terms):
            word = jnp.where(place == lows[k] - I16(top * TILE), units[k], word)
        store(top, tall, word)


def unpack(word_ref, field, lanes, count_ref):
    words = word_ref[:, :, lanes]
    if field < FIELDS - 1:
        counts = words & (15 << (4 * field))
    else:
        counts = (words >> (4 * field)) & 15
    count_ref[...] = counts.astype(BF16).reshape(count_ref.shape)


def unpacked_scale(field):
    return 16.0**field if field < FIELDS - 1 else 1.0


def rows_kernel(
    shard_bits, half_rows, chunks, members,
    place_ref, count_ref, index_ref, out_grad_ref, pre_act_ref, layer_two_ref,
    row_grad_ref, own_ref, send_ref, word_ref,
    masked_ref, sum_ref,
):
    rows = out_grad_ref.shape[0] // chunks
    blocks = [slice(chunk * rows, (chunk + 1) * rows) for chunk in range(chunks)]
    own_shard, own_core = place_ref[0], place_ref[1]
    part_bits = shard_bits - 1

    def build(tile):
        lanes = slice(tile * 128, (tile + 1) * 128)
        index = index_ref[:, lanes]
        row = index & ((1 << part_bits) - 1)
        half = ((index >> part_bits) & 1) ^ own_core ^ 1
        index = half * half_rows + (((index >> shard_bits) ^ own_shard) << part_bits) + row

        def store(top, tall, words):
            word_ref[top : top + tall, :, lanes] = words

        build_words(index, word_ref.shape[0] * TILE, store)

    tiles = row_grad_ref.shape[0] // 128
    ends = [tiles * chunk // chunks for chunk in range(chunks + 1)]
    for chunk, block in enumerate(blocks):
        live = count_ref[0] - chunk * rows

        @pl.when(live >= rows)
        def _(block=block):
            masked_ref[block, :] = out_grad_ref[block, :]

        @pl.when(live < rows)
        def _(block=block, live=live):
            out_grad = out_grad_ref[block, :].astype(F32)
            place = lax.broadcasted_iota(jnp.int32, out_grad.shape, 0)
            masked = jnp.where(place < live, out_grad, jnp.zeros_like(out_grad))
            masked_ref[block, :] = masked.astype(BF16)

    for chunk, block in enumerate(blocks):
        masked = masked_ref[block, :]
        pre_act = pre_act_ref[block, :]
        back = lax.dot_general(
            masked, layer_two_ref[...], (((1,), (1,)), ((), ())), preferred_element_type=F32
        )
        row_grad_ref[block, :] = jnp.where(
            pre_act.astype(F32) > 0, back, jnp.zeros_like(back)
        ).astype(BF16)
        activ = jnp.maximum(pre_act, jnp.zeros_like(pre_act))
        part = transposed_dot(activ, masked)
        sum_ref[...] = part if chunk == 0 else sum_ref[...] + part
        for tile in range(ends[chunk], ends[chunk + 1]):
            build(tile)
    halves(sum_ref, own_ref, send_ref, own_shard, own_core, members)


def row_gradients(place, batch_count, out_grad, pre_act, layer_two, index, hot_total, shard_rows):
    rows, d_out = out_grad.shape
    d_h = pre_act.shape[1]
    chunks = 4
    deep = hot_total // FIELDS // TILE
    half = jax.ShapeDtypeStruct((d_h, d_out // 2), BF16)
    return pl.pallas_call(
        functools.partial(
            rows_kernel,
            shard_rows.bit_length() - 1,
            hot_total // 2,
            chunks,
            hot_total // shard_rows,
        ),
        in_specs=[scalars(), scalars()] + [whole()] * 4,
        out_specs=[whole()] * 4,
        out_shape=[
            jax.ShapeDtypeStruct((rows, d_h), BF16),
            half,
            half,
            jax.ShapeDtypeStruct((deep, TILE, rows), I16),
        ],
        scratch_shapes=[
            pltpu.VMEM((rows, d_out), BF16),
            pltpu.VMEM((d_h, d_out), F32),
        ],
        compiler_params=params(ROWS_MIB),
        cost_estimate=cost(10**10, 10**8),
        name="row_gradients",
    )(place, batch_count, index, out_grad, pre_act, layer_two)


def build_tiles(index_ref, word_ref, first, count, word_first):
    for tile in range(count):
        here = slice((first + tile) * 128, (first + tile + 1) * 128)
        lanes = slice((word_first + tile) * 128, (word_first + tile + 1) * 128)

        def store(top, deep, words, lanes=lanes):
            word_ref[top : top + deep, :, lanes] = words

        build_words(index_ref[:, here], word_ref.shape[0] * TILE, store)


def hot_kernel(
    scale, word_in, row_grad_in, index_in, send_ref, keep_ref, cold_word_out,
    word_ref, row_grad_ref, index_ref, sums_ref, cold_word_ref, *counts
):
    word_ref[...] = word_in[...]
    row_grad_ref[...] = row_grad_in[...]
    index_ref[...] = index_in[...]
    tall, rows = counts[0].shape
    tiles = rows // 128 // 2 // FIELDS
    unpack(word_ref, 0, slice(None), counts[0])
    for field in range(FIELDS):
        found = jnp.dot(counts[field % 2][...], row_grad_ref[...], preferred_element_type=F32)
        found = found * (scale / unpacked_scale(field))
        sums_ref[field * tall : (field + 1) * tall, :] = found.astype(BF16)
        if field + 1 < FIELDS:
            unpack(word_ref, field + 1, slice(None), counts[(field + 1) % 2])
        build_tiles(index_ref, cold_word_ref, field * tiles, tiles, field * tiles)
    send_ref[...] = sums_ref[: 2 * tall, :]
    keep_ref[...] = sums_ref[2 * tall :, :]
    cold_word_out[...] = cold_word_ref[...]


def hot_sums(words, row_grad, cold_index, cold_rows, fanout):
    rows, d_h = row_grad.shape
    q_rows = words.shape[0] * TILE
    half = jax.ShapeDtypeStruct((q_rows * FIELDS // 2, d_h), BF16)
    return pl.pallas_call(
        functools.partial(hot_kernel, 1.0 / fanout),
        in_specs=[whole(), whole(), whole()],
        out_specs=[whole()] * 3,
        out_shape=[
            half,
            half,
            jax.ShapeDtypeStruct((cold_rows // FIELDS // TILE, TILE, rows // 2), I16),
        ],
        scratch_shapes=[
            pltpu.VMEM(words.shape, I16),
            pltpu.VMEM(row_grad.shape, BF16),
            pltpu.VMEM(cold_index.shape, jnp.int32),
            pltpu.VMEM((q_rows * FIELDS, d_h), BF16),
            pltpu.VMEM((cold_rows // FIELDS // TILE, TILE, rows // 2), I16),
            pltpu.VMEM((q_rows, rows), BF16),
            pltpu.VMEM((q_rows, rows), BF16),
        ],
        compiler_params=params(40),
        cost_estimate=cost(10**10, 10**8),
        name="hot_sums",
    )(words, row_grad, cold_index)


def cold_kernel(
    scale, word_in, index_in, row_grad_in, feats_ref, grad_out,
    word_ref, index_ref, row_grad_ref, grad_ref, part_ref, sums_ref, held_ref, sem, *counts
):
    fetch = pltpu.make_async_copy(feats_ref, held_ref, sem)
    fetch.start()
    tall, half = counts[0].shape
    word_ref[:, :, :half] = word_in[...]
    index_ref[...] = index_in[...]
    row_grad_ref[...] = row_grad_in[...]
    tiles = half // 128 // FIELDS

    def add_product(field):
        rows = slice(field * tall, (field + 1) * tall)
        part = transposed_dot(held_ref[rows, :], sums_ref[rows, :])
        grad_ref[...] = part if field == 0 else grad_ref[...] + part

    steps = [(k, field) for k in range(2) for field in range(FIELDS)]
    unpack(word_ref, 0, slice(half), counts[0])
    for step, (k, field) in enumerate(steps):
        depth, rows = slice(k * half, (k + 1) * half), slice(field * tall, (field + 1) * tall)
        found = jnp.dot(counts[step % 2][...], row_grad_ref[depth, :], preferred_element_type=F32)
        if k == 0:
            part_ref[rows, :] = found
            first = half // 128 + field * tiles
            build_tiles(index_ref, word_ref, first, tiles, first)
        else:
            found = (part_ref[rows, :] + found) * (scale / unpacked_scale(field))
            sums_ref[rows, :] = found.astype(BF16)
        if step + 1 < len(steps):
            ahead, next_field = steps[step + 1]
            lanes = slice(ahead * half, (ahead + 1) * half)
            unpack(word_ref, next_field, lanes, counts[(step + 1) % 2])
        if k == 1 and field == 0:
            fetch.wait()
        if k == 1 and field > 0:
            add_product(field - 1)
    add_product(FIELDS - 1)
    grad_out[...] = grad_ref[...]


def cold_grad(words, index, row_grad, feats, fanout):
    rows, d_h = row_grad.shape
    cold_rows, d_in = feats.shape
    q_rows = cold_rows // FIELDS
    return pl.pallas_call(
        functools.partial(cold_kernel, 1.0 / fanout),
        in_specs=[whole(), whole(), whole(), in_place()],
        out_specs=whole(),
        out_shape=jax.ShapeDtypeStruct((d_in, d_h), F32),
        scratch_shapes=[
            pltpu.VMEM((q_rows // TILE, TILE, rows), I16),
            pltpu.VMEM(index.shape, jnp.int32),
            pltpu.VMEM(row_grad.shape, BF16),
            pltpu.VMEM((d_in, d_h), F32),
            pltpu.VMEM((cold_rows, d_h), F32),
            pltpu.VMEM((cold_rows, d_h), BF16),
            pltpu.VMEM((cold_rows, d_in), BF16),
            pltpu.SemaphoreType.DMA,
            pltpu.VMEM((q_rows, rows // 2), BF16),
            pltpu.VMEM((q_rows, rows // 2), BF16),
        ],
        compiler_params=params(40),
        cost_estimate=cost(10**10, 10**8),
        name="cold_grad",
    )(words, index, row_grad, feats)


def join_kernel(parts, place_ref, cold_ref, keep_ref, other_ref, *rest):
    feats, (own_ref, send_ref, sums_ref, held_ref, total_ref) = rest[:parts], rest[parts:]
    d_in, wide = own_ref.shape
    sums = keep_ref[...].astype(F32) + other_ref[...].astype(F32)
    sums_ref[...] = sums.astype(BF16)
    base = 0
    for part in feats:
        held_ref[base : base + part.shape[0], :] = part[:, :d_in]
        base += part.shape[0]
    total_ref[...] = cold_ref[...]
    for left in range(0, d_in, 256):
        rows = slice(left, left + 256)
        total_ref[rows, :] += transposed_dot(held_ref[:, rows], sums_ref[...])
    total = total_ref[...].astype(BF16)
    store_halves(total, slice(None), place_ref[1], own_ref, send_ref)


def store_halves(total, rows, own_core, own_ref, send_ref):
    wide = own_ref.shape[1]
    first, second = total[:, :wide], total[:, wide:]

    @pl.when(own_core == 0)
    def _():
        own_ref[rows, :] = first
        send_ref[rows, :] = second

    @pl.when(own_core == 1)
    def _():
        own_ref[rows, :] = second
        send_ref[rows, :] = first


def join(place, cold, keep, other, feats):
    d_in, d_h = cold.shape
    half = jax.ShapeDtypeStruct((d_in, d_h // 2), BF16)
    return pl.pallas_call(
        functools.partial(join_kernel, len(feats)),
        in_specs=[scalars()] + [whole()] * (3 + len(feats)),
        out_specs=[whole()] * 2,
        out_shape=[half, half],
        scratch_shapes=[
            pltpu.VMEM(keep.shape, BF16),
            pltpu.VMEM((keep.shape[0], d_in), BF16),
            pltpu.VMEM((d_in, d_h), F32),
        ],
        compiler_params=params(32),
        cost_estimate=cost(2 * keep.shape[0] * d_h * d_in, 4 * d_in * d_h),
        name="join",
    )(place, cold, keep, other, *feats)


def share_rows(rows, members, place_ref, core, turn):
    size = rows // members
    partner = turn
    if members == 4 and turn == 1:
        partner = 3
    elif members == 4 and turn > 1:
        partner = jnp.where(core == 0, turn - 1, 4 - turn)
    return pl.ds(pl.multiple_of((place_ref[0] ^ partner) * size, TILE), size)


def pair_kernel(members, place_ref, one_ref, other_ref, *rest):
    out_refs = rest[-members:]
    rows = one_ref.shape[0] // members
    for k, out_ref in enumerate(out_refs):
        here = share_rows(one_ref.shape[0], members, place_ref, place_ref[1], k)
        total = one_ref[here, :].astype(F32) + other_ref[here, :].astype(F32)
        out_ref[:rows, :] = total.astype(BF16)
    for beside_ref in rest[:-members]:
        out_refs[1][rows:, :] = beside_ref[...]


def pair_sums(place, one, other, members, beside):
    rows, wide = one.shape
    share = jax.ShapeDtypeStruct((rows // members, wide), BF16)
    first = jax.ShapeDtypeStruct((rows // members + sum(x.shape[0] for x in beside), wide), BF16)
    return pl.pallas_call(
        functools.partial(pair_kernel, members),
        in_specs=[scalars()] + [whole()] * (2 + len(beside)),
        out_specs=[whole()] * members,
        out_shape=[share, first] + [share] * (members - 2),
        compiler_params=params(16),
        cost_estimate=cost(0, 6 * rows * wide),
        name="pair_sums",
    )(place, one, other, *beside)


def laid_turns(members):
    return [0, members - 1, *range(1, members - 1)]


def lay_kernel(members, parts, twin, place_ref, *refs):
    halves_in, refs = refs[:parts], refs[parts:]
    refs = refs[2:] if twin else refs
    outs, held, sems = refs[:2], refs[2:4], refs[4]
    core = 1 - place_ref[1] if twin else place_ref[1]
    wide = halves_in[0].shape[1]
    lanes = pl.ds(pl.multiple_of(core * wide, wide), wide)
    each = members // parts
    copies = []
    for k, turn in enumerate(laid_turns(members)):
        base = k % each * (halves_in[0].shape[0] // each)
        for at, (out_ref, held_ref) in enumerate(zip(outs, held)):
            here = share_rows(out_ref.shape[0], members, place_ref, core, turn)
            held_ref[here, :] = halves_in[k // each][base : base + here.size, :].astype(F32)
            copy = pltpu.make_async_copy(
                held_ref.at[here, :], out_ref.at[here, lanes], sems.at[2 * k + at]
            )
            copy.start()
            copies.append(copy)
            base += here.size
    for copy in copies:
        copy.wait()


def lay(place, parts, members, rows_of, before=()):
    wide = parts[0].shape[1]
    count = 1 + len(parts)
    return pl.pallas_call(
        functools.partial(lay_kernel, members, len(parts), bool(before)),
        in_specs=[scalars()] + [whole()] * len(parts) + [in_place()] * len(before),
        out_specs=[in_place()] * len(rows_of),
        out_shape=[jax.ShapeDtypeStruct((rows, 2 * wide), F32) for rows in rows_of],
        input_output_aliases={count + at: at for at in range(len(before))},
        scratch_shapes=[pltpu.VMEM((rows, wide), F32) for rows in rows_of]
        + [pltpu.SemaphoreType.DMA((2 * members,))],
        compiler_params=params(16),
        cost_estimate=cost(10**10, 10**8),
        name="lay",
    )(place, *parts, *before)


def exchange(array, axis, step):
    size = lax.axis_size(axis)
    return lax.ppermute(array, axis, [(source, source ^ step) for source in range(size)])


def added(*arrays):
    total = arrays[0].astype(F32)
    for array in arrays[1:]:
        total = total + array.astype(F32)
    return total.astype(BF16)


def route_of(n_clique, n_copy, turn):
    moves = [(0, 0), (3, 3), (1, 2), (2, 1)][turn] if n_clique == 4 else (turn, turn)
    return [
        (i * n_copy + j, (i ^ moves[j & 1]) * n_copy + j)
        for i in range(n_clique)
        for j in range(n_copy)
    ]


def trade(arrays):
    n_clique, n_copy = lax.axis_size("clique"), lax.axis_size("copy")
    return [arrays[0]] + [
        lax.ppermute(arrays[turn], ("clique", "copy"), route_of(n_clique, n_copy, turn))
        for turn in range(1, n_clique)
    ]


def sum_over_slice(shares, two):
    got = trade(shares)
    rows = shares[0].shape[0]
    if got[1].shape[0] > rows:
        two = added(two, got[1][rows:])
    own = jnp.concatenate([added(*[array[:rows] for array in got]), two], axis=0)
    n_copy = lax.axis_size("copy")
    steps = [2 << bit for bit in range((n_copy // 2).bit_length() - 1)]
    for near, far in zip(steps, reversed(steps)):
        route = [(j, j ^ (far if j & 1 else near)) for j in range(n_copy)]
        own = added(own, lax.ppermute(own, "copy", route))
    return trade([own] * len(shares))


def gather(own, two):
    members = lax.axis_size("clique")
    rows = two.shape[0] // members
    shares = [two[k * rows : (k + 1) * rows] for k in range(members)]
    middle, d_in = own.shape[0] // 2, own.shape[1]
    if members != 4 or rows != middle:
        feats = [own] + [exchange(own, "clique", k) for k in range(1, members)]
        got = shares[:1] + [exchange(shares[k], "clique", k) for k in range(1, members)]
        return feats, added(*got), []
    one, other = exchange(own, "clique", 1), exchange(own, "clique", 2)
    top = exchange(jnp.concatenate([other[:middle], shares[1]], axis=1), "clique", 1)
    bottom = exchange(jnp.concatenate([one[middle:], shares[2]], axis=1), "clique", 2)
    total = added(shares[0], top[:, d_in:], bottom[:, d_in:])
    return [own, one, other, top, bottom], total, shares[3:]


def on_device(
    out_grad, pre_act, batch_count, layer_two, hot_slots, cold_index, hot_feats, cold_feats
):
    n_clique = lax.axis_size("clique")
    shard_rows, d_in = hot_feats.shape
    d_h = pre_act.shape[1]
    cold_rows = cold_feats.shape[0]
    fanout = hot_slots.shape[1] + cold_index.shape[1]
    copy_at = lax.axis_index("copy")
    place = jnp.stack([lax.axis_index("clique"), copy_at & 1]).astype(jnp.int32)

    half_feats = half_of(place, hot_feats)
    row_grad, own_two, twin_two, words = row_gradients(
        place, batch_count, out_grad, pre_act, layer_two, hot_slots.T, shard_rows * n_clique, shard_rows
    )
    two = added(own_two, exchange(twin_two, "copy", 1))
    feats, two, far = gather(half_feats, two)
    send, keep, words = hot_sums(words, row_grad, cold_index.T, cold_rows, fanout)
    other = exchange(send, "copy", 1)
    cold = cold_grad(words, cold_index.T, row_grad, cold_feats, fanout)
    own_one, twin_one = join(place, cold, keep, other, feats)
    shares = pair_sums(place, own_one, exchange(twin_one, "copy", 1), n_clique, far)
    shares = sum_over_slice(shares, two)
    middle = n_clique // 2
    shares = [shares[turn] for turn in laid_turns(n_clique)]
    parts = [jnp.concatenate(part, axis=0) for part in (shares[:middle], shares[middle:])]
    others = [exchange(part, "copy", 1) for part in parts]
    rows_of = (d_in, d_h)
    own = lay(place, parts, n_clique, rows_of)
    return tuple(lay(place, others, n_clique, rows_of, own))


def solution(mesh):
    placed = (
        P(("clique", "copy"), None),
        P(("clique", "copy"), None),
        P(("clique", "copy")),
        P(),
        P(("clique", "copy"), None),
        P(("clique", "copy"), None),
        P("clique", None),
        P(("clique", "copy"), None),
    )
    return jax.shard_map(
        on_device, mesh=mesh, in_specs=placed, out_specs=(P(), P()), check_vma=False
    )
```
